512 devices in a mesh: gx: 64 (over y_hi, z, core), gy: 8 (over x, y_lo).
Axes of the slice: x: 4, y: 8 (y_hi: 4, y_lo: 2; y = y_hi * 2 + y_lo), z: 8, core: 2. Of those that a mesh axis runs over, the one named last changes fastest.
Arguments:
- gas_state: float32 [5, 512, 64, 256], P(None, 'gx', 'gy'), may hold values from -3 to 3
- pressure_guess: float32 [512, 64, 256], P('gx', 'gy'), may hold values from -6 to 6
- drop_motion: float32 [4, 64, 32768], P(None, 'gx', 'gy'), may hold values from -6 to 6
- drop_size: float32 [64, 32768], P('gx', 'gy'), may hold values from 0.5 to 2
- drop_cell: int32 [64, 32768], P('gx', 'gy'), may hold values from 0 to 16383
- drop_target: int32 [64, 32768], P('gx', 'gy'), may hold values from -1 to 4, as said below
- spray_on: int32 [64, 64], P('gx', 'gy'), may hold values 0 or 1
- spray_time: int32 [64, 64], P('gx', 'gy'), may hold values from 0 to 100
- spray_cell: int32 [64, 64], P('gx', 'gy'), may hold values from 0 to 16383
Outputs:
- gas_next: float32 [5, 512, 64, 256], P(None, 'gx', 'gy')
- pressure: float32 [512, 64, 256], P('gx', 'gy')
- drop_kept: float32 [5, 64, 32768], P(None, 'gx', 'gy')
- drop_arrived: float32 [4, 5, 64, 4096], P(None, None, 'gx', 'gy')
The draws below stay inside these ranges and needn't reach their ends.
Inputs may be any that keep to these rules, and one draw needn't show every extreme that they name: `drop_target`: in each device's 4096 slots at most 512 droplets have any one of the targets 0, 1, 2, 3, and on every device one of these targets has exactly 512.
All inputs are finite; a program needn't handle non-finite values. No bound on the sum of `spray_on` on one device may be relied on, other than what follows from the above.
Results may differ from the reference program's by a relative error of at most 0.00002.
Values sent between devices are 32-bit elements; how exact they have to be, the bound alone decides.
No kernel may reach another device: no remote copies, remote signals or barrier semaphores. Data moves between devices by JAX's collectives and lax.ppermute only.
A program may use at most 128 MiB of HBM per device.

```python
import math
import jax
import jax.numpy as jnp

CX = 8
CY = 8
NZ = 256
PD = 4096
SP = 8
ITERS = 8
CAP = 512
NX = 512
NY = 64
N_GX = 64
N_GY = 8


def draw_drop_target(key, part):
    devices = N_GX * N_GY
    key_counts, key_full, key_stay, key_order = jax.random.split(key, 4)
    counts = jax.random.randint(key_counts, (devices, 4), CAP // 3, CAP + 1)
    full = jax.random.randint(key_full, (devices,), 0, 4)
    counts = jnp.where(jnp.arange(4)[None, :] == full[:, None], CAP, counts)
    stayers = jax.random.randint(key_stay, (devices,), 0, PD - 4 * CAP + 1)
    bounds = jnp.cumsum(counts, axis=1)
    slots = jnp.arange(PD, dtype=jnp.int32)
    which = jnp.sum((slots[None, :, None] >= bounds[:, None, :]).astype(jnp.int32), axis=2)
    alive = slots[None, :] < bounds[:, 3:4] + stayers[:, None]
    target = jnp.where(alive, which, -1)
    scores = jax.random.randint(key_order, (devices, PD), 0, 65536) * PD + slots[None, :]
    order = jnp.argsort(scores, axis=1)
    target = jnp.take_along_axis(target, order, axis=1)
    return target.reshape(N_GX, N_GY * PD).astype(jnp.int32)


def set_ends(entries, key, low, high):
    dims = entries.shape
    spot = [jax.random.randint(jax.random.fold_in(key, axis), (), 0, dims[axis]) for axis in range(len(dims))]
    entries = entries.at[tuple(spot)].set(low)
    longest = dims.index(max(dims))
    spot[longest] = (spot[longest] + 1) % dims[longest]
    return entries.at[tuple(spot)].set(high)


def levels(own_key, shape, cuts, smallest, high):
    def one(dim, parts):
        heights = jax.random.uniform(jax.random.fold_in(jax.random.fold_in(own_key, 6), dim), (parts,), jnp.float32, smallest / len(cuts), high / len(cuts))
        return jnp.repeat(jnp.exp(heights), shape[dim] // parts).reshape((-1,) + (1,) * (len(shape) - dim - 1))

    loudness = one(*cuts[0])
    for cut in cuts[1:]:
        loudness = loudness * one(*cut)
    return loudness


def bell_draw(own_key, dims, scale, limit, cuts=(), kind=jnp.bfloat16):
    values = scale * jax.random.normal(own_key, dims, jnp.float32)
    if cuts:
        values = values * levels(own_key, dims, cuts, -0.22, 0.18)
    return jnp.clip(values, -limit, limit).astype(kind)


def setup_inputs(seed: int = 0) -> dict:
    keys = jax.random.split(jax.random.key(seed), 10)
    gas_state = bell_draw(keys[0], (5, NX, NY, NZ), 0.5, 3.0, ((1, 64), (2, 8)), jnp.float32)
    pressure_guess = bell_draw(keys[1], (NX, NY, NZ), 1.0, 6.0, ((0, 64), (1, 8)), jnp.float32)
    drop_motion = bell_draw(keys[2], (4, N_GX, N_GY * PD), 1.0, 6.0, ((1, 64), (2, 8)), jnp.float32)
    drop_size = jnp.clip(jnp.exp(math.log(2.0) - 1.3862944 * jax.random.uniform(keys[3], (N_GX, N_GY * PD), jnp.float32) ** levels(keys[3], (N_GX, N_GY * PD), ((0, 64), (1, 8)), -0.2, 0.2)), 0.5, 2.0)
    drop_cell = set_ends(jax.random.randint(keys[4], (N_GX, N_GY * PD), 0, CX * CY * NZ), jax.random.fold_in(keys[4], 1), 0, (CX * CY * NZ) - 1).astype(jnp.int32)
    drop_target = draw_drop_target(jax.random.fold_in(keys[9], 71), 0)
    spray_on = set_ends((jax.random.randint(keys[6], (N_GX, N_GY * SP), 0, 2) < 1).astype(jnp.int32), jax.random.fold_in(keys[6], 1), 0, 1)
    spray_time = set_ends(jax.random.randint(keys[7], (N_GX, N_GY * SP), 0, 101), jax.random.fold_in(keys[7], 1), 0, 100).astype(jnp.int32)
    spray_cell = set_ends(jax.random.randint(keys[8], (N_GX, N_GY * SP), 0, CX * CY * NZ), jax.random.fold_in(keys[8], 1), 0, (CX * CY * NZ) - 1).astype(jnp.int32)
    return dict(gas_state=gas_state, pressure_guess=pressure_guess, drop_motion=drop_motion, drop_size=drop_size, drop_cell=drop_cell, drop_target=drop_target, spray_on=spray_on, spray_time=spray_time, spray_cell=spray_cell)


TIME_STEP = 0.2
DIFFUSION = 0.1
DRAG_TIME = 0.5
HEAT_TIME = 1.0
GRAVITY = 1.0
VAPOUR_RATE = 0.5
DRAG_COUPLING = 0.5
LATENT = 2.0
VAPOUR_YIELD = 1.0
SPRAY_RATE = 3.0
CLOCK = 100.0
SPRAY_RAMP = 50.0


def window(padded, along_x, along_y, along_z):
    a = padded.shape[-3] - 4
    b = padded.shape[-2] - 4
    c = padded.shape[-1] - 4
    return padded[..., 2 + along_x:2 + along_x + a, 2 + along_y:2 + along_y + b, 2 + along_z:2 + along_z + c]


def gradient(padded, along_x, along_y, along_z):
    near = window(padded, along_x, along_y, along_z) - window(padded, -along_x, -along_y, -along_z)
    far = window(padded, 2 * along_x, 2 * along_y, 2 * along_z) - window(padded, -2 * along_x, -2 * along_y, -2 * along_z)
    return (8.0 * near - far) / 12.0


def predict(padded):
    speed_x = window(padded[0], 0, 0, 0)
    speed_y = window(padded[1], 0, 0, 0)
    speed_z = window(padded[2], 0, 0, 0)
    results = []
    for field in range(padded.shape[0]):
        single = padded[field]
        centre = window(single, 0, 0, 0)
        laplace = window(single, 1, 0, 0) + window(single, -1, 0, 0) + window(single, 0, 1, 0)
        laplace = laplace + window(single, 0, -1, 0) + window(single, 0, 0, 1) + window(single, 0, 0, -1) - 6.0 * centre
        transport = speed_x * gradient(single, 1, 0, 0) + speed_y * gradient(single, 0, 1, 0) + speed_z * gradient(single, 0, 0, 1)
        results.append(centre + TIME_STEP * (DIFFUSION * laplace - transport))
    return jnp.stack(results)


def divergence(flow_x, flow_y, vertical):
    lifted = jnp.pad(vertical, ((0, 0), (0, 0), (1, 1)))
    spread = 0.5 * (flow_x[2:, 1:-1] - flow_x[:-2, 1:-1]) + 0.5 * (flow_y[1:-1, 2:] - flow_y[1:-1, :-2])
    spread = spread + 0.5 * (lifted[:, :, 2:] - lifted[:, :, :-2])
    return spread / TIME_STEP


def sweep(bordered, source):
    inner = bordered[1:-1, 1:-1]
    lifted = jnp.pad(inner, ((0, 0), (0, 0), (1, 1)))
    beside_all = bordered[2:, 1:-1] + bordered[:-2, 1:-1] + bordered[1:-1, 2:] + bordered[1:-1, :-2]
    beside_all = beside_all + lifted[:, :, 2:] + lifted[:, :, :-2]
    return (beside_all - source) / 6.0


def correct(star, bordered):
    inner = bordered[1:-1, 1:-1]
    lifted = jnp.pad(inner, ((0, 0), (0, 0), (1, 1)))
    flow_x = star[0] - TIME_STEP * 0.5 * (bordered[2:, 1:-1] - bordered[:-2, 1:-1])
    flow_y = star[1] - TIME_STEP * 0.5 * (bordered[1:-1, 2:] - bordered[1:-1, :-2])
    vertical = star[2] - TIME_STEP * 0.5 * (lifted[:, :, 2:] - lifted[:, :, :-2])
    return jnp.concatenate([jnp.stack([flow_x, flow_y, vertical]), star[3:]], axis=0)


def droplets(motion, diameter, local):
    excess = local[3] - motion[3]
    vapour = VAPOUR_RATE * diameter * jax.nn.sigmoid(excess)
    renewed = jnp.stack([
        motion[0] + TIME_STEP * (local[0] - motion[0]) / DRAG_TIME,
        motion[1] + TIME_STEP * (local[1] - motion[1]) / DRAG_TIME,
        motion[2] + TIME_STEP * ((local[2] - motion[2]) / DRAG_TIME - GRAVITY),
        motion[3] + TIME_STEP * excess / HEAT_TIME,
        diameter - TIME_STEP * vapour])
    sources = jnp.stack([DRAG_COUPLING * diameter * diameter * (motion[2] - local[2]), -LATENT * vapour, VAPOUR_YIELD * vapour])
    return renewed, sources


def spray(flags, times):
    ramp = jnp.clip((CLOCK - times.astype(jnp.float32)) / SPRAY_RAMP, 0.0, 1.0)
    strength = SPRAY_RATE * ramp * flags.astype(jnp.float32)
    return jnp.stack([-strength, -strength, jnp.zeros_like(strength)])


def locate(cells, per_device):
    column = jnp.arange(N_GY * per_device, dtype=jnp.int32)[None, :] // per_device
    row = jnp.arange(N_GX, dtype=jnp.int32)[:, None]
    at_x = row * CX + cells // (CY * NZ)
    at_y = column * CY + (cells // NZ) % CY
    at_z = cells % NZ
    return at_x, at_y, at_z


def reference(gas_state, pressure_guess, drop_motion, drop_size, drop_cell, drop_target, spray_on, spray_time, spray_cell):
    at_x, at_y, at_z = locate(drop_cell, PD)
    local = gas_state[:, at_x, at_y, at_z]
    renewed, drop_sources = droplets(drop_motion, drop_size, local)
    drop_sources = jnp.where((drop_target >= 0)[None], drop_sources, 0.0)
    sources = jnp.zeros((3, NX, NY, NZ), jnp.float32).at[:, at_x, at_y, at_z].add(drop_sources)
    head_x, head_y, head_z = locate(spray_cell, SP)
    sources = sources.at[:, head_x, head_y, head_z].add(spray(spray_on, spray_time))
    padded = jnp.pad(gas_state, ((0, 0), (2, 2), (2, 2), (2, 2)))
    star = predict(padded)
    star = jnp.concatenate([star[:2], star[2:] + TIME_STEP * sources], axis=0)
    flows = jnp.pad(star[:2], ((0, 0), (1, 1), (1, 1), (0, 0)))
    source = divergence(flows[0], flows[1], star[2])
    field = pressure_guess
    for turn in range(ITERS):
        field = sweep(jnp.pad(field, ((1, 1), (1, 1), (0, 0))), source)
    gas_next = correct(star, jnp.pad(field, ((1, 1), (1, 1), (0, 0))))
    target = drop_target.reshape(N_GX, N_GY, PD)
    records = renewed.reshape(5, N_GX, N_GY, PD)
    rows = jnp.arange(N_GX, dtype=jnp.int32)[:, None, None]
    columns = jnp.arange(N_GY, dtype=jnp.int32)[None, :, None]
    parcels = []
    for heading in range(4):
        chosen = target == heading
        order = jnp.cumsum(chosen.astype(jnp.int32), axis=2) - 1
        place = jnp.where(chosen, order, CAP)
        parcel = jnp.zeros((5, N_GX, N_GY, CAP + 1), jnp.float32).at[:, rows, columns, place].set(records)
        parcels.append(parcel[..., :CAP])
    arrived = jnp.stack([
        jnp.pad(parcels[0], ((0, 0), (1, 0), (0, 0), (0, 0)))[:, :-1],
        jnp.pad(parcels[1], ((0, 0), (0, 1), (0, 0), (0, 0)))[:, 1:],
        jnp.pad(parcels[2], ((0, 0), (0, 0), (1, 0), (0, 0)))[:, :, :-1],
        jnp.pad(parcels[3], ((0, 0), (0, 0), (0, 1), (0, 0)))[:, :, 1:]])
    drop_arrived = arrived.reshape(4, 5, N_GX, N_GY * CAP)
    drop_kept = jnp.where((drop_target == 4)[None], renewed, 0.0)
    return gas_next, field, drop_kept, drop_arrived
```

```python
import functools

import jax
import jax.numpy as jnp
from jax import lax
from jax.experimental import pallas as pl
from jax.experimental.pallas import tpu as pltpu
from jax.sharding import PartitionSpec as P

B = 8
NZ = 256
PD = 4096
CAP = 512
CHUNK = 512
F32 = jnp.float32
BF16 = jnp.bfloat16
VMEM = pl.BlockSpec(memory_space=pltpu.VMEM)
SMEM = pl.BlockSpec(memory_space=pltpu.SMEM)

Y_LAYERS = [(1, 0), (1, 1), (1, 2), (0, 0), (0, 1), (2, 0), (2, 1), (3, 0), (3, 1), (4, 0), (4, 1), (5, 0)]
X_LAYERS = [(0, 0), (0, 1), (0, 2), (1, 0), (1, 1), (2, 0), (2, 1), (3, 0), (3, 1), (4, 0), (4, 1), (5, 0)]
NL = 12


def params(limit=16):
    return pltpu.CompilerParams(vmem_limit_bytes=limit * 1024 * 1024)


def tiles(n):
    return jax.ShapeDtypeStruct((n, B, NZ), F32)


def call(kernel, outs, n_in, cost, scratch=(), smem=(), limit=16):
    return pl.pallas_call(
        kernel,
        out_shape=outs,
        in_specs=[SMEM if i in smem else VMEM for i in range(n_in)],
        out_specs=[VMEM] * len(outs),
        scratch_shapes=list(scratch),
        compiler_params=params(limit),
        cost_estimate=pl.CostEstimate(flops=cost, bytes_accessed=cost // 8, transcendentals=0),
    )


def pack_y_kernel(gas, guess, low, high):
    for r, (field, depth) in enumerate(Y_LAYERS):
        for side, y in ((low, depth), (high, B - 1 - depth)):
            side[r] = guess[:, y, :] if field == 5 else gas[field, :, y, :]


def split(value):
    high = value.astype(BF16).astype(F32)
    return high, value - high


def droplet_kernel(gas, motion, size, cell, target, on, when, head, sources, kept, parcels):
    table = jnp.concatenate([gas[f].reshape(B * B, NZ) for f in range(4)], axis=0)
    high, low = split(table)
    table = jnp.concatenate([high.astype(BF16), low.astype(BF16)], axis=1)
    at_z = lax.broadcasted_iota(jnp.int32, (NZ, CHUNK), 0)
    at_xy = lax.broadcasted_iota(jnp.int32, (B * B, CHUNK), 0)
    at_high = lax.broadcasted_iota(jnp.int32, (B, CHUNK), 0)
    heading = lax.broadcasted_iota(jnp.int32, (B, CHUNK), 0)
    a = lax.broadcasted_iota(jnp.int32, (CHUNK, CHUNK), 0)
    b = lax.broadcasted_iota(jnp.int32, (CHUNK, CHUNK), 1)
    upper = jnp.where(a <= b, 1.0, 0.0).astype(BF16)
    before = jnp.zeros((B, 1), F32)
    total = jnp.zeros((4 * B * B, NZ), F32)
    moved = jnp.zeros((10 * B, NZ), F32)
    across = (((1,), (1,)), ((), ()))
    for n in range(PD // CHUNK):
        part = slice(n * CHUNK, (n + 1) * CHUNK)
        cells = cell[:, part]
        goal = target[:, part]
        in_z = jnp.where(at_z == (cells & (NZ - 1)), 1.0, 0.0).astype(BF16)
        in_xy = at_xy == (cells >> 8)
        found = jnp.dot(table, jnp.concatenate([in_z, in_z], axis=0), preferred_element_type=F32)
        local = [
            jnp.sum(jnp.where(in_xy, found[f * B * B : (f + 1) * B * B], 0.0), axis=0, keepdims=True)
            for f in range(4)
        ]
        u, v, w, temperature = (motion[f, :, part] for f in range(4))
        diameter = size[:, part]
        excess = local[3] - temperature
        vapour = 0.5 * diameter * jax.nn.sigmoid(excess)
        renewed = [
            u + 0.4 * (local[0] - u),
            v + 0.4 * (local[1] - v),
            w + 0.2 * ((local[2] - w) * 2.0 - 1.0),
            temperature + 0.2 * excess,
            diameter - 0.2 * vapour,
        ]
        drag = 0.5 * diameter * diameter * (w - local[2])
        alive = goal >= 0
        for f in range(5):
            kept[f, :, part] = jnp.where(goal == 4, renewed[f], 0.0)
        pieces = [*split(jnp.where(alive, drag, 0.0)), *split(jnp.where(alive, vapour, 0.0))]
        given = jnp.concatenate([jnp.where(in_xy, piece, 0.0).astype(BF16) for piece in pieces], axis=0)
        total = total + lax.dot_general(given, in_z, across, preferred_element_type=F32)
        chosen = heading == goal
        rank = jnp.dot(jnp.where(chosen, 1.0, 0.0).astype(BF16), upper, preferred_element_type=F32) + before
        before = rank[:, CHUNK - 1 :]
        place = (rank - 1.0).astype(jnp.int32) + heading * CAP
        leaves = chosen & (heading < 4)
        place = jnp.sum(jnp.where(leaves, place + 1, 0), axis=0, keepdims=True) - 1
        in_low = jnp.where(at_z == (place & (NZ - 1)), 1.0, 0.0).astype(BF16)
        in_high = at_high == (place >> 8)
        split_up = [split(value) for value in renewed]
        rows = [jnp.where(in_high, split_up[f][piece], 0.0) for piece in range(2) for f in range(5)]
        moved = moved + lax.dot_general(
            jnp.concatenate(rows, axis=0).astype(BF16), in_low, across, preferred_element_type=F32
        )
    q = B * B
    steam = total[2 * q : 3 * q] + total[3 * q :]
    sources[0] = total[:q] + total[q : 2 * q]
    sources[1] = -2.0 * steam
    sources[2] = steam
    lanes = lax.broadcasted_iota(jnp.int32, (1, NZ), 1)
    for s in range(B):
        ramp = jnp.clip((100.0 - when[0, s].astype(F32)) / 50.0, 0.0, 1.0)
        strength = 3.0 * ramp * on[0, s].astype(F32)
        where = head[0, s]
        row = pl.ds(where >> 8, 1)
        taken = jnp.where(lanes == (where & (NZ - 1)), strength, 0.0)
        for f in range(2):
            sources[f, row, :] = sources[f, row, :] - taken
    moved = moved[: 5 * B] + moved[5 * B :]
    for d in range(4):
        for f in range(5):
            for half in range(2):
                at = f * B + 2 * d + half
                r = 2 * f + half
                parcels[d, r // B, r % B : r % B + 1, :] = moved[at : at + 1]
        parcels[d, 1, 2:, :] = jnp.zeros((B - 2, NZ), F32)


def pack_x_kernel(gas, guess, below, above, parcels, low, high):
    for side, near, step, heading in ((low, 0, 1, 1), (high, B - 1, -1, 0)):
        for r, (field, depth) in enumerate(X_LAYERS):
            x = near + step * depth
            side[r] = guess[x] if field == 5 else gas[field, x]
        for h, halo in enumerate((below, above)):
            for r, (layer, x) in enumerate(((3, near), (4, near), (0, near), (0, near + step))):
                side[NL, 4 * h + r : 4 * h + r + 1, :] = halo[layer, x : x + 1, :]
        side[NL + 1] = parcels[heading, 0]
        side[NL + 2] = parcels[heading, 1]


def beside(value, by):
    lane = lax.broadcasted_iota(jnp.int32, value.shape, 1)
    turned = pltpu.roll(value, (-by) % NZ, axis=1)
    return jnp.where((lane < NZ - by) if by > 0 else (lane >= -by), turned, 0.0)


def advance(e, f, x, rows, first):
    def at(field, dx, dy):
        return e[field, x + dx, first + dy : first + dy + rows, :]

    centre = at(f, 0, 0)
    xs = {s: at(f, s, 0) for s in (-2, -1, 1, 2)}
    ys = {s: at(f, 0, s) for s in (-2, -1, 1, 2)}
    zs = {s: beside(centre, s) for s in (-2, -1, 1, 2)}
    laplace = xs[1] + xs[-1] + ys[1] + ys[-1] + zs[1] + zs[-1] - 6.0 * centre
    transport = 0.0
    for axis, shifted in enumerate((xs, ys, zs)):
        slope = 8.0 * (shifted[1] - shifted[-1]) - (shifted[2] - shifted[-2])
        transport = transport + at(axis, 0, 0) * slope
    return centre + (0.02 * laplace - (0.2 / 12.0) * transport)


def predict_kernel(gas, guess, below, above, left, right, sources, parcels, star, up, down, e, wide, tall, q):
    gx = lax.axis_index("gx")
    gy = lax.axis_index("gy")
    has_left, has_right = gx > 0, gx < lax.axis_size("gx") - 1
    has_below, has_above = gy > 0, gy < lax.axis_size("gy") - 1
    for f in range(5):
        e[f, 3 : 3 + B, B : 2 * B, :] = gas[f]
    q[1 : 1 + B, B : 2 * B, :] = guess[...]
    for r, (field, depth) in enumerate(Y_LAYERS):
        for halo, y in ((below, B - 1 - depth), (above, 2 * B + depth)):
            if field == 5:
                q[1 : 1 + B, y, :] = halo[r]
            else:
                e[field, 3 : 3 + B, y, :] = halo[r]
    for r, (field, depth) in enumerate(X_LAYERS):
        for halo, x in ((left, -1 - depth), (right, B + depth)):
            if field == 5:
                q[x + 1, B : 2 * B, :] = halo[r]
            else:
                e[field, x + 3, B : 2 * B, :] = halo[r]
    for halo, near, step in ((left, 2, -1), (right, 3 + B, 1)):
        for h, (y, onward) in enumerate(((B - 1, -1), (2 * B, 1))):
            spots = ((0, near, y), (0, near, y + onward), (1, near, y), (1, near + step, y))
            for r, (field, x, row) in enumerate(spots):
                e[field, x, row : row + 1, :] = halo[NL, 4 * h + r : 4 * h + r + 1, :]
    for x in range(-1, B + 1):
        value = advance(e, 0, x + 3, B, B)
        if x < 0:
            value = jnp.where(has_left, value, 0.0)
        if x == B:
            value = jnp.where(has_right, value, 0.0)
        wide[x + 1] = value
        if 0 <= x < B:
            star[0, x] = value
    for x in range(B):
        value = advance(e, 1, x + 3, B + 2, B - 1)
        row = lax.broadcasted_iota(jnp.int32, value.shape, 0)
        inside = ((row > 0) | has_below) & ((row < B + 1) | has_above)
        value = jnp.where(inside, value, 0.0)
        tall[x, : B + 2, :] = value
        star[1, x] = value[1 : 1 + B]
    for f in (3, 4):
        for x in range(B):
            star[f, x] = advance(e, f, x + 3, B, B) + 0.2 * sources[f - 2, x]
    for x in range(B):
        w = advance(e, 2, x + 3, B, B) + 0.2 * sources[0, x]
        star[2, x] = w
        spread = wide[x + 2] - wide[x] + (tall[x, 2 : 2 + B, :] - tall[x, :B, :])
        source = 2.5 * (spread + (beside(w, 1) - beside(w, -1)))
        centre = q[x + 1, B : 2 * B, :]
        around = q[x + 2, B : 2 * B, :] + q[x, B : 2 * B, :]
        around = around + q[x + 1, B + 1 : 2 * B + 1, :] + q[x + 1, B - 1 : 2 * B - 1, :]
        field = (around + beside(centre, 1) + beside(centre, -1) - source) * (1.0 / 6.0)
        for side in (up, down):
            side[x] = field
            side[B + x] = source
    for side, heading in ((up, 2), (down, 3)):
        side[2 * B] = parcels[heading, 0]
        side[2 * B + 1] = parcels[heading, 1]


NX2 = 28


def pack_x2_kernel(own, below, above, low, high):
    row = lax.broadcasted_iota(jnp.int32, (B, NZ), 0)
    for side, near, step in ((low, -1, 1), (high, B, -1)):
        for d in range(1, B + 1):
            side[d - 1] = own[near + step * d]
        for m in range(1, B):
            lower = below[near + step * m]
            upper = above[near + step * (B - m)]
            side[B - 1 + m] = jnp.where(row >= m, lower, upper)
        base = 2 * B - 1
        for d in range(1, B):
            side[base + d - 1] = own[B + near + step * d]
        for m in range(1, B - 1):
            lower = below[B + near + step * m]
            upper = above[B + near + step * (B - 1 - m)]
            side[base + B - 2 + m] = jnp.where(row >= m + 1, lower, upper)


def finish_kernel(star, own, below, above, left, right, early_left, early_right, gas_next, pressure, arrived, p0, p1, s, c):
    gx = lax.axis_index("gx")
    gy = lax.axis_index("gy")
    inside_x = [gx > 0, None, gx < lax.axis_size("gx") - 1]
    inside_y = [gy > 0, None, gy < lax.axis_size("gy") - 1]
    for i in range(3):
        for j in range(3):
            value = jnp.full((B, NZ), 1.0 / 6.0, F32)
            for flag in (inside_x[i], inside_y[j]):
                if flag is not None:
                    value = jnp.where(flag, value, 0.0)
            c[i, j * B : (j + 1) * B, :] = value
    for x in range(B):
        for k, halo in enumerate((below, own, above)):
            p0[B + x, k * B : (k + 1) * B, :] = halo[x]
            s[B + x, k * B : (k + 1) * B, :] = halo[B + x]
    base = 2 * B - 1
    for halo, near, step in ((left, B, -1), (right, 2 * B - 1, 1)):
        for d in range(1, B + 1):
            p0[near + step * d, B : 2 * B, :] = halo[d - 1]
            if d < B:
                s[near + step * d, B : 2 * B, :] = halo[base + d - 1]
        for m in range(1, B):
            piece = halo[B - 1 + m]
            p0[near + step * m, :B, :] = piece
            p0[near + step * (B - m), 2 * B :, :] = piece
        for m in range(1, B - 1):
            piece = halo[base + B - 2 + m]
            s[near + step * m, :B, :] = piece
            s[near + step * (B - 1 - m), 2 * B :, :] = piece
        p0[near + step * B, :B, :] = halo[0]
        p0[near + step * B, 2 * B :, :] = halo[0]
        s[near + step * (B - 1), :B, :] = halo[0]
        s[near + step * (B - 1), 2 * B :, :] = halo[0]
    now, later = p0, p1
    for turn in range(2, 9):
        reach = 9 - turn
        for x in range(B - reach, 2 * B + reach):
            centre = now[x]
            around = now[x - 1] + now[x + 1]
            around = around + pltpu.roll(centre, 1, axis=0) + pltpu.roll(centre, 3 * B - 1, axis=0)
            around = around + beside(centre, 1) + beside(centre, -1)
            later[x] = (around - s[x]) * c[0 if x < B else (1 if x < 2 * B else 2)]
        now, later = later, now
    for x in range(B):
        centre = now[B + x, B : 2 * B, :]
        pressure[x] = centre
        gas_next[0, x] = star[0, x] - 0.1 * (now[B + x + 1, B : 2 * B, :] - now[B + x - 1, B : 2 * B, :])
        gas_next[1, x] = star[1, x] - 0.1 * (now[B + x, B + 1 : 2 * B + 1, :] - now[B + x, B - 1 : 2 * B - 1, :])
        gas_next[2, x] = star[2, x] - 0.1 * (beside(centre, 1) - beside(centre, -1))
        gas_next[3, x] = star[3, x]
        gas_next[4, x] = star[4, x]
    for d, (halo, base) in enumerate(((early_left, NL + 1), (early_right, NL + 1), (below, 2 * B), (above, 2 * B))):
        for f in range(5):
            for half in range(2):
                r = 2 * f + half
                arrived[d, f, :, half * NZ : (half + 1) * NZ] = halo[base + r // B, r % B : r % B + 1, :]


def shifted(shard, axis, by):
    peers = lax.axis_size(axis)
    pairs = [(i, i + by) for i in range(peers) if 0 <= i + by < peers]
    return lax.ppermute(shard, axis, pairs)


def body(gas, guess, motion, size, cell, target, on, when, head):
    low, high = call(pack_y_kernel, [tiles(NL)] * 2, 2, 10**6)(gas, guess)
    below = shifted(high, "gy", 1)
    above = shifted(low, "gy", -1)
    sources, kept, parcels = call(
        droplet_kernel,
        [
            jax.ShapeDtypeStruct((3, B * B, NZ), F32),
            jax.ShapeDtypeStruct((5, 1, PD), F32),
            jax.ShapeDtypeStruct((4, 2, B, NZ), F32),
        ],
        8,
        10**9,
        smem=(5, 6, 7),
    )(gas, motion, size, cell, target, on, when, head)
    low, high = call(pack_x_kernel, [tiles(NL + 3)] * 2, 5, 10**6)(gas, guess, below, above, parcels)
    left = shifted(high, "gx", 1)
    right = shifted(low, "gx", -1)
    star, up, down = call(
        predict_kernel,
        [jax.ShapeDtypeStruct((5, B, B, NZ), F32), tiles(2 * B + 2), tiles(2 * B + 2)],
        8,
        10**7,
        scratch=[
            pltpu.VMEM((5, B + 6, 3 * B, NZ), F32),
            pltpu.VMEM((B + 2, B, NZ), F32),
            pltpu.VMEM((B, 2 * B, NZ), F32),
            pltpu.VMEM((B + 2, 3 * B, NZ), F32),
        ],
    )(gas, guess, below, above, left, right, sources.reshape(3, B, B, NZ), parcels)
    below = shifted(up, "gy", 1)
    above = shifted(down, "gy", -1)
    low, high = call(pack_x2_kernel, [tiles(NX2)] * 2, 3, 10**6)(up, below, above)
    far_left = shifted(high, "gx", 1)
    far_right = shifted(low, "gx", -1)
    gas_next, pressure, arrived = call(
        finish_kernel,
        [
            jax.ShapeDtypeStruct((5, B, B, NZ), F32),
            jax.ShapeDtypeStruct((B, B, NZ), F32),
            jax.ShapeDtypeStruct((4, 5, 1, CAP), F32),
        ],
        8,
        10**7,
        scratch=[
            pltpu.VMEM((3 * B, 3 * B, NZ), F32),
            pltpu.VMEM((3 * B, 3 * B, NZ), F32),
            pltpu.VMEM((3 * B, 3 * B, NZ), F32),
            pltpu.VMEM((3, 3 * B, NZ), F32),
        ],
    )(star, up, below, above, far_left, far_right, left, right)
    return gas_next, pressure, kept, arrived


def solution(mesh):
    in_specs = (
        P(None, "gx", "gy", None),
        P("gx", "gy", None),
        P(None, "gx", "gy"),
        P("gx", "gy"),
        P("gx", "gy"),
        P("gx", "gy"),
        P("gx", "gy"),
        P("gx", "gy"),
        P("gx", "gy"),
    )
    out_specs = (
        P(None, "gx", "gy", None),
        P("gx", "gy", None),
        P(None, "gx", "gy"),
        P(None, None, "gx", "gy"),
    )
    return jax.shard_map(body, mesh=mesh, in_specs=in_specs, out_specs=out_specs, check_vma=False)
```

```python
import jax
import jax.numpy as jnp
from jax import lax
from jax.experimental import pallas as pl
from jax.experimental.pallas import tpu as pltpu
from jax.sharding import PartitionSpec as P

B = 8
NZ = 256
PD = 4096
CAP = 512
CHUNK = 512
F32 = jnp.float32
BF16 = jnp.bfloat16
VMEM = pl.BlockSpec(memory_space=pltpu.VMEM)
SMEM = pl.BlockSpec(memory_space=pltpu.SMEM)

Y_LAYERS = [(1, 0), (1, 1), (1, 2), (0, 0), (0, 1), (2, 0), (2, 1), (3, 0), (3, 1), (4, 0), (4, 1), (5, 0)]
X_LAYERS = [(0, 0), (0, 1), (0, 2), (1, 0), (1, 1), (2, 0), (2, 1), (3, 0), (3, 1), (4, 0), (4, 1), (5, 0)]
NL = 12


def params(limit=16):
    return pltpu.CompilerParams(vmem_limit_bytes=limit * 1024 * 1024)


def tiles(n):
    return jax.ShapeDtypeStruct((n, B, NZ), F32)


def call(kernel, outs, n_in, cost, scratch=(), smem=(), limit=16):
    return pl.pallas_call(
        kernel,
        out_shape=outs,
        in_specs=[SMEM if i in smem else VMEM for i in range(n_in)],
        out_specs=[VMEM] * len(outs),
        scratch_shapes=list(scratch),
        compiler_params=params(limit),
        cost_estimate=pl.CostEstimate(flops=cost, bytes_accessed=cost // 8, transcendentals=0),
    )


def by_parity(axis, act, even, odd):
    first = lax.rem(lax.axis_index(axis), 2) == 0

    @pl.when(first)
    def _():
        act(odd, even)

    @pl.when(jnp.logical_not(first))
    def _():
        act(even, odd)


def swap(shard, axis, start):
    peers = lax.axis_size(axis)
    pairs = [(i + a, i + 1 - a) for i in range(start, peers - 1, 2) for a in range(2)]
    return lax.ppermute(shard, axis, pairs)


def pack_y_kernel(gas, guess, even, odd):
    def act(low, high):
        for r, (field, depth) in enumerate(Y_LAYERS):
            for side, y in ((low, depth), (high, B - 1 - depth)):
                side[r] = guess[:, y, :] if field == 5 else gas[field, :, y, :]

    by_parity("gy", act, even, odd)


def split(value):
    high = value.astype(BF16).astype(F32)
    return high, value - high


def renew_kernel(gas, motion, size, cell, target, kept, rows):
    table = jnp.concatenate([gas[f].reshape(B * B, NZ) for f in range(4)], axis=0)
    high, low = split(table)
    table = jnp.concatenate([high.astype(BF16), low.astype(BF16)], axis=1)
    at_z = lax.broadcasted_iota(jnp.int32, (NZ, CHUNK), 0)
    at_xy = lax.broadcasted_iota(jnp.int32, (B * B, CHUNK), 0)
    heading = lax.broadcasted_iota(jnp.int32, (B, CHUNK), 0)
    a = lax.broadcasted_iota(jnp.int32, (CHUNK, CHUNK), 0)
    b = lax.broadcasted_iota(jnp.int32, (CHUNK, CHUNK), 1)
    upper = jnp.where(a <= b, 1.0, 0.0).astype(BF16)
    before = jnp.zeros((B, 1), F32)
    for n in range(PD // CHUNK):
        part = slice(n * CHUNK, (n + 1) * CHUNK)
        cells = cell[:, part]
        goal = target[:, part]
        in_z = jnp.where(at_z == (cells & (NZ - 1)), 1.0, 0.0).astype(BF16)
        in_xy = at_xy == (cells >> 8)
        found = jnp.dot(table, jnp.concatenate([in_z, in_z], axis=0), preferred_element_type=F32)
        local = [
            jnp.sum(jnp.where(in_xy, found[f * B * B : (f + 1) * B * B], 0.0), axis=0, keepdims=True)
            for f in range(4)
        ]
        u, v, w, temperature = (motion[f, :, part] for f in range(4))
        diameter = size[:, part]
        excess = local[3] - temperature
        vapour = 0.5 * diameter * jax.nn.sigmoid(excess)
        renewed = [
            u + 0.4 * (local[0] - u),
            v + 0.4 * (local[1] - v),
            w + 0.2 * ((local[2] - w) * 2.0 - 1.0),
            temperature + 0.2 * excess,
            diameter - 0.2 * vapour,
        ]
        drag = 0.5 * diameter * diameter * (w - local[2])
        alive = goal >= 0
        for f in range(5):
            kept[f, :, part] = jnp.where(goal == 4, renewed[f], 0.0)
            rows[f : f + 1, part] = renewed[f]
        rows[5:6, part] = jnp.where(alive, drag, 0.0)
        rows[6:7, part] = jnp.where(alive, vapour, 0.0)
        chosen = heading == goal
        rank = jnp.dot(jnp.where(chosen, 1.0, 0.0).astype(BF16), upper, preferred_element_type=F32) + before
        before = rank[:, CHUNK - 1 :]
        leaves = chosen & (heading < 4)
        place = jnp.where(leaves, rank + heading.astype(F32) * float(CAP), 0.0)
        rows[7:8, part] = jnp.sum(place, axis=0, keepdims=True) - 1.0


def spread_kernel(rows, cell, on, when, head, _, sources, parcels):
    at_z = lax.broadcasted_iota(jnp.int32, (NZ, CHUNK), 0)
    at_xy = lax.broadcasted_iota(jnp.int32, (B * B, CHUNK), 0)
    at_high = lax.broadcasted_iota(jnp.int32, (B, CHUNK), 0)
    total = jnp.zeros((4 * B * B, NZ), F32)
    moved = jnp.zeros((10 * B, NZ), F32)
    across = (((1,), (1,)), ((), ()))
    for n in range(PD // CHUNK):
        part = slice(n * CHUNK, (n + 1) * CHUNK)
        cells = cell[:, part]
        in_z = jnp.where(at_z == (cells & (NZ - 1)), 1.0, 0.0).astype(BF16)
        in_xy = at_xy == (cells >> 8)
        pieces = [*split(rows[5:6, part]), *split(rows[6:7, part])]
        given = jnp.concatenate([jnp.where(in_xy, piece, 0.0).astype(BF16) for piece in pieces], axis=0)
        total = total + lax.dot_general(given, in_z, across, preferred_element_type=F32)
        place = rows[7:8, part].astype(jnp.int32)
        in_low = jnp.where(at_z == (place & (NZ - 1)), 1.0, 0.0).astype(BF16)
        in_high = at_high == (place >> 8)
        split_up = [split(rows[f : f + 1, part]) for f in range(5)]
        leaving = [jnp.where(in_high, split_up[f][piece], 0.0) for piece in range(2) for f in range(5)]
        moved = moved + lax.dot_general(
            jnp.concatenate(leaving, axis=0).astype(BF16), in_low, across, preferred_element_type=F32
        )
    q = B * B
    steam = total[2 * q : 3 * q] + total[3 * q :]
    sources[0] = total[:q] + total[q : 2 * q]
    sources[1] = -2.0 * steam
    sources[2] = steam
    lanes = lax.broadcasted_iota(jnp.int32, (1, NZ), 1)
    for s in range(B):
        ramp = jnp.clip((100.0 - when[0, s].astype(F32)) / 50.0, 0.0, 1.0)
        strength = 3.0 * ramp * on[0, s].astype(F32)
        where = head[0, s]
        row = pl.ds(where >> 8, 1)
        taken = jnp.where(lanes == (where & (NZ - 1)), strength, 0.0)
        for f in range(2):
            sources[f, row, :] = sources[f, row, :] - taken
    moved = moved[: 5 * B] + moved[5 * B :]
    for d in range(4):
        for f in range(5):
            for half in range(2):
                at = f * B + 2 * d + half
                r = 2 * f + half
                parcels[d, r // B, r % B : r % B + 1, :] = moved[at : at + 1]
        parcels[d, 1, 2:, :] = jnp.zeros((B - 2, NZ), F32)


def pack_x_kernel(gas, guess, y_even, y_odd, _, even, odd):
    def planes(low, high):
        for side, near, step in ((low, 0, 1), (high, B - 1, -1)):
            for r, (field, depth) in enumerate(X_LAYERS):
                x = near + step * depth
                side[r] = guess[x] if field == 5 else gas[field, x]

            def corners(below, above, side=side, near=near, step=step):
                for h, halo in enumerate((below, above)):
                    for r, (layer, x) in enumerate(((3, near), (4, near), (0, near), (0, near + step))):
                        side[NL, 4 * h + r : 4 * h + r + 1, :] = halo[layer, x : x + 1, :]

            by_parity("gy", corners, y_even, y_odd)

    by_parity("gx", planes, even, odd)


def beside(value, by):
    lane = lax.broadcasted_iota(jnp.int32, value.shape, 1)
    turned = pltpu.roll(value, (-by) % NZ, axis=1)
    return jnp.where((lane < NZ - by) if by > 0 else (lane >= -by), turned, 0.0)


def advance(e, f, x, rows, first):
    def at(field, dx, dy):
        return e[field, x + dx, first + dy : first + dy + rows, :]

    centre = at(f, 0, 0)
    xs = {s: at(f, s, 0) for s in (-2, -1, 1, 2)}
    ys = {s: at(f, 0, s) for s in (-2, -1, 1, 2)}
    zs = {s: beside(centre, s) for s in (-2, -1, 1, 2)}
    laplace = xs[1] + xs[-1] + ys[1] + ys[-1] + zs[1] + zs[-1] - 6.0 * centre
    transport = 0.0
    for axis, shifted in enumerate((xs, ys, zs)):
        slope = 8.0 * (shifted[1] - shifted[-1]) - (shifted[2] - shifted[-2])
        transport = transport + at(axis, 0, 0) * slope
    return centre + (0.02 * laplace - (0.2 / 12.0) * transport)


def fill_own(gas, e, fields):
    for k, f in enumerate(fields):
        e[k, 3 : 3 + B, B : 2 * B, :] = gas[f]


def predict_kernel(gas, guess, y_even, y_odd, x_even, x_odd, sources, parcels, star, even, odd, e, wide, tall, q):
    gx = lax.axis_index("gx")
    gy = lax.axis_index("gy")
    has_left, has_right = gx > 0, gx < lax.axis_size("gx") - 1
    has_below, has_above = gy > 0, gy < lax.axis_size("gy") - 1
    fill_own(gas, e, range(3))
    q[1 : 1 + B, B : 2 * B, :] = guess[...]

    def fill_y(below, above):
        for r, (field, depth) in enumerate(Y_LAYERS):
            for halo, y in ((below, B - 1 - depth), (above, 2 * B + depth)):
                if field == 5:
                    q[1 : 1 + B, y, :] = halo[r]
                elif field < 3:
                    e[field, 3 : 3 + B, y, :] = halo[r]

    def fill_x(left, right):
        for r, (field, depth) in enumerate(X_LAYERS):
            for halo, x in ((left, -1 - depth), (right, B + depth)):
                if field == 5:
                    q[x + 1, B : 2 * B, :] = halo[r]
                elif field < 3:
                    e[field, x + 3, B : 2 * B, :] = halo[r]
        for halo, near, step in ((left, 2, -1), (right, 3 + B, 1)):
            for h, (y, onward) in enumerate(((B - 1, -1), (2 * B, 1))):
                spots = ((0, near, y), (0, near, y + onward), (1, near, y), (1, near + step, y))
                for r, (field, x, row) in enumerate(spots):
                    e[field, x, row : row + 1, :] = halo[NL, 4 * h + r : 4 * h + r + 1, :]

    by_parity("gy", fill_y, y_even, y_odd)
    by_parity("gx", fill_x, x_even, x_odd)
    for x in range(-1, B + 1):
        value = advance(e, 0, x + 3, B, B)
        if x < 0:
            value = jnp.where(has_left, value, 0.0)
        if x == B:
            value = jnp.where(has_right, value, 0.0)
        wide[x + 1] = value
        if 0 <= x < B:
            star[0, x] = value
    for x in range(B):
        value = advance(e, 1, x + 3, B + 2, B - 1)
        row = lax.broadcasted_iota(jnp.int32, value.shape, 0)
        inside = ((row > 0) | has_below) & ((row < B + 1) | has_above)
        value = jnp.where(inside, value, 0.0)
        tall[x, : B + 2, :] = value
        star[1, x] = value[1 : 1 + B]
    for x in range(B):
        w = advance(e, 2, x + 3, B, B) + 0.2 * sources[0, x]
        star[2, x] = w
        spread = wide[x + 2] - wide[x] + (tall[x, 2 : 2 + B, :] - tall[x, :B, :])
        source = 2.5 * (spread + (beside(w, 1) - beside(w, -1)))
        centre = q[x + 1, B : 2 * B, :]
        around = q[x + 2, B : 2 * B, :] + q[x, B : 2 * B, :]
        around = around + q[x + 1, B + 1 : 2 * B + 1, :] + q[x + 1, B - 1 : 2 * B - 1, :]
        field = (around + beside(centre, 1) + beside(centre, -1) - source) * (1.0 / 6.0)
        for side in (even, odd):
            side[x] = field
            side[B + x] = source

    def attach(low, high):
        for side, heading in ((high, 2), (low, 3)):
            side[2 * B] = parcels[heading, 0]
            side[2 * B + 1] = parcels[heading, 1]

    by_parity("gy", attach, even, odd)


def scalars_kernel(gas, y_even, y_odd, x_even, x_odd, sources, _, star, e):
    fill_own(gas, e, range(5))

    def fill_y(below, above):
        for r, (field, depth) in enumerate(Y_LAYERS):
            if field in (3, 4):
                e[field, 3 : 3 + B, B - 1 - depth, :] = below[r]
                e[field, 3 : 3 + B, 2 * B + depth, :] = above[r]

    def fill_x(left, right):
        for r, (field, depth) in enumerate(X_LAYERS):
            if field in (3, 4):
                e[field, 2 - depth, B : 2 * B, :] = left[r]
                e[field, B + 3 + depth, B : 2 * B, :] = right[r]

    by_parity("gy", fill_y, y_even, y_odd)
    by_parity("gx", fill_x, x_even, x_odd)
    for f in (3, 4):
        for x in range(B):
            star[f - 3, x] = advance(e, f, x + 3, B, B) + 0.2 * sources[f - 2, x]


NX2 = 28


def pack_x2_kernel(own, y_even, y_odd, parcels, even, odd):
    row = lax.broadcasted_iota(jnp.int32, (B, NZ), 0)
    base = 2 * B - 1

    def planes(low, high):
        for side, near, step, heading in ((low, -1, 1, 1), (high, B, -1, 0)):
            for d in range(1, B + 1):
                side[d - 1] = own[near + step * d]
            for d in range(1, B):
                side[base + d - 1] = own[B + near + step * d]
            side[NX2] = parcels[heading, 0]
            side[NX2 + 1] = parcels[heading, 1]

            def merged(below, above, side=side, near=near, step=step):
                for m in range(1, B):
                    lower = below[near + step * m]
                    upper = above[near + step * (B - m)]
                    side[B - 1 + m] = jnp.where(row >= m, lower, upper)
                for m in range(1, B - 1):
                    lower = below[B + near + step * m]
                    upper = above[B + near + step * (B - 1 - m)]
                    side[base + B - 2 + m] = jnp.where(row >= m + 1, lower, upper)

            by_parity("gy", merged, y_even, y_odd)

    by_parity("gx", planes, even, odd)


def finish_kernel(star, star_rest, own, y_even, y_odd, x_even, x_odd, gas_next, pressure, arrived, p0, p1, s, c):
    gx = lax.axis_index("gx")
    gy = lax.axis_index("gy")
    inside_x = [gx > 0, None, gx < lax.axis_size("gx") - 1]
    inside_y = [gy > 0, None, gy < lax.axis_size("gy") - 1]
    for i in range(3):
        for j in range(3):
            value = jnp.full((B, NZ), 1.0 / 6.0, F32)
            for flag in (inside_x[i], inside_y[j]):
                if flag is not None:
                    value = jnp.where(flag, value, 0.0)
            c[i, j * B : (j + 1) * B, :] = value
    for x in range(B):
        p0[B + x, B : 2 * B, :] = own[x]
        s[B + x, B : 2 * B, :] = own[B + x]
    base = 2 * B - 1

    def arrive(d, halo, at):
        for f in range(5):
            for half in range(2):
                r = 2 * f + half
                arrived[d, f, :, half * NZ : (half + 1) * NZ] = halo[at + r // B, r % B : r % B + 1, :]

    def fill_y(below, above):
        for x in range(B):
            for k, halo in ((0, below), (2, above)):
                p0[B + x, k * B : (k + 1) * B, :] = halo[x]
                s[B + x, k * B : (k + 1) * B, :] = halo[B + x]
        arrive(2, below, 2 * B)
        arrive(3, above, 2 * B)

    def fill_x(left, right):
        for halo, near, step in ((left, B, -1), (right, 2 * B - 1, 1)):
            for d in range(1, B + 1):
                p0[near + step * d, B : 2 * B, :] = halo[d - 1]
                if d < B:
                    s[near + step * d, B : 2 * B, :] = halo[base + d - 1]
            for m in range(1, B):
                piece = halo[B - 1 + m]
                p0[near + step * m, :B, :] = piece
                p0[near + step * (B - m), 2 * B :, :] = piece
            for m in range(1, B - 1):
                piece = halo[base + B - 2 + m]
                s[near + step * m, :B, :] = piece
                s[near + step * (B - 1 - m), 2 * B :, :] = piece
            p0[near + step * B, :B, :] = halo[0]
            p0[near + step * B, 2 * B :, :] = halo[0]
            s[near + step * (B - 1), :B, :] = halo[0]
            s[near + step * (B - 1), 2 * B :, :] = halo[0]
        arrive(0, left, NX2)
        arrive(1, right, NX2)

    by_parity("gy", fill_y, y_even, y_odd)
    by_parity("gx", fill_x, x_even, x_odd)
    now, later = p0, p1
    for turn in range(2, 9):
        reach = 9 - turn
        for x in range(B - reach, 2 * B + reach):
            centre = now[x]
            around = now[x - 1] + now[x + 1]
            around = around + pltpu.roll(centre, 1, axis=0) + pltpu.roll(centre, 3 * B - 1, axis=0)
            around = around + beside(centre, 1) + beside(centre, -1)
            later[x] = (around - s[x]) * c[0 if x < B else (1 if x < 2 * B else 2)]
        now, later = later, now
    for x in range(B):
        centre = now[B + x, B : 2 * B, :]
        pressure[x] = centre
        gas_next[0, x] = star[0, x] - 0.1 * (now[B + x + 1, B : 2 * B, :] - now[B + x - 1, B : 2 * B, :])
        gas_next[1, x] = star[1, x] - 0.1 * (now[B + x, B + 1 : 2 * B + 1, :] - now[B + x, B - 1 : 2 * B - 1, :])
        gas_next[2, x] = star[2, x] - 0.1 * (beside(centre, 1) - beside(centre, -1))
        gas_next[3, x] = star_rest[0, x]
        gas_next[4, x] = star_rest[1, x]


def body(gas, guess, motion, size, cell, target, on, when, head):
    shape = jax.ShapeDtypeStruct
    y_even, y_odd = call(pack_y_kernel, [tiles(NL)] * 2, 2, 10**6)(gas, guess)
    y_odd = swap(y_odd, "gy", 1)
    y_even = swap(y_even, "gy", 0)
    kept, rows = call(renew_kernel, [shape((5, 1, PD), F32), shape((8, PD), F32)], 5, 10**9)(
        gas, motion, size, cell, target
    )
    x_even, x_odd = call(pack_x_kernel, [tiles(NL + 1)] * 2, 5, 10**6)(gas, guess, y_even, y_odd, rows)
    sources, parcels = call(
        spread_kernel,
        [shape((3, B * B, NZ), F32), shape((4, 2, B, NZ), F32)],
        6,
        10**9,
        smem=(2, 3, 4),
    )(rows, cell, on, when, head, x_odd)
    sources = sources.reshape(3, B, B, NZ)
    x_even = swap(x_even, "gx", 0)
    x_odd = swap(x_odd, "gx", 1)
    wide = pltpu.VMEM((5, B + 6, 3 * B, NZ), F32)
    star, ps_even, ps_odd = call(
        predict_kernel,
        [shape((3, B, B, NZ), F32), tiles(2 * B + 2), tiles(2 * B + 2)],
        8,
        10**7,
        scratch=[
            wide,
            pltpu.VMEM((B + 2, B, NZ), F32),
            pltpu.VMEM((B, 2 * B, NZ), F32),
            pltpu.VMEM((B + 2, 3 * B, NZ), F32),
        ],
    )(gas, guess, y_even, y_odd, x_even, x_odd, sources, parcels)
    [star_rest] = call(scalars_kernel, [shape((2, B, B, NZ), F32)], 7, 10**8, scratch=[wide])(
        gas, y_even, y_odd, x_even, x_odd, sources, ps_odd
    )
    y_odd = swap(ps_odd, "gy", 1)
    y_even = swap(ps_even, "gy", 0)
    x_even, x_odd = call(pack_x2_kernel, [tiles(NX2 + 2)] * 2, 4, 10**6)(ps_even, y_even, y_odd, parcels)
    x_even = swap(x_even, "gx", 0)
    x_odd = swap(x_odd, "gx", 1)
    gas_next, pressure, arrived = call(
        finish_kernel,
        [shape((5, B, B, NZ), F32), shape((B, B, NZ), F32), shape((4, 5, 1, CAP), F32)],
        7,
        10**7,
        scratch=[
            pltpu.VMEM((3 * B, 3 * B, NZ), F32),
            pltpu.VMEM((3 * B, 3 * B, NZ), F32),
            pltpu.VMEM((3 * B, 3 * B, NZ), F32),
            pltpu.VMEM((3, 3 * B, NZ), F32),
        ],
    )(star, star_rest, ps_even, y_even, y_odd, x_even, x_odd)
    return gas_next, pressure, kept, arrived


def solution(mesh):
    in_specs = (
        P(None, "gx", "gy", None),
        P("gx", "gy", None),
        P(None, "gx", "gy"),
        P("gx", "gy"),
        P("gx", "gy"),
        P("gx", "gy"),
        P("gx", "gy"),
        P("gx", "gy"),
        P("gx", "gy"),
    )
    out_specs = (
        P(None, "gx", "gy", None),
        P("gx", "gy", None),
        P(None, "gx", "gy"),
        P(None, None, "gx", "gy"),
    )
    return jax.shard_map(body, mesh=mesh, in_specs=in_specs, out_specs=out_specs, check_vma=False)
```

```python
import jax
import jax.numpy as jnp
from jax import lax
from jax.experimental import pallas as pl
from jax.experimental.pallas import tpu as pltpu
from jax.sharding import PartitionSpec as P

B = 8
NZ = 256
PD = 4096
CAP = 512
CHUNK = 512
F32 = jnp.float32
BF16 = jnp.bfloat16
VMEM = pl.BlockSpec(memory_space=pltpu.VMEM)
SMEM = pl.BlockSpec(memory_space=pltpu.SMEM)

Y_LAYERS = [(1, 0), (1, 1), (1, 2), (0, 0), (0, 1), (2, 0), (2, 1), (3, 0), (3, 1), (4, 0), (4, 1), (5, 0)]
X_LAYERS = [(0, 0), (0, 1), (0, 2), (1, 0), (1, 1), (2, 0), (2, 1), (3, 0), (3, 1), (4, 0), (4, 1), (5, 0)]
NL = 12


def params(limit=16):
    return pltpu.CompilerParams(vmem_limit_bytes=limit * 1024 * 1024)


def tiles(n):
    return jax.ShapeDtypeStruct((n, B, NZ), F32)


def call(kernel, outs, n_in, cost, scratch=(), smem=(), limit=16):
    return pl.pallas_call(
        kernel,
        out_shape=outs,
        in_specs=[SMEM if i in smem else VMEM for i in range(n_in)],
        out_specs=[VMEM] * len(outs),
        scratch_shapes=list(scratch),
        compiler_params=params(limit),
        cost_estimate=pl.CostEstimate(flops=cost, bytes_accessed=cost // 8, transcendentals=0),
    )


def by_parity(axis, act, even, odd):
    first = lax.rem(lax.axis_index(axis), 2) == 0

    @pl.when(first)
    def _():
        act(odd, even)

    @pl.when(jnp.logical_not(first))
    def _():
        act(even, odd)


def swap(shard, axis, start):
    peers = lax.axis_size(axis)
    pairs = [(i + a, i + 1 - a) for i in range(start, peers - 1, 2) for a in range(2)]
    return lax.ppermute(shard, axis, pairs)


def pack_y_kernel(gas, edges, even, odd):
    def act(low, high):
        for r, (field, depth) in enumerate(Y_LAYERS):
            for side, y, edge in ((low, depth, 0), (high, B - 1 - depth, 1)):
                side[r] = edges[edge] if field == 5 else gas[field, :, y, :]

    by_parity("gy", act, even, odd)


def split(value):
    high = value.astype(BF16).astype(F32)
    return high, value - high


def place_kernel(target, place):
    heading = lax.broadcasted_iota(jnp.int32, (B, CHUNK), 0)
    a = lax.broadcasted_iota(jnp.int32, (CHUNK, CHUNK), 0)
    b = lax.broadcasted_iota(jnp.int32, (CHUNK, CHUNK), 1)
    upper = jnp.where(a <= b, 1.0, 0.0).astype(BF16)
    before = jnp.zeros((B, 1), F32)
    for n in range(PD // CHUNK):
        part = slice(n * CHUNK, (n + 1) * CHUNK)
        chosen = heading == target[:, part]
        rank = jnp.dot(jnp.where(chosen, 1.0, 0.0).astype(BF16), upper, preferred_element_type=F32) + before
        before = rank[:, CHUNK - 1 :]
        leaves = chosen & (heading < 4)
        value = jnp.where(leaves, rank + heading.astype(F32) * float(CAP), 0.0)
        place[:, part] = jnp.sum(value, axis=0, keepdims=True).astype(jnp.int32) - 1


def droplet_kernel(gas, motion, size, cell, target, place, on, when, head, _, sources, parcels, kept):
    table = jnp.concatenate([gas[f].reshape(B * B, NZ) for f in range(4)], axis=0)
    high, low = split(table)
    table = jnp.concatenate([high.astype(BF16), low.astype(BF16)], axis=1)
    at_z = lax.broadcasted_iota(jnp.int32, (NZ, CHUNK), 0)
    at_xy = lax.broadcasted_iota(jnp.int32, (B * B, CHUNK), 0)
    at_high = lax.broadcasted_iota(jnp.int32, (B, CHUNK), 0)
    total = jnp.zeros((4 * B * B, NZ), F32)
    moved = jnp.zeros((10 * B, NZ), F32)
    across = (((1,), (1,)), ((), ()))
    for n in range(PD // CHUNK):
        part = slice(n * CHUNK, (n + 1) * CHUNK)
        cells = cell[:, part]
        goal = target[:, part]
        in_z = jnp.where(at_z == (cells & (NZ - 1)), 1.0, 0.0).astype(BF16)
        in_xy = at_xy == (cells >> 8)
        found = jnp.dot(table, jnp.concatenate([in_z, in_z], axis=0), preferred_element_type=F32)
        local = [
            jnp.sum(jnp.where(in_xy, found[f * B * B : (f + 1) * B * B], 0.0), axis=0, keepdims=True)
            for f in range(4)
        ]
        u, v, w, temperature = (motion[f, :, part] for f in range(4))
        diameter = size[:, part]
        excess = local[3] - temperature
        vapour = 0.5 * diameter * jax.nn.sigmoid(excess)
        renewed = [
            u + 0.4 * (local[0] - u),
            v + 0.4 * (local[1] - v),
            w + 0.2 * ((local[2] - w) * 2.0 - 1.0),
            temperature + 0.2 * excess,
            diameter - 0.2 * vapour,
        ]
        drag = 0.5 * diameter * diameter * (w - local[2])
        alive = goal >= 0
        for f in range(5):
            kept[f, :, part] = jnp.where(goal == 4, renewed[f], 0.0)
        pieces = [*split(jnp.where(alive, drag, 0.0)), *split(jnp.where(alive, vapour, 0.0))]
        given = jnp.concatenate([jnp.where(in_xy, piece, 0.0).astype(BF16) for piece in pieces], axis=0)
        total = total + lax.dot_general(given, in_z, across, preferred_element_type=F32)
        spot = place[:, part]
        in_low = jnp.where(at_z == (spot & (NZ - 1)), 1.0, 0.0).astype(BF16)
        in_high = at_high == (spot >> 8)
        split_up = [split(value) for value in renewed]
        leaving = [jnp.where(in_high, split_up[f][piece], 0.0) for piece in range(2) for f in range(5)]
        moved = moved + lax.dot_general(
            jnp.concatenate(leaving, axis=0).astype(BF16), in_low, across, preferred_element_type=F32
        )
    q = B * B
    steam = total[2 * q : 3 * q] + total[3 * q :]
    sources[0] = total[:q] + total[q : 2 * q]
    sources[1] = -2.0 * steam
    sources[2] = steam
    lanes = lax.broadcasted_iota(jnp.int32, (1, NZ), 1)
    for s in range(B):
        ramp = jnp.clip((100.0 - when[0, s].astype(F32)) / 50.0, 0.0, 1.0)
        strength = 3.0 * ramp * on[0, s].astype(F32)
        where = head[0, s]
        row = pl.ds(where >> 8, 1)
        taken = jnp.where(lanes == (where & (NZ - 1)), strength, 0.0)
        for f in range(2):
            sources[f, row, :] = sources[f, row, :] - taken
    moved = moved[: 5 * B] + moved[5 * B :]
    for d in range(4):
        for f in range(5):
            for half in range(2):
                at = f * B + 2 * d + half
                r = 2 * f + half
                parcels[d, r // B, r % B : r % B + 1, :] = moved[at : at + 1]
        parcels[d, 1, 2:, :] = jnp.zeros((B - 2, NZ), F32)


def pack_x_kernel(gas, guess, y_odd, y_even, _, even, odd):
    def planes(low, high):
        for side, near, step in ((low, 0, 1), (high, B - 1, -1)):
            for r, (field, depth) in enumerate(X_LAYERS):
                x = near + step * depth
                side[r] = guess[x] if field == 5 else gas[field, x]

            def corners(below, above, side=side, near=near, step=step):
                for h, halo in enumerate((below, above)):
                    for r, (layer, x) in enumerate(((3, near), (4, near), (0, near), (0, near + step))):
                        side[NL, 4 * h + r : 4 * h + r + 1, :] = halo[layer, x : x + 1, :]

            by_parity("gy", corners, y_even, y_odd)

    by_parity("gx", planes, even, odd)


def beside(value, by):
    lane = lax.broadcasted_iota(jnp.int32, value.shape, 1)
    turned = pltpu.roll(value, (-by) % NZ, axis=1)
    return jnp.where((lane < NZ - by) if by > 0 else (lane >= -by), turned, 0.0)


def advance(e, f, x, rows, first):
    def at(field, dx, dy):
        return e[field, x + dx, first + dy : first + dy + rows, :]

    centre = at(f, 0, 0)
    xs = {s: at(f, s, 0) for s in (-2, -1, 1, 2)}
    ys = {s: at(f, 0, s) for s in (-2, -1, 1, 2)}
    zs = {s: beside(centre, s) for s in (-2, -1, 1, 2)}
    laplace = xs[1] + xs[-1] + ys[1] + ys[-1] + zs[1] + zs[-1] - 6.0 * centre
    transport = 0.0
    for axis, shifted in enumerate((xs, ys, zs)):
        slope = 8.0 * (shifted[1] - shifted[-1]) - (shifted[2] - shifted[-2])
        transport = transport + at(axis, 0, 0) * slope
    return centre + (0.02 * laplace - (0.2 / 12.0) * transport)


def fill_own(gas, e, fields):
    for k, f in enumerate(fields):
        e[k, 3 : 3 + B, B : 2 * B, :] = gas[f]


def predict_kernel(gas, guess, y_odd, y_even, x_odd, x_even, sources, parcels, star, even, odd, e, wide, tall, q):
    gx = lax.axis_index("gx")
    gy = lax.axis_index("gy")
    has_left, has_right = gx > 0, gx < lax.axis_size("gx") - 1
    has_below, has_above = gy > 0, gy < lax.axis_size("gy") - 1
    fill_own(gas, e, range(3))
    q[1 : 1 + B, B : 2 * B, :] = guess[...]

    def fill_y(below, above):
        for r, (field, depth) in enumerate(Y_LAYERS):
            for halo, y in ((below, B - 1 - depth), (above, 2 * B + depth)):
                if field == 5:
                    q[1 : 1 + B, y, :] = halo[r]
                elif field < 3:
                    e[field, 3 : 3 + B, y, :] = halo[r]

    def fill_x(left, right):
        for r, (field, depth) in enumerate(X_LAYERS):
            for halo, x in ((left, -1 - depth), (right, B + depth)):
                if field == 5:
                    q[x + 1, B : 2 * B, :] = halo[r]
                elif field < 3:
                    e[field, x + 3, B : 2 * B, :] = halo[r]
        for halo, near, step in ((left, 2, -1), (right, 3 + B, 1)):
            for h, (y, onward) in enumerate(((B - 1, -1), (2 * B, 1))):
                spots = ((0, near, y), (0, near, y + onward), (1, near, y), (1, near + step, y))
                for r, (field, x, row) in enumerate(spots):
                    e[field, x, row : row + 1, :] = halo[NL, 4 * h + r : 4 * h + r + 1, :]

    by_parity("gy", fill_y, y_even, y_odd)
    by_parity("gx", fill_x, x_even, x_odd)
    for x in range(-1, B + 1):
        value = advance(e, 0, x + 3, B, B)
        if x < 0:
            value = jnp.where(has_left, value, 0.0)
        if x == B:
            value = jnp.where(has_right, value, 0.0)
        wide[x + 1] = value
        if 0 <= x < B:
            star[0, x] = value
    for x in range(B):
        value = advance(e, 1, x + 3, B + 2, B - 1)
        row = lax.broadcasted_iota(jnp.int32, value.shape, 0)
        inside = ((row > 0) | has_below) & ((row < B + 1) | has_above)
        value = jnp.where(inside, value, 0.0)
        tall[x, : B + 2, :] = value
        star[1, x] = value[1 : 1 + B]
    for x in range(B):
        w = advance(e, 2, x + 3, B, B) + 0.2 * sources[0, x]
        star[2, x] = w
        spread = wide[x + 2] - wide[x] + (tall[x, 2 : 2 + B, :] - tall[x, :B, :])
        source = 2.5 * (spread + (beside(w, 1) - beside(w, -1)))
        centre = q[x + 1, B : 2 * B, :]
        around = q[x + 2, B : 2 * B, :] + q[x, B : 2 * B, :]
        around = around + q[x + 1, B + 1 : 2 * B + 1, :] + q[x + 1, B - 1 : 2 * B - 1, :]
        field = (around + beside(centre, 1) + beside(centre, -1) - source) * (1.0 / 6.0)
        for side in (even, odd):
            side[x] = field
            side[B + x] = source

    def attach(low, high):
        for side, heading in ((high, 2), (low, 3)):
            side[2 * B] = parcels[heading, 0]
            side[2 * B + 1] = parcels[heading, 1]

    by_parity("gy", attach, even, odd)


def scalars_kernel(gas, y_odd, y_even, x_odd, x_even, sources, _, star, e):
    fill_own(gas, e, range(5))

    def fill_y(below, above):
        for r, (field, depth) in enumerate(Y_LAYERS):
            if field in (3, 4):
                e[field, 3 : 3 + B, B - 1 - depth, :] = below[r]
                e[field, 3 : 3 + B, 2 * B + depth, :] = above[r]

    def fill_x(left, right):
        for r, (field, depth) in enumerate(X_LAYERS):
            if field in (3, 4):
                e[field, 2 - depth, B : 2 * B, :] = left[r]
                e[field, B + 3 + depth, B : 2 * B, :] = right[r]

    by_parity("gy", fill_y, y_even, y_odd)
    by_parity("gx", fill_x, x_even, x_odd)
    for f in (3, 4):
        for x in range(B):
            star[f - 3, x] = advance(e, f, x + 3, B, B) + 0.2 * sources[f - 2, x]


NX2 = 28


def pack_x2_kernel(own, y_even, y_odd, parcels, even, odd):
    row = lax.broadcasted_iota(jnp.int32, (B, NZ), 0)
    base = 2 * B - 1

    def planes(low, high):
        for side, near, step, heading in ((low, -1, 1, 1), (high, B, -1, 0)):
            for d in range(1, B + 1):
                side[d - 1] = own[near + step * d]
            for d in range(1, B):
                side[base + d - 1] = own[B + near + step * d]
            side[NX2] = parcels[heading, 0]
            side[NX2 + 1] = parcels[heading, 1]

            def merged(below, above, side=side, near=near, step=step):
                for m in range(1, B):
                    lower = below[near + step * m]
                    upper = above[near + step * (B - m)]
                    side[B - 1 + m] = jnp.where(row >= m, lower, upper)
                for m in range(1, B - 1):
                    lower = below[B + near + step * m]
                    upper = above[B + near + step * (B - 1 - m)]
                    side[base + B - 2 + m] = jnp.where(row >= m + 1, lower, upper)

            by_parity("gy", merged, y_even, y_odd)

    by_parity("gx", planes, even, odd)


def finish_kernel(star, star_rest, own, y_even, y_odd, x_odd, x_even, gas_next, pressure, arrived, p0, p1, s, c):
    gx = lax.axis_index("gx")
    gy = lax.axis_index("gy")
    inside_x = [gx > 0, None, gx < lax.axis_size("gx") - 1]
    inside_y = [gy > 0, None, gy < lax.axis_size("gy") - 1]
    for i in range(3):
        for j in range(3):
            value = jnp.full((B, NZ), 1.0 / 6.0, F32)
            for flag in (inside_x[i], inside_y[j]):
                if flag is not None:
                    value = jnp.where(flag, value, 0.0)
            c[i, j * B : (j + 1) * B, :] = value
    for x in range(B):
        p0[B + x, B : 2 * B, :] = own[x]
        s[B + x, B : 2 * B, :] = own[B + x]
    base = 2 * B - 1

    def arrive(d, halo, at):
        for f in range(5):
            for half in range(2):
                r = 2 * f + half
                arrived[d, f, :, half * NZ : (half + 1) * NZ] = halo[at + r // B, r % B : r % B + 1, :]

    def fill_y(below, above):
        for x in range(B):
            for k, halo in ((0, below), (2, above)):
                p0[B + x, k * B : (k + 1) * B, :] = halo[x]
                s[B + x, k * B : (k + 1) * B, :] = halo[B + x]
        arrive(2, below, 2 * B)
        arrive(3, above, 2 * B)

    def fill_x(left, right):
        for halo, near, step in ((left, B, -1), (right, 2 * B - 1, 1)):
            for d in range(1, B + 1):
                p0[near + step * d, B : 2 * B, :] = halo[d - 1]
                if d < B:
                    s[near + step * d, B : 2 * B, :] = halo[base + d - 1]
            for m in range(1, B):
                piece = halo[B - 1 + m]
                p0[near + step * m, :B, :] = piece
                p0[near + step * (B - m), 2 * B :, :] = piece
            for m in range(1, B - 1):
                piece = halo[base + B - 2 + m]
                s[near + step * m, :B, :] = piece
                s[near + step * (B - 1 - m), 2 * B :, :] = piece
            p0[near + step * B, :B, :] = halo[0]
            p0[near + step * B, 2 * B :, :] = halo[0]
            s[near + step * (B - 1), :B, :] = halo[0]
            s[near + step * (B - 1), 2 * B :, :] = halo[0]
        arrive(0, left, NX2)
        arrive(1, right, NX2)

    by_parity("gy", fill_y, y_even, y_odd)
    by_parity("gx", fill_x, x_even, x_odd)
    now, later = p0, p1
    for turn in range(2, 9):
        reach = 9 - turn
        for x in range(B - reach, 2 * B + reach):
            centre = now[x]
            around = now[x - 1] + now[x + 1]
            around = around + pltpu.roll(centre, 1, axis=0) + pltpu.roll(centre, 3 * B - 1, axis=0)
            around = around + beside(centre, 1) + beside(centre, -1)
            later[x] = (around - s[x]) * c[0 if x < B else (1 if x < 2 * B else 2)]
        now, later = later, now
    for x in range(B):
        centre = now[B + x, B : 2 * B, :]
        pressure[x] = centre
        gas_next[0, x] = star[0, x] - 0.1 * (now[B + x + 1, B : 2 * B, :] - now[B + x - 1, B : 2 * B, :])
        gas_next[1, x] = star[1, x] - 0.1 * (now[B + x, B + 1 : 2 * B + 1, :] - now[B + x, B - 1 : 2 * B - 1, :])
        gas_next[2, x] = star[2, x] - 0.1 * (beside(centre, 1) - beside(centre, -1))
        gas_next[3, x] = star_rest[0, x]
        gas_next[4, x] = star_rest[1, x]


def body(gas, guess, motion, size, cell, target, on, when, head):
    shape = jax.ShapeDtypeStruct
    y_even, y_odd = call(pack_y_kernel, [tiles(NL)] * 2, 2, 10**6)(
        gas, jnp.stack([guess[:, 0], guess[:, B - 1]])
    )
    y_odd = swap(y_odd, "gy", 1)
    y_even = swap(y_even, "gy", 0)
    [place] = call(place_kernel, [shape((1, PD), jnp.int32)], 1, 10**9)(target)
    x_even, x_odd = call(pack_x_kernel, [tiles(NL + 1)] * 2, 5, 10**6)(gas, guess, y_odd, y_even, place)
    sources, parcels, kept = call(
        droplet_kernel,
        [shape((3, B * B, NZ), F32), shape((4, 2, B, NZ), F32), shape((5, 1, PD), F32)],
        10,
        2 * 10**9,
        smem=(6, 7, 8),
    )(gas, motion, size, cell, target, place, on, when, head, x_even)
    sources = sources.reshape(3, B, B, NZ)
    x_odd = swap(x_odd, "gx", 1)
    x_even = swap(x_even, "gx", 0)
    wide = pltpu.VMEM((5, B + 6, 3 * B, NZ), F32)
    star, ps_even, ps_odd = call(
        predict_kernel,
        [shape((3, B, B, NZ), F32), tiles(2 * B + 2), tiles(2 * B + 2)],
        8,
        10**7,
        scratch=[
            wide,
            pltpu.VMEM((B + 2, B, NZ), F32),
            pltpu.VMEM((B, 2 * B, NZ), F32),
            pltpu.VMEM((B + 2, 3 * B, NZ), F32),
        ],
    )(gas, guess, y_odd, y_even, x_odd, x_even, sources, parcels)
    [star_rest] = call(scalars_kernel, [shape((2, B, B, NZ), F32)], 7, 10**8, scratch=[wide])(
        gas, y_odd, y_even, x_odd, x_even, sources, ps_odd
    )
    y_odd = swap(ps_odd, "gy", 1)
    y_even = swap(ps_even, "gy", 0)
    x_even, x_odd = call(pack_x2_kernel, [tiles(NX2 + 2)] * 2, 4, 10**6)(ps_even, y_even, y_odd, parcels)
    x_odd = swap(x_odd, "gx", 1)
    x_even = swap(x_even, "gx", 0)
    gas_next, pressure, arrived = call(
        finish_kernel,
        [shape((5, B, B, NZ), F32), shape((B, B, NZ), F32), shape((4, 5, 1, CAP), F32)],
        7,
        10**7,
        scratch=[
            pltpu.VMEM((3 * B, 3 * B, NZ), F32),
            pltpu.VMEM((3 * B, 3 * B, NZ), F32),
            pltpu.VMEM((3 * B, 3 * B, NZ), F32),
            pltpu.VMEM((3, 3 * B, NZ), F32),
        ],
    )(star, star_rest, ps_even, y_even, y_odd, x_odd, x_even)
    return gas_next, pressure, kept, arrived


def solution(mesh):
    in_specs = (
        P(None, "gx", "gy", None),
        P("gx", "gy", None),
        P(None, "gx", "gy"),
        P("gx", "gy"),
        P("gx", "gy"),
        P("gx", "gy"),
        P("gx", "gy"),
        P("gx", "gy"),
        P("gx", "gy"),
    )
    out_specs = (
        P(None, "gx", "gy", None),
        P("gx", "gy", None),
        P(None, "gx", "gy"),
        P(None, None, "gx", "gy"),
    )
    return jax.shard_map(body, mesh=mesh, in_specs=in_specs, out_specs=out_specs, check_vma=False)
```

```python
import jax
import jax.numpy as jnp
from jax import lax
from jax.experimental import pallas as pl
from jax.experimental.pallas import tpu as pltpu
from jax.sharding import PartitionSpec as P

B = 8
NZ = 256
PD = 4096
CAP = 512
CHUNK = 512
F32 = jnp.float32
BF16 = jnp.bfloat16
VMEM = pl.BlockSpec(memory_space=pltpu.VMEM)
SMEM = pl.BlockSpec(memory_space=pltpu.SMEM)

Y_LAYERS = [(1, 0), (1, 1), (1, 2), (0, 0), (0, 1), (2, 0), (2, 1), (3, 0), (3, 1), (4, 0), (4, 1), (5, 0)]
X_LAYERS = [(0, 0), (0, 1), (0, 2), (1, 0), (1, 1), (2, 0), (2, 1), (3, 0), (3, 1), (4, 0), (4, 1), (5, 0)]
NL = 12


def params(limit=16):
    return pltpu.CompilerParams(vmem_limit_bytes=limit * 1024 * 1024)


def tiles(n):
    return jax.ShapeDtypeStruct((n, B, NZ), F32)


def call(kernel, outs, n_in, cost, scratch=(), smem=(), limit=16):
    return pl.pallas_call(
        kernel,
        out_shape=outs,
        in_specs=[SMEM if i in smem else VMEM for i in range(n_in)],
        out_specs=[VMEM] * len(outs),
        scratch_shapes=list(scratch),
        compiler_params=params(limit),
        cost_estimate=pl.CostEstimate(flops=cost, bytes_accessed=cost // 8, transcendentals=0),
    )


def by_parity(axis, act, even, odd):
    first = lax.rem(lax.axis_index(axis), 2) == 0

    @pl.when(first)
    def _():
        act(odd, even)

    @pl.when(jnp.logical_not(first))
    def _():
        act(even, odd)


def swap(shard, axis, start):
    peers = lax.axis_size(axis)
    pairs = [(i + a, i + 1 - a) for i in range(start, peers - 1, 2) for a in range(2)]
    return lax.ppermute(shard, axis, pairs)


def first_kernel(out):
    out[...] = jnp.zeros_like(out)


def pack_y_kernel(_, gas, guess, even, odd):
    def act(low, high):
        for r, (field, depth) in enumerate(Y_LAYERS):
            for side, y in ((low, depth), (high, B - 1 - depth)):
                side[r] = guess[:, y, :] if field == 5 else gas[field, :, y, :]

    by_parity("gy", act, even, odd)


def split(value):
    high = value.astype(BF16).astype(F32)
    return high, value - high


def place_kernel(target, place):
    heading = lax.broadcasted_iota(jnp.int32, (B, CHUNK), 0)
    a = lax.broadcasted_iota(jnp.int32, (CHUNK, CHUNK), 0)
    b = lax.broadcasted_iota(jnp.int32, (CHUNK, CHUNK), 1)
    upper = jnp.where(a <= b, 1.0, 0.0).astype(BF16)
    before = jnp.zeros((B, 1), F32)
    for n in range(PD // CHUNK):
        part = slice(n * CHUNK, (n + 1) * CHUNK)
        chosen = heading == target[:, part]
        rank = jnp.dot(jnp.where(chosen, 1.0, 0.0).astype(BF16), upper, preferred_element_type=F32) + before
        before = rank[:, CHUNK - 1 :]
        leaves = chosen & (heading < 4)
        value = jnp.where(leaves, rank + heading.astype(F32) * float(CAP), 0.0)
        place[:, part] = jnp.sum(value, axis=0, keepdims=True).astype(jnp.int32) - 1


def droplet_kernel(gas, motion, size, cell, target, place, on, when, head, _, sources, parcels, kept):
    table = jnp.concatenate([gas[f].reshape(B * B, NZ) for f in range(4)], axis=0)
    high, low = split(table)
    table = jnp.concatenate([high.astype(BF16), low.astype(BF16)], axis=1)
    at_z = lax.broadcasted_iota(jnp.int32, (NZ, CHUNK), 0)
    at_xy = lax.broadcasted_iota(jnp.int32, (B * B, CHUNK), 0)
    at_high = lax.broadcasted_iota(jnp.int32, (B, CHUNK), 0)
    total = jnp.zeros((4 * B * B, NZ), F32)
    moved = jnp.zeros((10 * B, NZ), F32)
    across = (((1,), (1,)), ((), ()))
    for n in range(PD // CHUNK):
        part = slice(n * CHUNK, (n + 1) * CHUNK)
        cells = cell[:, part]
        goal = target[:, part]
        in_z = jnp.where(at_z == (cells & (NZ - 1)), 1.0, 0.0).astype(BF16)
        in_xy = at_xy == (cells >> 8)
        found = jnp.dot(table, jnp.concatenate([in_z, in_z], axis=0), preferred_element_type=F32)
        local = [
            jnp.sum(jnp.where(in_xy, found[f * B * B : (f + 1) * B * B], 0.0), axis=0, keepdims=True)
            for f in range(4)
        ]
        u, v, w, temperature = (motion[f, :, part] for f in range(4))
        diameter = size[:, part]
        excess = local[3] - temperature
        vapour = 0.5 * diameter * jax.nn.sigmoid(excess)
        renewed = [
            u + 0.4 * (local[0] - u),
            v + 0.4 * (local[1] - v),
            w + 0.2 * ((local[2] - w) * 2.0 - 1.0),
            temperature + 0.2 * excess,
            diameter - 0.2 * vapour,
        ]
        drag = 0.5 * diameter * diameter * (w - local[2])
        alive = goal >= 0
        for f in range(5):
            kept[f, :, part] = jnp.where(goal == 4, renewed[f], 0.0)
        pieces = [*split(jnp.where(alive, drag, 0.0)), *split(jnp.where(alive, vapour, 0.0))]
        given = jnp.concatenate([jnp.where(in_xy, piece, 0.0).astype(BF16) for piece in pieces], axis=0)
        total = total + lax.dot_general(given, in_z, across, preferred_element_type=F32)
        spot = place[:, part]
        in_low = jnp.where(at_z == (spot & (NZ - 1)), 1.0, 0.0).astype(BF16)
        in_high = at_high == (spot >> 8)
        split_up = [split(value) for value in renewed]
        leaving = [jnp.where(in_high, split_up[f][piece], 0.0) for piece in range(2) for f in range(5)]
        moved = moved + lax.dot_general(
            jnp.concatenate(leaving, axis=0).astype(BF16), in_low, across, preferred_element_type=F32
        )
    q = B * B
    steam = total[2 * q : 3 * q] + total[3 * q :]
    sources[0] = total[:q] + total[q : 2 * q]
    sources[1] = -2.0 * steam
    sources[2] = steam
    lanes = lax.broadcasted_iota(jnp.int32, (1, NZ), 1)
    for s in range(B):
        ramp = jnp.clip((100.0 - when[0, s].astype(F32)) / 50.0, 0.0, 1.0)
        strength = 3.0 * ramp * on[0, s].astype(F32)
        where = head[0, s]
        row = pl.ds(where >> 8, 1)
        taken = jnp.where(lanes == (where & (NZ - 1)), strength, 0.0)
        for f in range(2):
            sources[f, row, :] = sources[f, row, :] - taken
    moved = moved[: 5 * B] + moved[5 * B :]
    for d in range(4):
        for f in range(5):
            for half in range(2):
                at = f * B + 2 * d + half
                r = 2 * f + half
                parcels[d, r // B, r % B : r % B + 1, :] = moved[at : at + 1]
        parcels[d, 1, 2:, :] = jnp.zeros((B - 2, NZ), F32)


def pack_x_kernel(gas, guess, y_odd, y_even, _, even, odd):
    def planes(low, high):
        for side, near, step in ((low, 0, 1), (high, B - 1, -1)):
            for r, (field, depth) in enumerate(X_LAYERS):
                x = near + step * depth
                side[r] = guess[x] if field == 5 else gas[field, x]

            def corners(below, above, side=side, near=near, step=step):
                for h, halo in enumerate((below, above)):
                    for r, (layer, x) in enumerate(((3, near), (4, near), (0, near), (0, near + step))):
                        side[NL, 4 * h + r : 4 * h + r + 1, :] = halo[layer, x : x + 1, :]

            by_parity("gy", corners, y_even, y_odd)

    by_parity("gx", planes, even, odd)


def beside(value, by):
    lane = lax.broadcasted_iota(jnp.int32, value.shape, 1)
    turned = pltpu.roll(value, (-by) % NZ, axis=1)
    return jnp.where((lane < NZ - by) if by > 0 else (lane >= -by), turned, 0.0)


def advance(e, f, x, rows, first):
    def at(field, dx, dy):
        return e[field, x + dx, first + dy : first + dy + rows, :]

    centre = at(f, 0, 0)
    xs = {s: at(f, s, 0) for s in (-2, -1, 1, 2)}
    ys = {s: at(f, 0, s) for s in (-2, -1, 1, 2)}
    zs = {s: beside(centre, s) for s in (-2, -1, 1, 2)}
    laplace = xs[1] + xs[-1] + ys[1] + ys[-1] + zs[1] + zs[-1] - 6.0 * centre
    transport = 0.0
    for axis, shifted in enumerate((xs, ys, zs)):
        slope = 8.0 * (shifted[1] - shifted[-1]) - (shifted[2] - shifted[-2])
        transport = transport + at(axis, 0, 0) * slope
    return centre + (0.02 * laplace - (0.2 / 12.0) * transport)


def fill_own(gas, e, fields):
    for k, f in enumerate(fields):
        e[k, 3 : 3 + B, B : 2 * B, :] = gas[f]


def predict_kernel(gas, guess, y_odd, y_even, x_odd, x_even, sources, parcels, star, even, odd, e, wide, tall, q):
    gx = lax.axis_index("gx")
    gy = lax.axis_index("gy")
    has_left, has_right = gx > 0, gx < lax.axis_size("gx") - 1
    has_below, has_above = gy > 0, gy < lax.axis_size("gy") - 1
    fill_own(gas, e, range(3))
    q[1 : 1 + B, B : 2 * B, :] = guess[...]

    def fill_y(below, above):
        for r, (field, depth) in enumerate(Y_LAYERS):
            for halo, y in ((below, B - 1 - depth), (above, 2 * B + depth)):
                if field == 5:
                    q[1 : 1 + B, y, :] = halo[r]
                elif field < 3:
                    e[field, 3 : 3 + B, y, :] = halo[r]

    def fill_x(left, right):
        for r, (field, depth) in enumerate(X_LAYERS):
            for halo, x in ((left, -1 - depth), (right, B + depth)):
                if field == 5:
                    q[x + 1, B : 2 * B, :] = halo[r]
                elif field < 3:
                    e[field, x + 3, B : 2 * B, :] = halo[r]
        for halo, near, step in ((left, 2, -1), (right, 3 + B, 1)):
            for h, (y, onward) in enumerate(((B - 1, -1), (2 * B, 1))):
                spots = ((0, near, y), (0, near, y + onward), (1, near, y), (1, near + step, y))
                for r, (field, x, row) in enumerate(spots):
                    e[field, x, row : row + 1, :] = halo[NL, 4 * h + r : 4 * h + r + 1, :]

    by_parity("gy", fill_y, y_even, y_odd)
    by_parity("gx", fill_x, x_even, x_odd)
    for x in range(-1, B + 1):
        value = advance(e, 0, x + 3, B, B)
        if x < 0:
            value = jnp.where(has_left, value, 0.0)
        if x == B:
            value = jnp.where(has_right, value, 0.0)
        wide[x + 1] = value
        if 0 <= x < B:
            star[0, x] = value
    for x in range(B):
        value = advance(e, 1, x + 3, B + 2, B - 1)
        row = lax.broadcasted_iota(jnp.int32, value.shape, 0)
        inside = ((row > 0) | has_below) & ((row < B + 1) | has_above)
        value = jnp.where(inside, value, 0.0)
        tall[x, : B + 2, :] = value
        star[1, x] = value[1 : 1 + B]
    for x in range(B):
        w = advance(e, 2, x + 3, B, B) + 0.2 * sources[0, x]
        star[2, x] = w
        spread = wide[x + 2] - wide[x] + (tall[x, 2 : 2 + B, :] - tall[x, :B, :])
        source = 2.5 * (spread + (beside(w, 1) - beside(w, -1)))
        centre = q[x + 1, B : 2 * B, :]
        around = q[x + 2, B : 2 * B, :] + q[x, B : 2 * B, :]
        around = around + q[x + 1, B + 1 : 2 * B + 1, :] + q[x + 1, B - 1 : 2 * B - 1, :]
        field = (around + beside(centre, 1) + beside(centre, -1) - source) * (1.0 / 6.0)
        for side in (even, odd):
            side[x] = field
            side[B + x] = source

    def attach(low, high):
        for side, heading in ((high, 2), (low, 3)):
            side[2 * B] = parcels[heading, 0]
            side[2 * B + 1] = parcels[heading, 1]

    by_parity("gy", attach, even, odd)


def scalars_kernel(gas, y_odd, y_even, x_odd, x_even, sources, _, star, e):
    fill_own(gas, e, range(5))

    def fill_y(below, above):
        for r, (field, depth) in enumerate(Y_LAYERS):
            if field in (3, 4):
                e[field, 3 : 3 + B, B - 1 - depth, :] = below[r]
                e[field, 3 : 3 + B, 2 * B + depth, :] = above[r]

    def fill_x(left, right):
        for r, (field, depth) in enumerate(X_LAYERS):
            if field in (3, 4):
                e[field, 2 - depth, B : 2 * B, :] = left[r]
                e[field, B + 3 + depth, B : 2 * B, :] = right[r]

    by_parity("gy", fill_y, y_even, y_odd)
    by_parity("gx", fill_x, x_even, x_odd)
    for f in (3, 4):
        for x in range(B):
            star[f - 3, x] = advance(e, f, x + 3, B, B) + 0.2 * sources[f - 2, x]


NH = 15
HALF = NZ // 2


def load(ref, *lead):
    return [[ref[(*lead, slice(B * t, B * t + B), slice(HALF * h, HALF * h + HALF))] for h in range(2)] for t in range(3)]


def store(ref, plane, *lead):
    for t in range(3):
        for h in range(2):
            ref[(*lead, slice(B * t, B * t + B), slice(HALF * h, HALF * h + HALF))] = plane[t][h]


def add(*planes):
    planes = [p for p in planes if p is not None]
    return [[sum((p[t][h] for p in planes[1:]), planes[0][t][h]) for h in range(2)] for t in range(3)]


def beside_plane(c):
    row = lax.broadcasted_iota(jnp.int32, (B, HALF), 0)
    lane = lax.broadcasted_iota(jnp.int32, (B, HALF), 1)
    top, bottom, start, end = row == 0, row == B - 1, lane == 0, lane == HALF - 1
    out = []
    for t in range(3):
        after = [pltpu.roll(c[t][h], 1, axis=1) for h in range(2)]
        ahead = [pltpu.roll(c[t][h], HALF - 1, axis=1) for h in range(2)]
        along_z = [
            jnp.where(start, 0.0, after[0]) + jnp.where(end, ahead[1], ahead[0]),
            jnp.where(start, after[0], after[1]) + jnp.where(end, 0.0, ahead[1]),
        ]
        tile = []
        for h in range(2):
            down = pltpu.roll(c[t][h], 1, axis=0)
            if t > 0:
                down = jnp.where(top, pltpu.roll(c[t - 1][h], 1, axis=0), down)
            up = pltpu.roll(c[t][h], B - 1, axis=0)
            if t < 2:
                up = jnp.where(bottom, pltpu.roll(c[t + 1][h], B - 1, axis=0), up)
            tile.append(along_z[h] + (down + up))
        out.append(tile)
    return out


def relax(centre, others, source, scale):
    total = add(*others, None if centre is None else beside_plane(centre))
    if source is not None:
        total = [[total[t][h] - source[t][h] for h in range(2)] for t in range(3)]
    return [[total[t][h] * scale[t] for h in range(2)] for t in range(3)]


def weights(flags_x, flags_y):
    out = []
    for flag_y in flags_y:
        value = jnp.full((B, HALF), 1.0 / 6.0, F32)
        for flag in (*flags_x, flag_y):
            if flag is not None:
                value = jnp.where(flag, value, 0.0)
        out.append(value)
    return out


def slab_kernel(own, y_odd, y_even, parcels, even, odd, first, source, f0, f1, low, high):
    gy = lax.axis_index("gy")
    scale = weights((), (gy > 0, None, gy < lax.axis_size("gy") - 1))
    row = lax.broadcasted_iota(jnp.int32, (B, HALF), 0)
    for x in range(B):
        first[x, B : 2 * B, :] = own[x]
        source[x, B : 2 * B, :] = own[B + x]

    def fill(below, above):
        for x in range(B):
            for k, halo in ((0, below), (2, above)):
                first[x, k * B : (k + 1) * B, :] = halo[x]
                source[x, k * B : (k + 1) * B, :] = halo[B + x]

    by_parity("gy", fill, y_even, y_odd)

    def keep(side, k, plane):
        for h in range(2):
            part = slice(HALF * h, HALF * h + HALF)
            side[k - 1, :, part] = plane[1][h]
            if k < B:
                side[B - 1 + k, k:, part] = plane[0][h][k:]
                side[2 * B - 1 - k, : B - k, part] = plane[2][h][: B - k]

    for side, x in ((low, 0), (high, B - 1)):
        keep(side, 1, load(first, x))
    now, later = first, f0
    for k in range(2, 9):
        depth = 9 - k
        for x in range(B):
            if depth <= x < B - depth:
                continue
            others = [load(now, y) for y in (x - 1, x + 1) if 0 <= y < B]
            plane = relax(load(now, x), others, load(source, x), scale)
            if k < 8:
                store(later, plane, x)
            for side, face in ((low, 0), (high, B - 1)):
                if x == face:
                    keep(side, k, plane)
        now, later = (f0, f1) if k == 2 else (later, now)
    for side, heading in ((low, 1), (high, 0)):
        side[NH] = parcels[heading, 0]
        side[NH + 1] = parcels[heading, 1]

    def send(low_out, high_out):
        low_out[...] = low[...]
        high_out[...] = high[...]

    by_parity("gx", send, even, odd)


def finish_kernel(star, star_rest, first, source, y_even, y_odd, x_odd, x_even, gas_next, pressure, arrived, o0, o1, r0, r1, hist):
    gx = lax.axis_index("gx")
    gy = lax.axis_index("gy")
    flags_y = (gy > 0, None, gy < lax.axis_size("gy") - 1)
    inner = weights((), flags_y)
    outer = [weights((gx > 0,), flags_y), weights((gx < lax.axis_size("gx") - 1,), flags_y)]

    def arrive(d, halo, at):
        for f in range(5):
            for half in range(2):
                r = 2 * f + half
                arrived[d, f, :, half * NZ : (half + 1) * NZ] = halo[at + r // B, r % B : r % B + 1, :]

    def take_y(below, above):
        arrive(2, below, 2 * B)
        arrive(3, above, 2 * B)

    def take_x(left, right):
        hist[0] = left[...]
        hist[1] = right[...]

    by_parity("gy", take_y, y_even, y_odd)
    by_parity("gx", take_x, x_even, x_odd)
    arrive(0, hist.at[0], NH)
    arrive(1, hist.at[1], NH)

    def history(side, k):
        at = (B - 1 + k, k - 1, 2 * B - 1 - k)
        return [[hist[side, at[t], :, slice(HALF * h, HALF * h + HALF)] for h in range(2)] for t in range(3)]

    owns = {1: first, **{k: (o0, o1)[k % 2] for k in range(2, 9)}}
    responses = {k: (r0, r1)[k % 2] for k in range(2, 9)}

    def at(k, x):
        if 0 <= x < B:
            return load(owns[k], x)
        side, depth = (0, -x) if x < 0 else (1, x - B + 1)
        return load(responses[k], side, depth - 1) if depth < k else None

    for k in range(2, 9):
        depth = min(k - 1, 9 - k)
        for x in range(-depth, B + depth):
            others = [at(k - 1, x - 1), at(k - 1, x + 1)]
            if 0 <= x < B:
                if x == 0:
                    others.append(history(0, k - 1))
                if x == B - 1:
                    others.append(history(1, k - 1))
                store(owns[k], relax(at(k - 1, x), others, load(source, x), inner), x)
            else:
                side, far = (0, -x) if x < 0 else (1, x - B + 1)
                store(responses[k], relax(at(k - 1, x), others, None, outer[side]), side, far - 1)
    last, edge = owns[8], responses[8]

    def level(x):
        if x < 0:
            return edge[0, 0, B : 2 * B, :] + hist[0, B - 1]
        if x >= B:
            return edge[1, 0, B : 2 * B, :] + hist[1, B - 1]
        return last[x, B : 2 * B, :]

    for x in range(B):
        centre = level(x)
        pressure[x] = centre
        gas_next[0, x] = star[0, x] - 0.1 * (level(x + 1) - level(x - 1))
        gas_next[1, x] = star[1, x] - 0.1 * (last[x, B + 1 : 2 * B + 1, :] - last[x, B - 1 : 2 * B - 1, :])
        gas_next[2, x] = star[2, x] - 0.1 * (beside(centre, 1) - beside(centre, -1))
        gas_next[3, x] = star_rest[0, x]
        gas_next[4, x] = star_rest[1, x]


def body(gas, guess, motion, size, cell, target, on, when, head):
    shape = jax.ShapeDtypeStruct
    [first] = call(first_kernel, [shape((B, 128), F32)], 0, 10**10)()
    y_even, y_odd = call(pack_y_kernel, [tiles(NL)] * 2, 3, 10**6)(first, gas, guess)
    y_odd = swap(y_odd, "gy", 1)
    y_even = swap(y_even, "gy", 0)
    [place] = call(place_kernel, [shape((1, PD), jnp.int32)], 1, 10**9)(target)
    x_even, x_odd = call(pack_x_kernel, [tiles(NL + 1)] * 2, 5, 10**6)(gas, guess, y_odd, y_even, place)
    sources, parcels, kept = call(
        droplet_kernel,
        [shape((3, B * B, NZ), F32), shape((4, 2, B, NZ), F32), shape((5, 1, PD), F32)],
        10,
        2 * 10**9,
        smem=(6, 7, 8),
    )(gas, motion, size, cell, target, place, on, when, head, x_even)
    sources = sources.reshape(3, B, B, NZ)
    x_odd = swap(x_odd, "gx", 1)
    x_even = swap(x_even, "gx", 0)
    wide = pltpu.VMEM((5, B + 6, 3 * B, NZ), F32)
    star, ps_even, ps_odd = call(
        predict_kernel,
        [shape((3, B, B, NZ), F32), tiles(2 * B + 2), tiles(2 * B + 2)],
        8,
        10**7,
        scratch=[
            wide,
            pltpu.VMEM((B + 2, B, NZ), F32),
            pltpu.VMEM((B, 2 * B, NZ), F32),
            pltpu.VMEM((B + 2, 3 * B, NZ), F32),
        ],
    )(gas, guess, y_odd, y_even, x_odd, x_even, sources, parcels)
    [star_rest] = call(scalars_kernel, [shape((2, B, B, NZ), F32)], 7, 10**8, scratch=[wide])(
        gas, y_odd, y_even, x_odd, x_even, sources, ps_odd
    )
    y_odd = swap(ps_odd, "gy", 1)
    y_even = swap(ps_even, "gy", 0)
    slab = shape((B, 3 * B, NZ), F32)
    scratch = pltpu.VMEM((B, 3 * B, NZ), F32)
    x_even, x_odd, first, source = call(
        slab_kernel,
        [tiles(NH + 2), tiles(NH + 2), slab, slab],
        4,
        10**7,
        scratch=[scratch, scratch, pltpu.VMEM((NH + 2, B, NZ), F32), pltpu.VMEM((NH + 2, B, NZ), F32)],
    )(ps_even, y_odd, y_even, parcels)
    x_odd = swap(x_odd, "gx", 1)
    x_even = swap(x_even, "gx", 0)
    response = pltpu.VMEM((2, 4, 3 * B, NZ), F32)
    gas_next, pressure, arrived = call(
        finish_kernel,
        [shape((5, B, B, NZ), F32), shape((B, B, NZ), F32), shape((4, 5, 1, CAP), F32)],
        8,
        10**7,
        scratch=[scratch, scratch, response, response, pltpu.VMEM((2, NH + 2, B, NZ), F32)],
    )(star, star_rest, first, source, y_even, y_odd, x_odd, x_even)
    return gas_next, pressure, kept, arrived


def solution(mesh):
    in_specs = (
        P(None, "gx", "gy", None),
        P("gx", "gy", None),
        P(None, "gx", "gy"),
        P("gx", "gy"),
        P("gx", "gy"),
        P("gx", "gy"),
        P("gx", "gy"),
        P("gx", "gy"),
        P("gx", "gy"),
    )
    out_specs = (
        P(None, "gx", "gy", None),
        P("gx", "gy", None),
        P(None, "gx", "gy"),
        P(None, None, "gx", "gy"),
    )
    return jax.shard_map(body, mesh=mesh, in_specs=in_specs, out_specs=out_specs, check_vma=False)
```

```python
import jax
import jax.numpy as jnp
from jax import lax
from jax.experimental import pallas as pl
from jax.experimental.pallas import tpu as pltpu
from jax.sharding import PartitionSpec as P

B = 8
NZ = 256
PD = 4096
CAP = 512
CHUNK = 512
F32 = jnp.float32
BF16 = jnp.bfloat16
VMEM = pl.BlockSpec(memory_space=pltpu.VMEM)
SMEM = pl.BlockSpec(memory_space=pltpu.SMEM)

Y_LAYERS = [(1, 0), (1, 1), (1, 2), (0, 0), (0, 1), (2, 0), (2, 1), (3, 0), (3, 1), (4, 0), (4, 1), (5, 0)]
X_LAYERS = [(0, 0), (0, 1), (0, 2), (1, 0), (1, 1), (2, 0), (2, 1), (3, 0), (3, 1), (4, 0), (4, 1), (5, 0)]
NL = 12


def params(limit=16):
    return pltpu.CompilerParams(vmem_limit_bytes=limit * 1024 * 1024)


def tiles(n):
    return jax.ShapeDtypeStruct((n, B, NZ), F32)


def call(kernel, outs, n_in, cost, scratch=(), smem=(), limit=16):
    return pl.pallas_call(
        kernel,
        out_shape=outs,
        in_specs=[SMEM if i in smem else VMEM for i in range(n_in)],
        out_specs=[VMEM] * len(outs),
        scratch_shapes=list(scratch),
        compiler_params=params(limit),
        cost_estimate=pl.CostEstimate(flops=cost, bytes_accessed=cost // 8, transcendentals=0),
    )


def by_parity(axis, act, even, odd):
    first = lax.rem(lax.axis_index(axis), 2) == 0

    @pl.when(first)
    def _():
        act(odd, even)

    @pl.when(jnp.logical_not(first))
    def _():
        act(even, odd)


def swap(shard, axis, start):
    peers = lax.axis_size(axis)
    pairs = [(i + a, i + 1 - a) for i in range(start, peers - 1, 2) for a in range(2)]
    return lax.ppermute(shard, axis, pairs)


def first_kernel(out):
    out[...] = jnp.zeros_like(out)


def pack_y_kernel(_, gas, guess, even, odd):
    def act(low, high):
        for r, (field, depth) in enumerate(Y_LAYERS):
            for side, y in ((low, depth), (high, B - 1 - depth)):
                side[r] = guess[:, y, :] if field == 5 else gas[field, :, y, :]

    by_parity("gy", act, even, odd)


def split(value):
    high = value.astype(BF16).astype(F32)
    return high, value - high


def renew_kernel(gas, motion, size, cell, target, kept, rows):
    table = jnp.concatenate([gas[f].reshape(B * B, NZ) for f in range(4)], axis=0)
    high, low = split(table)
    table = jnp.concatenate([high.astype(BF16), low.astype(BF16)], axis=1)
    at_z = lax.broadcasted_iota(jnp.int32, (NZ, CHUNK), 0)
    at_xy = lax.broadcasted_iota(jnp.int32, (B * B, CHUNK), 0)
    heading = lax.broadcasted_iota(jnp.int32, (B, CHUNK), 0)
    a = lax.broadcasted_iota(jnp.int32, (CHUNK, CHUNK), 0)
    b = lax.broadcasted_iota(jnp.int32, (CHUNK, CHUNK), 1)
    upper = jnp.where(a <= b, 1.0, 0.0).astype(BF16)
    before = jnp.zeros((B, 1), F32)
    for n in range(PD // CHUNK):
        part = slice(n * CHUNK, (n + 1) * CHUNK)
        cells = cell[:, part]
        goal = target[:, part]
        in_z = jnp.where(at_z == (cells & (NZ - 1)), 1.0, 0.0).astype(BF16)
        in_xy = at_xy == (cells >> 8)
        found = jnp.dot(table, jnp.concatenate([in_z, in_z], axis=0), preferred_element_type=F32)
        local = [
            jnp.sum(jnp.where(in_xy, found[f * B * B : (f + 1) * B * B], 0.0), axis=0, keepdims=True)
            for f in range(4)
        ]
        u, v, w, temperature = (motion[f, :, part] for f in range(4))
        diameter = size[:, part]
        excess = local[3] - temperature
        vapour = 0.5 * diameter * jax.nn.sigmoid(excess)
        renewed = [
            u + 0.4 * (local[0] - u),
            v + 0.4 * (local[1] - v),
            w + 0.2 * ((local[2] - w) * 2.0 - 1.0),
            temperature + 0.2 * excess,
            diameter - 0.2 * vapour,
        ]
        drag = 0.5 * diameter * diameter * (w - local[2])
        alive = goal >= 0
        for f in range(5):
            kept[f, :, part] = jnp.where(goal == 4, renewed[f], 0.0)
            rows[f : f + 1, part] = renewed[f]
        rows[5:6, part] = jnp.where(alive, drag, 0.0)
        rows[6:7, part] = jnp.where(alive, vapour, 0.0)
        chosen = heading == goal
        rank = jnp.dot(jnp.where(chosen, 1.0, 0.0).astype(BF16), upper, preferred_element_type=F32) + before
        before = rank[:, CHUNK - 1 :]
        leaves = chosen & (heading < 4)
        place = jnp.where(leaves, rank + heading.astype(F32) * float(CAP), 0.0)
        rows[7:8, part] = jnp.sum(place, axis=0, keepdims=True) - 1.0


def spread_kernel(rows, cell, on, when, head, _, sources, parcels):
    at_z = lax.broadcasted_iota(jnp.int32, (NZ, CHUNK), 0)
    at_xy = lax.broadcasted_iota(jnp.int32, (B * B, CHUNK), 0)
    at_high = lax.broadcasted_iota(jnp.int32, (B, CHUNK), 0)
    total = jnp.zeros((4 * B * B, NZ), F32)
    moved = jnp.zeros((10 * B, NZ), F32)
    across = (((1,), (1,)), ((), ()))
    for n in range(PD // CHUNK):
        part = slice(n * CHUNK, (n + 1) * CHUNK)
        cells = cell[:, part]
        in_z = jnp.where(at_z == (cells & (NZ - 1)), 1.0, 0.0).astype(BF16)
        in_xy = at_xy == (cells >> 8)
        pieces = [*split(rows[5:6, part]), *split(rows[6:7, part])]
        given = jnp.concatenate([jnp.where(in_xy, piece, 0.0).astype(BF16) for piece in pieces], axis=0)
        total = total + lax.dot_general(given, in_z, across, preferred_element_type=F32)
        place = rows[7:8, part].astype(jnp.int32)
        in_low = jnp.where(at_z == (place & (NZ - 1)), 1.0, 0.0).astype(BF16)
        in_high = at_high == (place >> 8)
        split_up = [split(rows[f : f + 1, part]) for f in range(5)]
        leaving = [jnp.where(in_high, split_up[f][piece], 0.0) for piece in range(2) for f in range(5)]
        moved = moved + lax.dot_general(
            jnp.concatenate(leaving, axis=0).astype(BF16), in_low, across, preferred_element_type=F32
        )
    q = B * B
    steam = total[2 * q : 3 * q] + total[3 * q :]
    sources[0] = total[:q] + total[q : 2 * q]
    sources[1] = -2.0 * steam
    sources[2] = steam
    lanes = lax.broadcasted_iota(jnp.int32, (1, NZ), 1)
    for s in range(B):
        ramp = jnp.clip((100.0 - when[0, s].astype(F32)) / 50.0, 0.0, 1.0)
        strength = 3.0 * ramp * on[0, s].astype(F32)
        where = head[0, s]
        row = pl.ds(where >> 8, 1)
        taken = jnp.where(lanes == (where & (NZ - 1)), strength, 0.0)
        for f in range(2):
            sources[f, row, :] = sources[f, row, :] - taken
    moved = moved[: 5 * B] + moved[5 * B :]
    for d in range(4):
        for f in range(5):
            for half in range(2):
                at = f * B + 2 * d + half
                r = 2 * f + half
                parcels[d, r // B, r % B : r % B + 1, :] = moved[at : at + 1]
        parcels[d, 1, 2:, :] = jnp.zeros((B - 2, NZ), F32)


def pack_x_kernel(gas, guess, y_odd, y_even, _, even, odd):
    def planes(low, high):
        for side, near, step in ((low, 0, 1), (high, B - 1, -1)):
            for r, (field, depth) in enumerate(X_LAYERS):
                x = near + step * depth
                side[r] = guess[x] if field == 5 else gas[field, x]

            def corners(below, above, side=side, near=near, step=step):
                for h, halo in enumerate((below, above)):
                    for r, (layer, x) in enumerate(((3, near), (4, near), (0, near), (0, near + step))):
                        side[NL, 4 * h + r : 4 * h + r + 1, :] = halo[layer, x : x + 1, :]

            by_parity("gy", corners, y_even, y_odd)

    by_parity("gx", planes, even, odd)


def beside(value, by):
    lane = lax.broadcasted_iota(jnp.int32, value.shape, 1)
    turned = pltpu.roll(value, (-by) % NZ, axis=1)
    return jnp.where((lane < NZ - by) if by > 0 else (lane >= -by), turned, 0.0)


def advance(e, f, x, rows, first):
    def at(field, dx, dy):
        return e[field, x + dx, first + dy : first + dy + rows, :]

    centre = at(f, 0, 0)
    xs = {s: at(f, s, 0) for s in (-2, -1, 1, 2)}
    ys = {s: at(f, 0, s) for s in (-2, -1, 1, 2)}
    zs = {s: beside(centre, s) for s in (-2, -1, 1, 2)}
    laplace = xs[1] + xs[-1] + ys[1] + ys[-1] + zs[1] + zs[-1] - 6.0 * centre
    transport = 0.0
    for axis, shifted in enumerate((xs, ys, zs)):
        slope = 8.0 * (shifted[1] - shifted[-1]) - (shifted[2] - shifted[-2])
        transport = transport + at(axis, 0, 0) * slope
    return centre + (0.02 * laplace - (0.2 / 12.0) * transport)


def fill_own(gas, e, fields):
    for k, f in enumerate(fields):
        e[k, 3 : 3 + B, B : 2 * B, :] = gas[f]


def predict_kernel(gas, guess, y_odd, y_even, x_odd, x_even, sources, parcels, star, even, odd, e, wide, tall, q):
    gx = lax.axis_index("gx")
    gy = lax.axis_index("gy")
    has_left, has_right = gx > 0, gx < lax.axis_size("gx") - 1
    has_below, has_above = gy > 0, gy < lax.axis_size("gy") - 1
    fill_own(gas, e, range(3))
    q[1 : 1 + B, B : 2 * B, :] = guess[...]

    def fill_y(below, above):
        for r, (field, depth) in enumerate(Y_LAYERS):
            for halo, y in ((below, B - 1 - depth), (above, 2 * B + depth)):
                if field == 5:
                    q[1 : 1 + B, y, :] = halo[r]
                elif field < 3:
                    e[field, 3 : 3 + B, y, :] = halo[r]

    def fill_x(left, right):
        for r, (field, depth) in enumerate(X_LAYERS):
            for halo, x in ((left, -1 - depth), (right, B + depth)):
                if field == 5:
                    q[x + 1, B : 2 * B, :] = halo[r]
                elif field < 3:
                    e[field, x + 3, B : 2 * B, :] = halo[r]
        for halo, near, step in ((left, 2, -1), (right, 3 + B, 1)):
            for h, (y, onward) in enumerate(((B - 1, -1), (2 * B, 1))):
                spots = ((0, near, y), (0, near, y + onward), (1, near, y), (1, near + step, y))
                for r, (field, x, row) in enumerate(spots):
                    e[field, x, row : row + 1, :] = halo[NL, 4 * h + r : 4 * h + r + 1, :]

    by_parity("gy", fill_y, y_even, y_odd)
    by_parity("gx", fill_x, x_even, x_odd)
    for x in range(-1, B + 1):
        value = advance(e, 0, x + 3, B, B)
        if x < 0:
            value = jnp.where(has_left, value, 0.0)
        if x == B:
            value = jnp.where(has_right, value, 0.0)
        wide[x + 1] = value
        if 0 <= x < B:
            star[0, x] = value
    for x in range(B):
        value = advance(e, 1, x + 3, B + 2, B - 1)
        row = lax.broadcasted_iota(jnp.int32, value.shape, 0)
        inside = ((row > 0) | has_below) & ((row < B + 1) | has_above)
        value = jnp.where(inside, value, 0.0)
        tall[x, : B + 2, :] = value
        star[1, x] = value[1 : 1 + B]
    for x in range(B):
        w = advance(e, 2, x + 3, B, B) + 0.2 * sources[0, x]
        star[2, x] = w
        spread = wide[x + 2] - wide[x] + (tall[x, 2 : 2 + B, :] - tall[x, :B, :])
        source = 2.5 * (spread + (beside(w, 1) - beside(w, -1)))
        centre = q[x + 1, B : 2 * B, :]
        around = q[x + 2, B : 2 * B, :] + q[x, B : 2 * B, :]
        around = around + q[x + 1, B + 1 : 2 * B + 1, :] + q[x + 1, B - 1 : 2 * B - 1, :]
        field = (around + beside(centre, 1) + beside(centre, -1) - source) * (1.0 / 6.0)
        for side in (even, odd):
            side[x] = field
            side[B + x] = source

    def attach(low, high):
        for side, heading in ((high, 2), (low, 3)):
            side[2 * B] = parcels[heading, 0]
            side[2 * B + 1] = parcels[heading, 1]

    by_parity("gy", attach, even, odd)


def scalars_kernel(gas, y_odd, y_even, x_odd, x_even, sources, _, star, e):
    fill_own(gas, e, range(5))

    def fill_y(below, above):
        for r, (field, depth) in enumerate(Y_LAYERS):
            if field in (3, 4):
                e[field, 3 : 3 + B, B - 1 - depth, :] = below[r]
                e[field, 3 : 3 + B, 2 * B + depth, :] = above[r]

    def fill_x(left, right):
        for r, (field, depth) in enumerate(X_LAYERS):
            if field in (3, 4):
                e[field, 2 - depth, B : 2 * B, :] = left[r]
                e[field, B + 3 + depth, B : 2 * B, :] = right[r]

    by_parity("gy", fill_y, y_even, y_odd)
    by_parity("gx", fill_x, x_even, x_odd)
    for f in (3, 4):
        for x in range(B):
            star[f - 3, x] = advance(e, f, x + 3, B, B) + 0.2 * sources[f - 2, x]


NH = 15
HALF = NZ // 2


def load(ref, *lead):
    return [[ref[(*lead, slice(B * t, B * t + B), slice(HALF * h, HALF * h + HALF))] for h in range(2)] for t in range(3)]


def store(ref, plane, *lead):
    for t in range(3):
        for h in range(2):
            ref[(*lead, slice(B * t, B * t + B), slice(HALF * h, HALF * h + HALF))] = plane[t][h]


def add(*planes):
    planes = [p for p in planes if p is not None]
    return [[sum((p[t][h] for p in planes[1:]), planes[0][t][h]) for h in range(2)] for t in range(3)]


def beside_plane(c):
    row = lax.broadcasted_iota(jnp.int32, (B, HALF), 0)
    lane = lax.broadcasted_iota(jnp.int32, (B, HALF), 1)
    top, bottom, start, end = row == 0, row == B - 1, lane == 0, lane == HALF - 1
    out = []
    for t in range(3):
        after = [pltpu.roll(c[t][h], 1, axis=1) for h in range(2)]
        ahead = [pltpu.roll(c[t][h], HALF - 1, axis=1) for h in range(2)]
        along_z = [
            jnp.where(start, 0.0, after[0]) + jnp.where(end, ahead[1], ahead[0]),
            jnp.where(start, after[0], after[1]) + jnp.where(end, 0.0, ahead[1]),
        ]
        tile = []
        for h in range(2):
            down = pltpu.roll(c[t][h], 1, axis=0)
            if t > 0:
                down = jnp.where(top, pltpu.roll(c[t - 1][h], 1, axis=0), down)
            up = pltpu.roll(c[t][h], B - 1, axis=0)
            if t < 2:
                up = jnp.where(bottom, pltpu.roll(c[t + 1][h], B - 1, axis=0), up)
            tile.append(along_z[h] + (down + up))
        out.append(tile)
    return out


def relax(centre, others, source, scale):
    total = add(*others, None if centre is None else beside_plane(centre))
    if source is not None:
        total = [[total[t][h] - source[t][h] for h in range(2)] for t in range(3)]
    return [[total[t][h] * scale[t] for h in range(2)] for t in range(3)]


def weights(flags_x, flags_y):
    out = []
    for flag_y in flags_y:
        value = jnp.full((B, HALF), 1.0 / 6.0, F32)
        for flag in (*flags_x, flag_y):
            if flag is not None:
                value = jnp.where(flag, value, 0.0)
        out.append(value)
    return out


def slab_kernel(own, y_odd, y_even, parcels, even, odd, first, source, f0, f1, low, high):
    gy = lax.axis_index("gy")
    scale = weights((), (gy > 0, None, gy < lax.axis_size("gy") - 1))
    row = lax.broadcasted_iota(jnp.int32, (B, HALF), 0)
    for x in range(B):
        first[x, B : 2 * B, :] = own[x]
        source[x, B : 2 * B, :] = own[B + x]

    def fill(below, above):
        for x in range(B):
            for k, halo in ((0, below), (2, above)):
                first[x, k * B : (k + 1) * B, :] = halo[x]
                source[x, k * B : (k + 1) * B, :] = halo[B + x]

    by_parity("gy", fill, y_even, y_odd)

    def keep(side, k, plane):
        for h in range(2):
            part = slice(HALF * h, HALF * h + HALF)
            side[k - 1, :, part] = plane[1][h]
            if k < B:
                side[B - 1 + k, k:, part] = plane[0][h][k:]
                side[2 * B - 1 - k, : B - k, part] = plane[2][h][: B - k]

    for side, x in ((low, 0), (high, B - 1)):
        keep(side, 1, load(first, x))
    now, later = first, f0
    for k in range(2, 9):
        depth = 9 - k
        for x in range(B):
            if depth <= x < B - depth:
                continue
            others = [load(now, y) for y in (x - 1, x + 1) if 0 <= y < B]
            plane = relax(load(now, x), others, load(source, x), scale)
            if k < 8:
                store(later, plane, x)
            for side, face in ((low, 0), (high, B - 1)):
                if x == face:
                    keep(side, k, plane)
        now, later = (f0, f1) if k == 2 else (later, now)
    for side, heading in ((low, 1), (high, 0)):
        side[NH] = parcels[heading, 0]
        side[NH + 1] = parcels[heading, 1]

    def send(low_out, high_out):
        low_out[...] = low[...]
        high_out[...] = high[...]

    by_parity("gx", send, even, odd)


def finish_kernel(star, star_rest, first, source, y_even, y_odd, x_odd, x_even, gas_next, pressure, arrived, o0, o1, r0, r1, hist):
    gx = lax.axis_index("gx")
    gy = lax.axis_index("gy")
    flags_y = (gy > 0, None, gy < lax.axis_size("gy") - 1)
    inner = weights((), flags_y)
    outer = [weights((gx > 0,), flags_y), weights((gx < lax.axis_size("gx") - 1,), flags_y)]

    def arrive(d, halo, at):
        for f in range(5):
            for half in range(2):
                r = 2 * f + half
                arrived[d, f, :, half * NZ : (half + 1) * NZ] = halo[at + r // B, r % B : r % B + 1, :]

    def take_y(below, above):
        arrive(2, below, 2 * B)
        arrive(3, above, 2 * B)

    def take_x(left, right):
        hist[0] = left[...]
        hist[1] = right[...]

    by_parity("gy", take_y, y_even, y_odd)
    by_parity("gx", take_x, x_even, x_odd)
    arrive(0, hist.at[0], NH)
    arrive(1, hist.at[1], NH)

    def history(side, k):
        at = (B - 1 + k, k - 1, 2 * B - 1 - k)
        return [[hist[side, at[t], :, slice(HALF * h, HALF * h + HALF)] for h in range(2)] for t in range(3)]

    owns = {1: first, **{k: (o0, o1)[k % 2] for k in range(2, 9)}}
    responses = {k: (r0, r1)[k % 2] for k in range(2, 9)}

    def at(k, x):
        if 0 <= x < B:
            return load(owns[k], x)
        side, depth = (0, -x) if x < 0 else (1, x - B + 1)
        return load(responses[k], side, depth - 1) if depth < k else None

    for k in range(2, 9):
        depth = min(k - 1, 9 - k)
        for x in range(-depth, B + depth):
            others = [at(k - 1, x - 1), at(k - 1, x + 1)]
            if 0 <= x < B:
                if x == 0:
                    others.append(history(0, k - 1))
                if x == B - 1:
                    others.append(history(1, k - 1))
                store(owns[k], relax(at(k - 1, x), others, load(source, x), inner), x)
            else:
                side, far = (0, -x) if x < 0 else (1, x - B + 1)
                store(responses[k], relax(at(k - 1, x), others, None, outer[side]), side, far - 1)
    last, edge = owns[8], responses[8]

    def level(x):
        if x < 0:
            return edge[0, 0, B : 2 * B, :] + hist[0, B - 1]
        if x >= B:
            return edge[1, 0, B : 2 * B, :] + hist[1, B - 1]
        return last[x, B : 2 * B, :]

    for x in range(B):
        centre = level(x)
        pressure[x] = centre
        gas_next[0, x] = star[0, x] - 0.1 * (level(x + 1) - level(x - 1))
        gas_next[1, x] = star[1, x] - 0.1 * (last[x, B + 1 : 2 * B + 1, :] - last[x, B - 1 : 2 * B - 1, :])
        gas_next[2, x] = star[2, x] - 0.1 * (beside(centre, 1) - beside(centre, -1))
        gas_next[3, x] = star_rest[0, x]
        gas_next[4, x] = star_rest[1, x]


def body(gas, guess, motion, size, cell, target, on, when, head):
    shape = jax.ShapeDtypeStruct
    [first] = call(first_kernel, [shape((B, 128), F32)], 0, 10**10)()
    y_even, y_odd = call(pack_y_kernel, [tiles(NL)] * 2, 3, 10**6)(first, gas, guess)
    y_odd = swap(y_odd, "gy", 1)
    y_even = swap(y_even, "gy", 0)
    kept, rows = call(renew_kernel, [shape((5, 1, PD), F32), shape((8, PD), F32)], 5, 10**9)(
        gas, motion, size, cell, target
    )
    x_even, x_odd = call(pack_x_kernel, [tiles(NL + 1)] * 2, 5, 10**6)(gas, guess, y_odd, y_even, rows)
    sources, parcels = call(
        spread_kernel,
        [shape((3, B * B, NZ), F32), shape((4, 2, B, NZ), F32)],
        6,
        10**9,
        smem=(2, 3, 4),
    )(rows, cell, on, when, head, x_even)
    sources = sources.reshape(3, B, B, NZ)
    x_odd = swap(x_odd, "gx", 1)
    x_even = swap(x_even, "gx", 0)
    wide = pltpu.VMEM((5, B + 6, 3 * B, NZ), F32)
    star, ps_even, ps_odd = call(
        predict_kernel,
        [shape((3, B, B, NZ), F32), tiles(2 * B + 2), tiles(2 * B + 2)],
        8,
        10**7,
        scratch=[
            wide,
            pltpu.VMEM((B + 2, B, NZ), F32),
            pltpu.VMEM((B, 2 * B, NZ), F32),
            pltpu.VMEM((B + 2, 3 * B, NZ), F32),
        ],
    )(gas, guess, y_odd, y_even, x_odd, x_even, sources, parcels)
    [star_rest] = call(scalars_kernel, [shape((2, B, B, NZ), F32)], 7, 10**8, scratch=[wide])(
        gas, y_odd, y_even, x_odd, x_even, sources, ps_odd
    )
    y_odd = swap(ps_odd, "gy", 1)
    y_even = swap(ps_even, "gy", 0)
    slab = shape((B, 3 * B, NZ), F32)
    scratch = pltpu.VMEM((B, 3 * B, NZ), F32)
    x_even, x_odd, first, source = call(
        slab_kernel,
        [tiles(NH + 2), tiles(NH + 2), slab, slab],
        4,
        10**7,
        scratch=[scratch, scratch, pltpu.VMEM((NH + 2, B, NZ), F32), pltpu.VMEM((NH + 2, B, NZ), F32)],
    )(ps_even, y_odd, y_even, parcels)
    x_odd = swap(x_odd, "gx", 1)
    x_even = swap(x_even, "gx", 0)
    response = pltpu.VMEM((2, 4, 3 * B, NZ), F32)
    gas_next, pressure, arrived = call(
        finish_kernel,
        [shape((5, B, B, NZ), F32), shape((B, B, NZ), F32), shape((4, 5, 1, CAP), F32)],
        8,
        10**7,
        scratch=[scratch, scratch, response, response, pltpu.VMEM((2, NH + 2, B, NZ), F32)],
    )(star, star_rest, first, source, y_even, y_odd, x_odd, x_even)
    return gas_next, pressure, kept, arrived


def solution(mesh):
    in_specs = (
        P(None, "gx", "gy", None),
        P("gx", "gy", None),
        P(None, "gx", "gy"),
        P("gx", "gy"),
        P("gx", "gy"),
        P("gx", "gy"),
        P("gx", "gy"),
        P("gx", "gy"),
        P("gx", "gy"),
    )
    out_specs = (
        P(None, "gx", "gy", None),
        P("gx", "gy", None),
        P(None, "gx", "gy"),
        P(None, None, "gx", "gy"),
    )
    return jax.shard_map(body, mesh=mesh, in_specs=in_specs, out_specs=out_specs, check_vma=False)
```

```python
import jax
import jax.numpy as jnp
from jax import lax
from jax.experimental import pallas as pl
from jax.experimental.pallas import tpu as pltpu
from jax.sharding import PartitionSpec as P

B = 8
NZ = 256
PD = 4096
CAP = 512
CHUNK = 512
F32 = jnp.float32
BF16 = jnp.bfloat16
VMEM = pl.BlockSpec(memory_space=pltpu.VMEM)
SMEM = pl.BlockSpec(memory_space=pltpu.SMEM)

Y_LAYERS = [(1, 0), (1, 1), (1, 2), (0, 0), (0, 1), (2, 0), (2, 1), (3, 0), (3, 1), (4, 0), (4, 1), (5, 0)]
X_LAYERS = [(0, 0), (0, 1), (0, 2), (1, 0), (1, 1), (2, 0), (2, 1), (3, 0), (3, 1), (4, 0), (4, 1), (5, 0)]
NL = 12


def params(limit=16):
    return pltpu.CompilerParams(vmem_limit_bytes=limit * 1024 * 1024)


def tiles(n):
    return jax.ShapeDtypeStruct((n, B, NZ), F32)


def call(kernel, outs, n_in, cost, scratch=(), smem=(), limit=16):
    return pl.pallas_call(
        kernel,
        out_shape=outs,
        in_specs=[SMEM if i in smem else VMEM for i in range(n_in)],
        out_specs=[VMEM] * len(outs),
        scratch_shapes=list(scratch),
        compiler_params=params(limit),
        cost_estimate=pl.CostEstimate(flops=cost, bytes_accessed=cost // 8, transcendentals=0),
    )


def by_parity(axis, act, even, odd):
    first = lax.rem(lax.axis_index(axis), 2) == 0

    @pl.when(first)
    def _():
        act(odd, even)

    @pl.when(jnp.logical_not(first))
    def _():
        act(even, odd)


def swap(shard, axis, start):
    peers = lax.axis_size(axis)
    pairs = [(i + a, i + 1 - a) for i in range(start, peers - 1, 2) for a in range(2)]
    return lax.ppermute(shard, axis, pairs)


def first_kernel(out):
    out[...] = jnp.zeros_like(out)


def pack_y_kernel(_, gas, guess, even, odd):
    def act(low, high):
        for r, (field, depth) in enumerate(Y_LAYERS):
            for side, y in ((low, depth), (high, B - 1 - depth)):
                side[r] = guess[:, y, :] if field == 5 else gas[field, :, y, :]

    by_parity("gy", act, even, odd)


def split(value):
    high = value.astype(BF16).astype(F32)
    return high, value - high


def counting(rows):
    return lax.broadcasted_iota(jnp.int32, (rows, CHUNK), 0).astype(F32).astype(BF16)


def exact(numbers):
    return numbers.astype(F32).astype(BF16)


def one_hot(counted, numbers):
    return jnp.where(counted == exact(numbers), jnp.ones((), BF16), jnp.zeros((), BF16))


def renew_kernel(gas, motion, size, cell, target, kept, rows, parcels, places):
    table = jnp.concatenate([gas[f].reshape(B * B, NZ) for f in range(4)], axis=0)
    high, low = split(table)
    table = jnp.concatenate([high.astype(BF16), low.astype(BF16)], axis=1)
    at_z = counting(NZ)
    at_xy = lax.broadcasted_iota(jnp.int32, (B * B, CHUNK), 0)
    heading = lax.broadcasted_iota(jnp.int32, (B, NZ), 0)
    blocks = [heading == target[:, n * NZ : (n + 1) * NZ] for n in range(PD // NZ)]
    a = lax.broadcasted_iota(jnp.int32, (NZ, NZ), 0)
    b = lax.broadcasted_iota(jnp.int32, (NZ, NZ), 1)
    upper = jnp.where(a <= b, 1.0, 0.0).astype(BF16)
    marks = jnp.concatenate([jnp.where(chosen, 1.0, 0.0) for chosen in blocks], axis=0).astype(BF16)
    ranks = jnp.dot(marks, upper, preferred_element_type=F32)
    before = jnp.zeros((B, 1), F32)
    for n, chosen in enumerate(blocks):
        rank = ranks[B * n : B * n + B] + before
        before = rank[:, NZ - 1 :]
        place = jnp.where(chosen & (heading < 4), rank + heading.astype(F32) * float(CAP), 0.0)
        places[:, n * NZ : (n + 1) * NZ] = jnp.sum(place, axis=0, keepdims=True).astype(jnp.int32) - 1
    moved = jnp.zeros((10 * B, NZ), F32)
    at_high = lax.broadcasted_iota(jnp.int32, (B, CHUNK), 0)
    across = (((1,), (1,)), ((), ()))
    for n in range(PD // CHUNK):
        part = slice(n * CHUNK, (n + 1) * CHUNK)
        cells = cell[:, part]
        goal = target[:, part]
        in_z = one_hot(at_z, cells & (NZ - 1))
        in_xy = at_xy == (cells >> 8)
        found = jnp.dot(table, jnp.concatenate([in_z, in_z], axis=0), preferred_element_type=F32)
        local = [
            jnp.sum(jnp.where(in_xy, found[f * B * B : (f + 1) * B * B], 0.0), axis=0, keepdims=True)
            for f in range(4)
        ]
        u, v, w, temperature = (motion[f, :, part] for f in range(4))
        diameter = size[:, part]
        excess = local[3] - temperature
        vapour = 0.5 * diameter * jax.nn.sigmoid(excess)
        renewed = [
            u + 0.4 * (local[0] - u),
            v + 0.4 * (local[1] - v),
            w + 0.2 * ((local[2] - w) * 2.0 - 1.0),
            temperature + 0.2 * excess,
            diameter - 0.2 * vapour,
        ]
        drag = 0.5 * diameter * diameter * (w - local[2])
        alive = goal >= 0
        for f in range(5):
            kept[f, :, part] = jnp.where(goal == 4, renewed[f], 0.0)
        rows[0:1, part] = jnp.where(alive, drag, 0.0)
        rows[1:2, part] = jnp.where(alive, vapour, 0.0)
        place = places[:, part]
        in_low = one_hot(at_z, place & (NZ - 1))
        in_high = at_high == (place >> 8)
        split_up = [split(value) for value in renewed]
        leaving = [jnp.where(in_high, split_up[f][piece], 0.0) for piece in range(2) for f in range(5)]
        moved = moved + lax.dot_general(
            jnp.concatenate(leaving, axis=0).astype(BF16), in_low, across, preferred_element_type=F32
        )
    moved = moved[: 5 * B] + moved[5 * B :]
    for d in range(4):
        for f in range(5):
            for half in range(2):
                at = f * B + 2 * d + half
                r = 2 * f + half
                parcels[d, r // B, r % B : r % B + 1, :] = moved[at : at + 1]
        parcels[d, 1, 2:, :] = jnp.zeros((B - 2, NZ), F32)


def spread_kernel(rows, cell, on, when, head, _, sources):
    at_z = counting(NZ)
    at_xy = counting(B * B)
    total = jnp.zeros((4 * B * B, NZ), F32)
    across = (((1,), (1,)), ((), ()))
    for n in range(PD // CHUNK):
        part = slice(n * CHUNK, (n + 1) * CHUNK)
        cells = cell[:, part]
        in_z = one_hot(at_z, cells & (NZ - 1))
        in_xy = at_xy == exact(cells >> 8)
        pieces = [*split(rows[0:1, part]), *split(rows[1:2, part])]
        given = jnp.concatenate([jnp.where(in_xy, piece.astype(BF16), jnp.zeros((), BF16)) for piece in pieces], axis=0)
        total = total + lax.dot_general(given, in_z, across, preferred_element_type=F32)
    q = B * B
    steam = total[2 * q : 3 * q] + total[3 * q :]
    sources[0] = total[:q] + total[q : 2 * q]
    sources[1] = -2.0 * steam
    sources[2] = steam
    lanes = lax.broadcasted_iota(jnp.int32, (1, NZ), 1)
    for s in range(B):
        ramp = jnp.clip((100.0 - when[0, s].astype(F32)) / 50.0, 0.0, 1.0)
        strength = 3.0 * ramp * on[0, s].astype(F32)
        where = head[0, s]
        row = pl.ds(where >> 8, 1)
        taken = jnp.where(lanes == (where & (NZ - 1)), strength, 0.0)
        for f in range(2):
            sources[f, row, :] = sources[f, row, :] - taken


def pack_x_kernel(gas, guess, y_odd, y_even, _, even, odd):
    def planes(low, high):
        for side, near, step in ((low, 0, 1), (high, B - 1, -1)):
            for r, (field, depth) in enumerate(X_LAYERS):
                x = near + step * depth
                side[r] = guess[x] if field == 5 else gas[field, x]

            def corners(below, above, side=side, near=near, step=step):
                for h, halo in enumerate((below, above)):
                    for r, (layer, x) in enumerate(((3, near), (4, near), (0, near), (0, near + step))):
                        side[NL, 4 * h + r : 4 * h + r + 1, :] = halo[layer, x : x + 1, :]

            by_parity("gy", corners, y_even, y_odd)

    by_parity("gx", planes, even, odd)


def beside(value, by):
    lane = lax.broadcasted_iota(jnp.int32, value.shape, 1)
    turned = pltpu.roll(value, (-by) % NZ, axis=1)
    return jnp.where((lane < NZ - by) if by > 0 else (lane >= -by), turned, 0.0)


def advance(e, f, x, rows, first):
    def at(field, dx, dy):
        return e[field, x + dx, first + dy : first + dy + rows, :]

    centre = at(f, 0, 0)
    xs = {s: at(f, s, 0) for s in (-2, -1, 1, 2)}
    ys = {s: at(f, 0, s) for s in (-2, -1, 1, 2)}
    zs = {s: beside(centre, s) for s in (-2, -1, 1, 2)}
    laplace = xs[1] + xs[-1] + ys[1] + ys[-1] + zs[1] + zs[-1] - 6.0 * centre
    transport = 0.0
    for axis, shifted in enumerate((xs, ys, zs)):
        slope = 8.0 * (shifted[1] - shifted[-1]) - (shifted[2] - shifted[-2])
        transport = transport + at(axis, 0, 0) * slope
    return centre + (0.02 * laplace - (0.2 / 12.0) * transport)


def fill_own(gas, e, fields):
    for k, f in enumerate(fields):
        e[k, 3 : 3 + B, B : 2 * B, :] = gas[f]


def predict_kernel(gas, guess, y_odd, y_even, x_odd, x_even, sources, parcels, star, even, odd, e, wide, tall, q):
    gx = lax.axis_index("gx")
    gy = lax.axis_index("gy")
    has_left, has_right = gx > 0, gx < lax.axis_size("gx") - 1
    has_below, has_above = gy > 0, gy < lax.axis_size("gy") - 1
    fill_own(gas, e, range(3))
    q[1 : 1 + B, B : 2 * B, :] = guess[...]

    def fill_y(below, above):
        for r, (field, depth) in enumerate(Y_LAYERS):
            for halo, y in ((below, B - 1 - depth), (above, 2 * B + depth)):
                if field == 5:
                    q[1 : 1 + B, y, :] = halo[r]
                elif field < 3:
                    e[field, 3 : 3 + B, y, :] = halo[r]

    def fill_x(left, right):
        for r, (field, depth) in enumerate(X_LAYERS):
            for halo, x in ((left, -1 - depth), (right, B + depth)):
                if field == 5:
                    q[x + 1, B : 2 * B, :] = halo[r]
                elif field < 3:
                    e[field, x + 3, B : 2 * B, :] = halo[r]
        for halo, near, step in ((left, 2, -1), (right, 3 + B, 1)):
            for h, (y, onward) in enumerate(((B - 1, -1), (2 * B, 1))):
                spots = ((0, near, y), (0, near, y + onward), (1, near, y), (1, near + step, y))
                for r, (field, x, row) in enumerate(spots):
                    e[field, x, row : row + 1, :] = halo[NL, 4 * h + r : 4 * h + r + 1, :]

    by_parity("gy", fill_y, y_even, y_odd)
    by_parity("gx", fill_x, x_even, x_odd)
    for x in range(-1, B + 1):
        value = advance(e, 0, x + 3, B, B)
        if x < 0:
            value = jnp.where(has_left, value, 0.0)
        if x == B:
            value = jnp.where(has_right, value, 0.0)
        wide[x + 1] = value
        if 0 <= x < B:
            star[0, x] = value
    for x in range(B):
        value = advance(e, 1, x + 3, B + 2, B - 1)
        row = lax.broadcasted_iota(jnp.int32, value.shape, 0)
        inside = ((row > 0) | has_below) & ((row < B + 1) | has_above)
        value = jnp.where(inside, value, 0.0)
        tall[x, : B + 2, :] = value
        star[1, x] = value[1 : 1 + B]
    for x in range(B):
        w = advance(e, 2, x + 3, B, B) + 0.2 * sources[0, x]
        star[2, x] = w
        spread = wide[x + 2] - wide[x] + (tall[x, 2 : 2 + B, :] - tall[x, :B, :])
        source = 2.5 * (spread + (beside(w, 1) - beside(w, -1)))
        centre = q[x + 1, B : 2 * B, :]
        around = q[x + 2, B : 2 * B, :] + q[x, B : 2 * B, :]
        around = around + q[x + 1, B + 1 : 2 * B + 1, :] + q[x + 1, B - 1 : 2 * B - 1, :]
        field = (around + beside(centre, 1) + beside(centre, -1) - source) * (1.0 / 6.0)
        for side in (even, odd):
            side[x] = field
            side[B + x] = source

    def attach(low, high):
        for side, heading in ((high, 2), (low, 3)):
            side[2 * B] = parcels[heading, 0]
            side[2 * B + 1] = parcels[heading, 1]

    by_parity("gy", attach, even, odd)


def scalars_kernel(gas, y_odd, y_even, x_odd, x_even, sources, _, star, e):
    fill_own(gas, e, range(5))

    def fill_y(below, above):
        for r, (field, depth) in enumerate(Y_LAYERS):
            if field in (3, 4):
                e[field, 3 : 3 + B, B - 1 - depth, :] = below[r]
                e[field, 3 : 3 + B, 2 * B + depth, :] = above[r]

    def fill_x(left, right):
        for r, (field, depth) in enumerate(X_LAYERS):
            if field in (3, 4):
                e[field, 2 - depth, B : 2 * B, :] = left[r]
                e[field, B + 3 + depth, B : 2 * B, :] = right[r]

    by_parity("gy", fill_y, y_even, y_odd)
    by_parity("gx", fill_x, x_even, x_odd)
    for f in (3, 4):
        for x in range(B):
            star[f - 3, x] = advance(e, f, x + 3, B, B) + 0.2 * sources[f - 2, x]


NH = 15
HALF = NZ // 2


def load(ref, *lead):
    return [[ref[(*lead, slice(B * t, B * t + B), slice(HALF * h, HALF * h + HALF))] for h in range(2)] for t in range(3)]


def store(ref, plane, *lead):
    for t in range(3):
        for h in range(2):
            ref[(*lead, slice(B * t, B * t + B), slice(HALF * h, HALF * h + HALF))] = plane[t][h]


def add(*planes):
    planes = [p for p in planes if p is not None]
    return [[sum((p[t][h] for p in planes[1:]), planes[0][t][h]) for h in range(2)] for t in range(3)]


def beside_plane(c):
    row = lax.broadcasted_iota(jnp.int32, (B, HALF), 0)
    lane = lax.broadcasted_iota(jnp.int32, (B, HALF), 1)
    top, bottom, start, end = row == 0, row == B - 1, lane == 0, lane == HALF - 1
    out = []
    for t in range(3):
        after = [pltpu.roll(c[t][h], 1, axis=1) for h in range(2)]
        ahead = [pltpu.roll(c[t][h], HALF - 1, axis=1) for h in range(2)]
        along_z = [
            jnp.where(start, 0.0, after[0]) + jnp.where(end, ahead[1], ahead[0]),
            jnp.where(start, after[0], after[1]) + jnp.where(end, 0.0, ahead[1]),
        ]
        tile = []
        for h in range(2):
            down = pltpu.roll(c[t][h], 1, axis=0)
            if t > 0:
                down = jnp.where(top, pltpu.roll(c[t - 1][h], 1, axis=0), down)
            up = pltpu.roll(c[t][h], B - 1, axis=0)
            if t < 2:
                up = jnp.where(bottom, pltpu.roll(c[t + 1][h], B - 1, axis=0), up)
            tile.append(along_z[h] + (down + up))
        out.append(tile)
    return out


def relax(centre, others, source, scale):
    total = add(*others, None if centre is None else beside_plane(centre))
    if source is not None:
        total = [[total[t][h] - source[t][h] for h in range(2)] for t in range(3)]
    return [[total[t][h] * scale[t] for h in range(2)] for t in range(3)]


def weights(flags_x, flags_y):
    out = []
    for flag_y in flags_y:
        value = jnp.full((B, HALF), 1.0 / 6.0, F32)
        for flag in (*flags_x, flag_y):
            if flag is not None:
                value = jnp.where(flag, value, 0.0)
        out.append(value)
    return out


def slab_kernel(own, y_odd, y_even, parcels, even, odd, first, source, f0, f1, low, high):
    gy = lax.axis_index("gy")
    scale = weights((), (gy > 0, None, gy < lax.axis_size("gy") - 1))
    row = lax.broadcasted_iota(jnp.int32, (B, HALF), 0)
    for x in range(B):
        first[x, B : 2 * B, :] = own[x]
        source[x, B : 2 * B, :] = own[B + x]

    def fill(below, above):
        for x in range(B):
            for k, halo in ((0, below), (2, above)):
                first[x, k * B : (k + 1) * B, :] = halo[x]
                source[x, k * B : (k + 1) * B, :] = halo[B + x]

    by_parity("gy", fill, y_even, y_odd)

    def keep(side, k, plane):
        for h in range(2):
            part = slice(HALF * h, HALF * h + HALF)
            side[k - 1, :, part] = plane[1][h]
            if k < B:
                side[B - 1 + k, k:, part] = plane[0][h][k:]
                side[2 * B - 1 - k, : B - k, part] = plane[2][h][: B - k]

    for side, x in ((low, 0), (high, B - 1)):
        keep(side, 1, load(first, x))
    now, later = first, f0
    for k in range(2, 9):
        depth = 9 - k
        for x in range(B):
            if depth <= x < B - depth:
                continue
            others = [load(now, y) for y in (x - 1, x + 1) if 0 <= y < B]
            plane = relax(load(now, x), others, load(source, x), scale)
            if k < 8:
                store(later, plane, x)
            for side, face in ((low, 0), (high, B - 1)):
                if x == face:
                    keep(side, k, plane)
        now, later = (f0, f1) if k == 2 else (later, now)
    for side, heading in ((low, 1), (high, 0)):
        side[NH] = parcels[heading, 0]
        side[NH + 1] = parcels[heading, 1]

    def send(low_out, high_out):
        low_out[...] = low[...]
        high_out[...] = high[...]

    by_parity("gx", send, even, odd)


def finish_kernel(star, star_rest, first, source, y_even, y_odd, x_odd, x_even, gas_next, pressure, arrived, o0, o1, r0, r1, hist):
    gx = lax.axis_index("gx")
    gy = lax.axis_index("gy")
    flags_y = (gy > 0, None, gy < lax.axis_size("gy") - 1)
    inner = weights((), flags_y)
    outer = [weights((gx > 0,), flags_y), weights((gx < lax.axis_size("gx") - 1,), flags_y)]

    def arrive(d, halo, at):
        for f in range(5):
            for half in range(2):
                r = 2 * f + half
                arrived[d, f, :, half * NZ : (half + 1) * NZ] = halo[at + r // B, r % B : r % B + 1, :]

    def take_y(below, above):
        arrive(2, below, 2 * B)
        arrive(3, above, 2 * B)

    def take_x(left, right):
        hist[0] = left[...]
        hist[1] = right[...]

    by_parity("gy", take_y, y_even, y_odd)
    by_parity("gx", take_x, x_even, x_odd)
    arrive(0, hist.at[0], NH)
    arrive(1, hist.at[1], NH)

    def history(side, k):
        at = (B - 1 + k, k - 1, 2 * B - 1 - k)
        return [[hist[side, at[t], :, slice(HALF * h, HALF * h + HALF)] for h in range(2)] for t in range(3)]

    owns = {1: first, **{k: (o0, o1)[k % 2] for k in range(2, 9)}}
    responses = {k: (r0, r1)[k % 2] for k in range(2, 9)}

    def at(k, x):
        if 0 <= x < B:
            return load(owns[k], x)
        side, depth = (0, -x) if x < 0 else (1, x - B + 1)
        return load(responses[k], side, depth - 1) if depth < k else None

    for k in range(2, 9):
        depth = min(k - 1, 9 - k)
        for x in range(-depth, B + depth):
            others = [at(k - 1, x - 1), at(k - 1, x + 1)]
            if 0 <= x < B:
                if x == 0:
                    others.append(history(0, k - 1))
                if x == B - 1:
                    others.append(history(1, k - 1))
                store(owns[k], relax(at(k - 1, x), others, load(source, x), inner), x)
            else:
                side, far = (0, -x) if x < 0 else (1, x - B + 1)
                store(responses[k], relax(at(k - 1, x), others, None, outer[side]), side, far - 1)
    last, edge = owns[8], responses[8]

    def level(x):
        if x < 0:
            return edge[0, 0, B : 2 * B, :] + hist[0, B - 1]
        if x >= B:
            return edge[1, 0, B : 2 * B, :] + hist[1, B - 1]
        return last[x, B : 2 * B, :]

    for x in range(B):
        centre = level(x)
        pressure[x] = centre
        gas_next[0, x] = star[0, x] - 0.1 * (level(x + 1) - level(x - 1))
        gas_next[1, x] = star[1, x] - 0.1 * (last[x, B + 1 : 2 * B + 1, :] - last[x, B - 1 : 2 * B - 1, :])
        gas_next[2, x] = star[2, x] - 0.1 * (beside(centre, 1) - beside(centre, -1))
        gas_next[3, x] = star_rest[0, x]
        gas_next[4, x] = star_rest[1, x]


def body(gas, guess, motion, size, cell, target, on, when, head):
    shape = jax.ShapeDtypeStruct
    [first] = call(first_kernel, [shape((B, 128), F32)], 0, 10**10)()
    y_even, y_odd = call(pack_y_kernel, [tiles(NL)] * 2, 3, 10**6)(first, gas, guess)
    y_odd = swap(y_odd, "gy", 1)
    y_even = swap(y_even, "gy", 0)
    kept, rows, parcels = call(
        renew_kernel,
        [shape((5, 1, PD), F32), shape((2, PD), F32), shape((4, 2, B, NZ), F32)],
        5,
        10**9,
        scratch=[pltpu.VMEM((1, PD), jnp.int32)],
    )(gas, motion, size, cell, target)
    x_even, x_odd = call(pack_x_kernel, [tiles(NL + 1)] * 2, 5, 10**6)(gas, guess, y_odd, y_even, rows)
    [sources] = call(spread_kernel, [shape((3, B * B, NZ), F32)], 6, 10**9, smem=(2, 3, 4))(
        rows, cell, on, when, head, x_even
    )
    sources = sources.reshape(3, B, B, NZ)
    x_odd = swap(x_odd, "gx", 1)
    x_even = swap(x_even, "gx", 0)
    wide = pltpu.VMEM((5, B + 6, 3 * B, NZ), F32)
    star, ps_even, ps_odd = call(
        predict_kernel,
        [shape((3, B, B, NZ), F32), tiles(2 * B + 2), tiles(2 * B + 2)],
        8,
        10**7,
        scratch=[
            wide,
            pltpu.VMEM((B + 2, B, NZ), F32),
            pltpu.VMEM((B, 2 * B, NZ), F32),
            pltpu.VMEM((B + 2, 3 * B, NZ), F32),
        ],
    )(gas, guess, y_odd, y_even, x_odd, x_even, sources, parcels)
    [star_rest] = call(scalars_kernel, [shape((2, B, B, NZ), F32)], 7, 10**8, scratch=[wide])(
        gas, y_odd, y_even, x_odd, x_even, sources, ps_odd
    )
    y_odd = swap(ps_odd, "gy", 1)
    y_even = swap(ps_even, "gy", 0)
    slab = shape((B, 3 * B, NZ), F32)
    scratch = pltpu.VMEM((B, 3 * B, NZ), F32)
    x_even, x_odd, first, source = call(
        slab_kernel,
        [tiles(NH + 2), tiles(NH + 2), slab, slab],
        4,
        10**7,
        scratch=[scratch, scratch, pltpu.VMEM((NH + 2, B, NZ), F32), pltpu.VMEM((NH + 2, B, NZ), F32)],
    )(ps_even, y_odd, y_even, parcels)
    x_odd = swap(x_odd, "gx", 1)
    x_even = swap(x_even, "gx", 0)
    response = pltpu.VMEM((2, 4, 3 * B, NZ), F32)
    gas_next, pressure, arrived = call(
        finish_kernel,
        [shape((5, B, B, NZ), F32), shape((B, B, NZ), F32), shape((4, 5, 1, CAP), F32)],
        8,
        10**7,
        scratch=[scratch, scratch, response, response, pltpu.VMEM((2, NH + 2, B, NZ), F32)],
    )(star, star_rest, first, source, y_even, y_odd, x_odd, x_even)
    return gas_next, pressure, kept, arrived


def solution(mesh):
    in_specs = (
        P(None, "gx", "gy", None),
        P("gx", "gy", None),
        P(None, "gx", "gy"),
        P("gx", "gy"),
        P("gx", "gy"),
        P("gx", "gy"),
        P("gx", "gy"),
        P("gx", "gy"),
        P("gx", "gy"),
    )
    out_specs = (
        P(None, "gx", "gy", None),
        P("gx", "gy", None),
        P(None, "gx", "gy"),
        P(None, None, "gx", "gy"),
    )
    return jax.shard_map(body, mesh=mesh, in_specs=in_specs, out_specs=out_specs, check_vma=False)
```

```python
import jax
import jax.numpy as jnp
from jax import lax
from jax.experimental import pallas as pl
from jax.experimental.pallas import tpu as pltpu
from jax.sharding import PartitionSpec as P

B = 8
NZ = 256
PD = 4096
CAP = 512
CHUNK = 512
F32 = jnp.float32
BF16 = jnp.bfloat16
VMEM = pl.BlockSpec(memory_space=pltpu.VMEM)
SMEM = pl.BlockSpec(memory_space=pltpu.SMEM)

Y_LAYERS = [(1, 0), (1, 1), (1, 2), (0, 0), (0, 1), (2, 0), (2, 1), (3, 0), (3, 1), (4, 0), (4, 1), (5, 0)]
X_LAYERS = [(0, 0), (0, 1), (0, 2), (1, 0), (1, 1), (2, 0), (2, 1), (3, 0), (3, 1), (4, 0), (4, 1), (5, 0)]
NL = 12


def params(limit=16):
    return pltpu.CompilerParams(vmem_limit_bytes=limit * 1024 * 1024)


def tiles(n):
    return jax.ShapeDtypeStruct((n, B, NZ), F32)


def call(kernel, outs, n_in, cost, scratch=(), smem=(), limit=16):
    return pl.pallas_call(
        kernel,
        out_shape=outs,
        in_specs=[SMEM if i in smem else VMEM for i in range(n_in)],
        out_specs=[VMEM] * len(outs),
        scratch_shapes=list(scratch),
        compiler_params=params(limit),
        cost_estimate=pl.CostEstimate(flops=cost, bytes_accessed=cost // 8, transcendentals=0),
    )


def by_parity(axis, act, even, odd):
    first = lax.rem(lax.axis_index(axis), 2) == 0

    @pl.when(first)
    def _():
        act(odd, even)

    @pl.when(jnp.logical_not(first))
    def _():
        act(even, odd)


def swap(shard, axis, start):
    peers = lax.axis_size(axis)
    pairs = [(i + a, i + 1 - a) for i in range(start, peers - 1, 2) for a in range(2)]
    return lax.ppermute(shard, axis, pairs)


def first_kernel(out):
    out[...] = jnp.zeros_like(out)


def pack_y_kernel(_, gas, guess, even, odd):
    def act(low, high):
        for r, (field, depth) in enumerate(Y_LAYERS):
            for side, y in ((low, depth), (high, B - 1 - depth)):
                side[r] = guess[:, y, :] if field == 5 else gas[field, :, y, :]

    by_parity("gy", act, even, odd)


def split(value):
    high = value.astype(BF16).astype(F32)
    return high, value - high


def counting(rows):
    return lax.broadcasted_iota(jnp.int32, (rows, CHUNK), 0).astype(F32).astype(BF16)


def exact(numbers):
    return numbers.astype(F32).astype(BF16)


def one_hot(counted, numbers):
    return jnp.where(counted == exact(numbers), jnp.ones((), BF16), jnp.zeros((), BF16))


def renew_kernel(gas, motion, size, cell, target, kept, rows, parcels, places):
    table = jnp.concatenate([gas[f].reshape(B * B, NZ) for f in range(4)], axis=0)
    high, low = split(table)
    table = jnp.concatenate([high.astype(BF16), low.astype(BF16)], axis=1)
    at_z = counting(NZ)
    at_xy = lax.broadcasted_iota(jnp.int32, (B * B, CHUNK), 0)
    heading = lax.broadcasted_iota(jnp.int32, (B, NZ), 0)
    blocks = [heading == target[:, n * NZ : (n + 1) * NZ] for n in range(PD // NZ)]
    a = lax.broadcasted_iota(jnp.int32, (NZ, NZ), 0)
    b = lax.broadcasted_iota(jnp.int32, (NZ, NZ), 1)
    upper = jnp.where(a <= b, 1.0, 0.0).astype(BF16)
    marks = jnp.concatenate([jnp.where(chosen, 1.0, 0.0) for chosen in blocks], axis=0).astype(BF16)
    ranks = jnp.dot(marks, upper, preferred_element_type=F32)
    before = jnp.zeros((B, 1), F32)
    for n, chosen in enumerate(blocks):
        rank = ranks[B * n : B * n + B] + before
        before = rank[:, NZ - 1 :]
        place = jnp.where(chosen & (heading < 4), rank + heading.astype(F32) * float(CAP), 0.0)
        places[:, n * NZ : (n + 1) * NZ] = jnp.sum(place, axis=0, keepdims=True).astype(jnp.int32) - 1
    moved = jnp.zeros((10 * B, NZ), F32)
    at_high = lax.broadcasted_iota(jnp.int32, (B, CHUNK), 0)
    across = (((1,), (1,)), ((), ()))
    for n in range(PD // CHUNK):
        part = slice(n * CHUNK, (n + 1) * CHUNK)
        cells = cell[:, part]
        goal = target[:, part]
        in_z = one_hot(at_z, cells & (NZ - 1))
        in_xy = at_xy == (cells >> 8)
        found = jnp.dot(table, jnp.concatenate([in_z, in_z], axis=0), preferred_element_type=F32)
        local = [
            jnp.sum(jnp.where(in_xy, found[f * B * B : (f + 1) * B * B], 0.0), axis=0, keepdims=True)
            for f in range(4)
        ]
        u, v, w, temperature = (motion[f, :, part] for f in range(4))
        diameter = size[:, part]
        excess = local[3] - temperature
        vapour = 0.5 * diameter * jax.nn.sigmoid(excess)
        renewed = [
            u + 0.4 * (local[0] - u),
            v + 0.4 * (local[1] - v),
            w + 0.2 * ((local[2] - w) * 2.0 - 1.0),
            temperature + 0.2 * excess,
            diameter - 0.2 * vapour,
        ]
        drag = 0.5 * diameter * diameter * (w - local[2])
        alive = goal >= 0
        for f in range(5):
            kept[f, :, part] = jnp.where(goal == 4, renewed[f], 0.0)
        rows[0:1, part] = jnp.where(alive, drag, 0.0)
        rows[1:2, part] = jnp.where(alive, vapour, 0.0)
        place = places[:, part]
        in_low = one_hot(at_z, place & (NZ - 1))
        in_high = at_high == (place >> 8)
        split_up = [split(value) for value in renewed]
        leaving = [jnp.where(in_high, split_up[f][piece], 0.0) for piece in range(2) for f in range(5)]
        moved = moved + lax.dot_general(
            jnp.concatenate(leaving, axis=0).astype(BF16), in_low, across, preferred_element_type=F32
        )
    moved = moved[: 5 * B] + moved[5 * B :]
    for d in range(4):
        for f in range(5):
            for half in range(2):
                at = f * B + 2 * d + half
                r = 2 * f + half
                parcels[d, r // B, r % B : r % B + 1, :] = moved[at : at + 1]
        parcels[d, 1, 2:, :] = jnp.zeros((B - 2, NZ), F32)


def spread_kernel(rows, cell, on, when, head, _, sources):
    at_z = counting(NZ)
    at_xy = counting(B * B)
    total = jnp.zeros((4 * B * B, NZ), F32)
    across = (((1,), (1,)), ((), ()))
    for n in range(PD // CHUNK):
        part = slice(n * CHUNK, (n + 1) * CHUNK)
        cells = cell[:, part]
        in_z = one_hot(at_z, cells & (NZ - 1))
        in_xy = at_xy == exact(cells >> 8)
        pieces = [*split(rows[0:1, part]), *split(rows[1:2, part])]
        given = jnp.concatenate([jnp.where(in_xy, piece.astype(BF16), jnp.zeros((), BF16)) for piece in pieces], axis=0)
        total = total + lax.dot_general(given, in_z, across, preferred_element_type=F32)
    q = B * B
    steam = total[2 * q : 3 * q] + total[3 * q :]
    sources[0] = total[:q] + total[q : 2 * q]
    sources[1] = -2.0 * steam
    sources[2] = steam
    lanes = lax.broadcasted_iota(jnp.int32, (1, NZ), 1)
    for s in range(B):
        ramp = jnp.clip((100.0 - when[0, s].astype(F32)) / 50.0, 0.0, 1.0)
        strength = 3.0 * ramp * on[0, s].astype(F32)
        where = head[0, s]
        row = pl.ds(where >> 8, 1)
        taken = jnp.where(lanes == (where & (NZ - 1)), strength, 0.0)
        for f in range(2):
            sources[f, row, :] = sources[f, row, :] - taken


def pack_x_kernel(gas, guess, y_odd, y_even, parcels, even, odd):
    def planes(low, high):
        for side, near, step, heading in ((low, 0, 1, 1), (high, B - 1, -1, 0)):
            side[NL + 1] = parcels[heading, 0]
            side[NL + 2] = parcels[heading, 1]
            for r, (field, depth) in enumerate(X_LAYERS):
                x = near + step * depth
                side[r] = guess[x] if field == 5 else gas[field, x]

            def corners(below, above, side=side, near=near, step=step):
                for h, halo in enumerate((below, above)):
                    for r, (layer, x) in enumerate(((3, near), (4, near), (0, near), (0, near + step))):
                        side[NL, 4 * h + r : 4 * h + r + 1, :] = halo[layer, x : x + 1, :]

            by_parity("gy", corners, y_even, y_odd)

    by_parity("gx", planes, even, odd)


def beside(value, by):
    lane = lax.broadcasted_iota(jnp.int32, value.shape, 1)
    turned = pltpu.roll(value, (-by) % NZ, axis=1)
    return jnp.where((lane < NZ - by) if by > 0 else (lane >= -by), turned, 0.0)


def advance(e, f, x, rows, first):
    def at(field, dx, dy):
        return e[field, x + dx, first + dy : first + dy + rows, :]

    centre = at(f, 0, 0)
    xs = {s: at(f, s, 0) for s in (-2, -1, 1, 2)}
    ys = {s: at(f, 0, s) for s in (-2, -1, 1, 2)}
    zs = {s: beside(centre, s) for s in (-2, -1, 1, 2)}
    laplace = xs[1] + xs[-1] + ys[1] + ys[-1] + zs[1] + zs[-1] - 6.0 * centre
    transport = 0.0
    for axis, shifted in enumerate((xs, ys, zs)):
        slope = 8.0 * (shifted[1] - shifted[-1]) - (shifted[2] - shifted[-2])
        transport = transport + at(axis, 0, 0) * slope
    return centre + (0.02 * laplace - (0.2 / 12.0) * transport)


def fill_own(gas, e, fields):
    for k, f in enumerate(fields):
        e[k, 3 : 3 + B, B : 2 * B, :] = gas[f]


def predict_kernel(gas, guess, y_odd, y_even, x_odd, x_even, sources, parcels, star, even, odd, e, wide, tall, q):
    gx = lax.axis_index("gx")
    gy = lax.axis_index("gy")
    has_left, has_right = gx > 0, gx < lax.axis_size("gx") - 1
    has_below, has_above = gy > 0, gy < lax.axis_size("gy") - 1
    fill_own(gas, e, range(3))
    q[1 : 1 + B, B : 2 * B, :] = guess[...]

    def fill_y(below, above):
        for r, (field, depth) in enumerate(Y_LAYERS):
            for halo, y in ((below, B - 1 - depth), (above, 2 * B + depth)):
                if field == 5:
                    q[1 : 1 + B, y, :] = halo[r]
                elif field < 3:
                    e[field, 3 : 3 + B, y, :] = halo[r]

    def fill_x(left, right):
        for r, (field, depth) in enumerate(X_LAYERS):
            for halo, x in ((left, -1 - depth), (right, B + depth)):
                if field == 5:
                    q[x + 1, B : 2 * B, :] = halo[r]
                elif field < 3:
                    e[field, x + 3, B : 2 * B, :] = halo[r]
        for halo, near, step in ((left, 2, -1), (right, 3 + B, 1)):
            for h, (y, onward) in enumerate(((B - 1, -1), (2 * B, 1))):
                spots = ((0, near, y), (0, near, y + onward), (1, near, y), (1, near + step, y))
                for r, (field, x, row) in enumerate(spots):
                    e[field, x, row : row + 1, :] = halo[NL, 4 * h + r : 4 * h + r + 1, :]

    by_parity("gy", fill_y, y_even, y_odd)
    by_parity("gx", fill_x, x_even, x_odd)
    for x in range(-1, B + 1):
        value = advance(e, 0, x + 3, B, B)
        if x < 0:
            value = jnp.where(has_left, value, 0.0)
        if x == B:
            value = jnp.where(has_right, value, 0.0)
        wide[x + 1] = value
        if 0 <= x < B:
            star[0, x] = value
    for x in range(B):
        value = advance(e, 1, x + 3, B + 2, B - 1)
        row = lax.broadcasted_iota(jnp.int32, value.shape, 0)
        inside = ((row > 0) | has_below) & ((row < B + 1) | has_above)
        value = jnp.where(inside, value, 0.0)
        tall[x, : B + 2, :] = value
        star[1, x] = value[1 : 1 + B]
    for x in range(B):
        w = advance(e, 2, x + 3, B, B) + 0.2 * sources[0, x]
        star[2, x] = w
        spread = wide[x + 2] - wide[x] + (tall[x, 2 : 2 + B, :] - tall[x, :B, :])
        source = 2.5 * (spread + (beside(w, 1) - beside(w, -1)))
        centre = q[x + 1, B : 2 * B, :]
        around = q[x + 2, B : 2 * B, :] + q[x, B : 2 * B, :]
        around = around + q[x + 1, B + 1 : 2 * B + 1, :] + q[x + 1, B - 1 : 2 * B - 1, :]
        field = (around + beside(centre, 1) + beside(centre, -1) - source) * (1.0 / 6.0)
        for side in (even, odd):
            side[x] = field
            side[B + x] = source

    def attach(low, high):
        for side, heading in ((high, 2), (low, 3)):
            side[2 * B] = parcels[heading, 0]
            side[2 * B + 1] = parcels[heading, 1]

    by_parity("gy", attach, even, odd)


def scalars_kernel(gas, y_odd, y_even, x_odd, x_even, sources, _, star, e):
    fill_own(gas, e, range(5))

    def fill_y(below, above):
        for r, (field, depth) in enumerate(Y_LAYERS):
            if field in (3, 4):
                e[field, 3 : 3 + B, B - 1 - depth, :] = below[r]
                e[field, 3 : 3 + B, 2 * B + depth, :] = above[r]

    def fill_x(left, right):
        for r, (field, depth) in enumerate(X_LAYERS):
            if field in (3, 4):
                e[field, 2 - depth, B : 2 * B, :] = left[r]
                e[field, B + 3 + depth, B : 2 * B, :] = right[r]

    by_parity("gy", fill_y, y_even, y_odd)
    by_parity("gx", fill_x, x_even, x_odd)
    for f in (3, 4):
        for x in range(B):
            star[f - 3, x] = advance(e, f, x + 3, B, B) + 0.2 * sources[f - 2, x]


NH = 15
HALF = NZ // 2


def load(ref, *lead):
    return [[ref[(*lead, slice(B * t, B * t + B), slice(HALF * h, HALF * h + HALF))] for h in range(2)] for t in range(3)]


def store(ref, plane, *lead):
    for t in range(3):
        for h in range(2):
            ref[(*lead, slice(B * t, B * t + B), slice(HALF * h, HALF * h + HALF))] = plane[t][h]


def add(*planes):
    planes = [p for p in planes if p is not None]
    return [[sum((p[t][h] for p in planes[1:]), planes[0][t][h]) for h in range(2)] for t in range(3)]


def beside_plane(c):
    row = lax.broadcasted_iota(jnp.int32, (B, HALF), 0)
    lane = lax.broadcasted_iota(jnp.int32, (B, HALF), 1)
    top, bottom, start, end = row == 0, row == B - 1, lane == 0, lane == HALF - 1
    out = []
    for t in range(3):
        after = [pltpu.roll(c[t][h], 1, axis=1) for h in range(2)]
        ahead = [pltpu.roll(c[t][h], HALF - 1, axis=1) for h in range(2)]
        along_z = [
            jnp.where(start, 0.0, after[0]) + jnp.where(end, ahead[1], ahead[0]),
            jnp.where(start, after[0], after[1]) + jnp.where(end, 0.0, ahead[1]),
        ]
        tile = []
        for h in range(2):
            down = pltpu.roll(c[t][h], 1, axis=0)
            if t > 0:
                down = jnp.where(top, pltpu.roll(c[t - 1][h], 1, axis=0), down)
            up = pltpu.roll(c[t][h], B - 1, axis=0)
            if t < 2:
                up = jnp.where(bottom, pltpu.roll(c[t + 1][h], B - 1, axis=0), up)
            tile.append(along_z[h] + (down + up))
        out.append(tile)
    return out


def relax(centre, others, source, scale):
    total = add(*others, None if centre is None else beside_plane(centre))
    if source is not None:
        total = [[total[t][h] - source[t][h] for h in range(2)] for t in range(3)]
    return [[total[t][h] * scale[t] for h in range(2)] for t in range(3)]


def weights(flags_x, flags_y):
    out = []
    for flag_y in flags_y:
        value = jnp.full((B, HALF), 1.0 / 6.0, F32)
        for flag in (*flags_x, flag_y):
            if flag is not None:
                value = jnp.where(flag, value, 0.0)
        out.append(value)
    return out


def slab_kernel(own, y_odd, y_even, even, odd, first, source, f2, f3, f4, f5, f6, low, high):
    gy = lax.axis_index("gy")
    scale = weights((), (gy > 0, None, gy < lax.axis_size("gy") - 1))
    row = lax.broadcasted_iota(jnp.int32, (B, HALF), 0)
    for x in range(B):
        first[x, B : 2 * B, :] = own[x]
        source[x, B : 2 * B, :] = own[B + x]

    def fill(below, above):
        for x in range(B):
            for k, halo in ((0, below), (2, above)):
                first[x, k * B : (k + 1) * B, :] = halo[x]
                source[x, k * B : (k + 1) * B, :] = halo[B + x]

    by_parity("gy", fill, y_even, y_odd)

    def keep(side, k, plane):
        for h in range(2):
            part = slice(HALF * h, HALF * h + HALF)
            side[k - 1, :, part] = plane[1][h]
            if k < B:
                side[B - 1 + k, k:, part] = plane[0][h][k:]
                side[2 * B - 1 - k, : B - k, part] = plane[2][h][: B - k]

    for side, x in ((low, 0), (high, B - 1)):
        keep(side, 1, load(first, x))
    levels = {1: first, 2: f2, 3: f3, 4: f4, 5: f5, 6: f6, 7: f5}
    for k in range(2, 9):
        depth = 9 - k
        now = levels[k - 1]
        for x in range(B):
            if depth <= x < B - depth:
                continue
            others = [load(now, y) for y in (x - 1, x + 1) if 0 <= y < B]
            plane = relax(load(now, x), others, load(source, x), scale)
            if k < 8:
                store(levels[k], plane, x)
            for side, face in ((low, 0), (high, B - 1)):
                if x == face:
                    keep(side, k, plane)

    def send(low_out, high_out):
        low_out[...] = low[...]
        high_out[...] = high[...]

    by_parity("gx", send, even, odd)


def finish_kernel(star, star_rest, first, source, f2, f3, f4, early_odd, early_even, y_even, y_odd, x_odd, x_even, gas_next, pressure, arrived, o0, o1, r0, r1, hist):
    gx = lax.axis_index("gx")
    gy = lax.axis_index("gy")
    flags_y = (gy > 0, None, gy < lax.axis_size("gy") - 1)
    inner = weights((), flags_y)
    outer = [weights((gx > 0,), flags_y), weights((gx < lax.axis_size("gx") - 1,), flags_y)]

    def arrive(d, halo, at):
        for f in range(5):
            for half in range(2):
                r = 2 * f + half
                arrived[d, f, :, half * NZ : (half + 1) * NZ] = halo[at + r // B, r % B : r % B + 1, :]

    def take_y(below, above):
        arrive(2, below, 2 * B)
        arrive(3, above, 2 * B)

    def take_x(left, right):
        hist[0] = left[...]
        hist[1] = right[...]

    by_parity("gy", take_y, y_even, y_odd)
    by_parity("gx", take_x, x_even, x_odd)

    def take_early(left, right):
        arrive(0, left, NL + 1)
        arrive(1, right, NL + 1)

    by_parity("gx", take_early, early_even, early_odd)

    def history(side, k):
        at = (B - 1 + k, k - 1, 2 * B - 1 - k)
        return [[hist[side, at[t], :, slice(HALF * h, HALF * h + HALF)] for h in range(2)] for t in range(3)]

    slabs = {1: first, 2: f2, 3: f3, 4: f4}
    owns = {k: (o0, o1)[k % 2] for k in range(2, 9)}

    def alone(k, x):
        return k in slabs and k - 1 <= x <= B - k

    responses = {k: (r0, r1)[k % 2] for k in range(2, 9)}

    def at(k, x):
        if 0 <= x < B:
            return load(slabs[k] if alone(k, x) else owns[k], x)
        side, depth = (0, -x) if x < 0 else (1, x - B + 1)
        return load(responses[k], side, depth - 1) if depth < k else None

    for k in range(2, 9):
        depth = min(k - 1, 9 - k)
        for x in range(-depth, B + depth):
            if alone(k, x):
                continue
            if k == 2 and 0 <= x < B:
                drive = history(0 if x == 0 else 1, 1)
                drive = [[drive[t][h] * inner[t] for h in range(2)] for t in range(3)]
                store(owns[k], add(load(f2, x), drive), x)
                continue
            others = [at(k - 1, x - 1), at(k - 1, x + 1)]
            if 0 <= x < B:
                if x == 0:
                    others.append(history(0, k - 1))
                if x == B - 1:
                    others.append(history(1, k - 1))
                store(owns[k], relax(at(k - 1, x), others, load(source, x), inner), x)
            else:
                side, far = (0, -x) if x < 0 else (1, x - B + 1)
                store(responses[k], relax(at(k - 1, x), others, None, outer[side]), side, far - 1)
    last, edge = owns[8], responses[8]

    def level(x):
        if x < 0:
            return edge[0, 0, B : 2 * B, :] + hist[0, B - 1]
        if x >= B:
            return edge[1, 0, B : 2 * B, :] + hist[1, B - 1]
        return last[x, B : 2 * B, :]

    for x in range(B):
        centre = level(x)
        pressure[x] = centre
        gas_next[0, x] = star[0, x] - 0.1 * (level(x + 1) - level(x - 1))
        gas_next[1, x] = star[1, x] - 0.1 * (last[x, B + 1 : 2 * B + 1, :] - last[x, B - 1 : 2 * B - 1, :])
        gas_next[2, x] = star[2, x] - 0.1 * (beside(centre, 1) - beside(centre, -1))
        gas_next[3, x] = star_rest[0, x]
        gas_next[4, x] = star_rest[1, x]


def body(gas, guess, motion, size, cell, target, on, when, head):
    shape = jax.ShapeDtypeStruct
    [first] = call(first_kernel, [shape((B, 128), F32)], 0, 10**10)()
    y_even, y_odd = call(pack_y_kernel, [tiles(NL)] * 2, 3, 10**6)(first, gas, guess)
    y_odd = swap(y_odd, "gy", 1)
    y_even = swap(y_even, "gy", 0)
    kept, rows, parcels = call(
        renew_kernel,
        [shape((5, 1, PD), F32), shape((2, PD), F32), shape((4, 2, B, NZ), F32)],
        5,
        10**9,
        scratch=[pltpu.VMEM((1, PD), jnp.int32)],
    )(gas, motion, size, cell, target)
    x_even, x_odd = call(pack_x_kernel, [tiles(NL + 3)] * 2, 5, 10**6)(gas, guess, y_odd, y_even, parcels)
    [sources] = call(spread_kernel, [shape((3, B * B, NZ), F32)], 6, 10**9, smem=(2, 3, 4))(
        rows, cell, on, when, head, x_even
    )
    sources = sources.reshape(3, B, B, NZ)
    x_odd = swap(x_odd, "gx", 1)
    x_even = swap(x_even, "gx", 0)
    wide = pltpu.VMEM((5, B + 6, 3 * B, NZ), F32)
    star, ps_even, ps_odd = call(
        predict_kernel,
        [shape((3, B, B, NZ), F32), tiles(2 * B + 2), tiles(2 * B + 2)],
        8,
        10**7,
        scratch=[
            wide,
            pltpu.VMEM((B + 2, B, NZ), F32),
            pltpu.VMEM((B, 2 * B, NZ), F32),
            pltpu.VMEM((B + 2, 3 * B, NZ), F32),
        ],
    )(gas, guess, y_odd, y_even, x_odd, x_even, sources, parcels)
    [star_rest] = call(scalars_kernel, [shape((2, B, B, NZ), F32)], 7, 10**8, scratch=[wide])(
        gas, y_odd, y_even, x_odd, x_even, sources, ps_odd
    )
    y_odd = swap(ps_odd, "gy", 1)
    y_even = swap(ps_even, "gy", 0)
    slab = shape((B, 3 * B, NZ), F32)
    scratch = pltpu.VMEM((B, 3 * B, NZ), F32)
    early_odd, early_even = x_odd, x_even
    x_even, x_odd, *slabs = call(
        slab_kernel,
        [tiles(NH), tiles(NH)] + [slab] * 5,
        3,
        10**7,
        scratch=[scratch, scratch, pltpu.VMEM((NH, B, NZ), F32), pltpu.VMEM((NH, B, NZ), F32)],
    )(ps_even, y_odd, y_even)
    x_odd = swap(x_odd, "gx", 1)
    x_even = swap(x_even, "gx", 0)
    response = pltpu.VMEM((2, 4, 3 * B, NZ), F32)
    gas_next, pressure, arrived = call(
        finish_kernel,
        [shape((5, B, B, NZ), F32), shape((B, B, NZ), F32), shape((4, 5, 1, CAP), F32)],
        13,
        10**7,
        scratch=[scratch, scratch, response, response, pltpu.VMEM((2, NH, B, NZ), F32)],
    )(star, star_rest, *slabs, early_odd, early_even, y_even, y_odd, x_odd, x_even)
    return gas_next, pressure, kept, arrived


def solution(mesh):
    in_specs = (
        P(None, "gx", "gy", None),
        P("gx", "gy", None),
        P(None, "gx", "gy"),
        P("gx", "gy"),
        P("gx", "gy"),
        P("gx", "gy"),
        P("gx", "gy"),
        P("gx", "gy"),
        P("gx", "gy"),
    )
    out_specs = (
        P(None, "gx", "gy", None),
        P("gx", "gy", None),
        P(None, "gx", "gy"),
        P(None, None, "gx", "gy"),
    )
    return jax.shard_map(body, mesh=mesh, in_specs=in_specs, out_specs=out_specs, check_vma=False)
```

```python
import jax
import jax.numpy as jnp
from jax import lax
from jax.experimental import pallas as pl
from jax.experimental.pallas import tpu as pltpu
from jax.sharding import PartitionSpec as P

B = 8
NZ = 256
PD = 4096
CAP = 512
CHUNK = 512
F32 = jnp.float32
BF16 = jnp.bfloat16
VMEM = pl.BlockSpec(memory_space=pltpu.VMEM)
SMEM = pl.BlockSpec(memory_space=pltpu.SMEM)

Y_LAYERS = [(1, 0), (1, 1), (1, 2), (0, 0), (0, 1), (2, 0), (2, 1), (3, 0), (3, 1), (4, 0), (4, 1), (5, 0)]
X_LAYERS = [(0, 0), (0, 1), (0, 2), (1, 0), (1, 1), (2, 0), (2, 1), (3, 0), (3, 1), (4, 0), (4, 1), (5, 0)]
NL = 12


def params(limit=16):
    return pltpu.CompilerParams(vmem_limit_bytes=limit * 1024 * 1024)


def tiles(n):
    return jax.ShapeDtypeStruct((n, B, NZ), F32)


def call(kernel, outs, n_in, cost, scratch=(), smem=(), limit=16):
    return pl.pallas_call(
        kernel,
        out_shape=outs,
        in_specs=[SMEM if i in smem else VMEM for i in range(n_in)],
        out_specs=[VMEM] * len(outs),
        scratch_shapes=list(scratch),
        compiler_params=params(limit),
        cost_estimate=pl.CostEstimate(flops=cost, bytes_accessed=cost // 8, transcendentals=0),
    )


def by_parity(axis, act, even, odd):
    first = lax.rem(lax.axis_index(axis), 2) == 0

    @pl.when(first)
    def _():
        act(odd, even)

    @pl.when(jnp.logical_not(first))
    def _():
        act(even, odd)


def swap(shard, axis, start):
    peers = lax.axis_size(axis)
    pairs = [(i + a, i + 1 - a) for i in range(start, peers - 1, 2) for a in range(2)]
    return lax.ppermute(shard, axis, pairs)


def first_kernel(out):
    out[...] = jnp.zeros_like(out)


def pack_y_kernel(_, gas, guess, even, odd):
    def act(low, high):
        for r, (field, depth) in enumerate(Y_LAYERS):
            for side, y in ((low, depth), (high, B - 1 - depth)):
                side[r] = guess[:, y, :] if field == 5 else gas[field, :, y, :]

    by_parity("gy", act, even, odd)


def split(value):
    high = value.astype(BF16).astype(F32)
    return high, value - high


def counting(rows):
    return lax.broadcasted_iota(jnp.int32, (rows, CHUNK), 0).astype(F32).astype(BF16)


def exact(numbers):
    return numbers.astype(F32).astype(BF16)


def one_hot(counted, numbers):
    return jnp.where(counted == exact(numbers), jnp.ones((), BF16), jnp.zeros((), BF16))


def renew_kernel(gas, motion, size, cell, target, kept, rows, parcels, places):
    table = jnp.concatenate([gas[f].reshape(B * B, NZ) for f in range(4)], axis=0)
    high, low = split(table)
    table = jnp.concatenate([high.astype(BF16), low.astype(BF16)], axis=1)
    at_z = counting(NZ)
    at_xy = lax.broadcasted_iota(jnp.int32, (B * B, CHUNK), 0)
    heading = lax.broadcasted_iota(jnp.int32, (B, NZ), 0)
    blocks = [heading == target[:, n * NZ : (n + 1) * NZ] for n in range(PD // NZ)]
    a = lax.broadcasted_iota(jnp.int32, (NZ, NZ), 0)
    b = lax.broadcasted_iota(jnp.int32, (NZ, NZ), 1)
    upper = jnp.where(a <= b, 1.0, 0.0).astype(BF16)
    marks = jnp.concatenate([jnp.where(chosen, 1.0, 0.0) for chosen in blocks], axis=0).astype(BF16)
    ranks = jnp.dot(marks, upper, preferred_element_type=F32)
    before = jnp.zeros((B, 1), F32)
    for n, chosen in enumerate(blocks):
        rank = ranks[B * n : B * n + B] + before
        before = rank[:, NZ - 1 :]
        place = jnp.where(chosen & (heading < 4), rank + heading.astype(F32) * float(CAP), 0.0)
        places[:, n * NZ : (n + 1) * NZ] = jnp.sum(place, axis=0, keepdims=True).astype(jnp.int32) - 1
    moved = jnp.zeros((10 * B, NZ), F32)
    at_high = lax.broadcasted_iota(jnp.int32, (B, CHUNK), 0)
    across = (((1,), (1,)), ((), ()))
    for n in range(PD // CHUNK):
        part = slice(n * CHUNK, (n + 1) * CHUNK)
        cells = cell[:, part]
        goal = target[:, part]
        in_z = one_hot(at_z, cells & (NZ - 1))
        in_xy = at_xy == (cells >> 8)
        found = jnp.dot(table, jnp.concatenate([in_z, in_z], axis=0), preferred_element_type=F32)
        local = [
            jnp.sum(jnp.where(in_xy, found[f * B * B : (f + 1) * B * B], 0.0), axis=0, keepdims=True)
            for f in range(4)
        ]
        u, v, w, temperature = (motion[f, :, part] for f in range(4))
        diameter = size[:, part]
        excess = local[3] - temperature
        vapour = 0.5 * diameter * jax.nn.sigmoid(excess)
        renewed = [
            u + 0.4 * (local[0] - u),
            v + 0.4 * (local[1] - v),
            w + 0.2 * ((local[2] - w) * 2.0 - 1.0),
            temperature + 0.2 * excess,
            diameter - 0.2 * vapour,
        ]
        drag = 0.5 * diameter * diameter * (w - local[2])
        alive = goal >= 0
        for f in range(5):
            kept[f, :, part] = jnp.where(goal == 4, renewed[f], 0.0)
        rows[0:1, part] = jnp.where(alive, drag, 0.0)
        rows[1:2, part] = jnp.where(alive, vapour, 0.0)
        place = places[:, part]
        in_low = one_hot(at_z, place & (NZ - 1))
        in_high = at_high == (place >> 8)
        split_up = [split(value) for value in renewed]
        leaving = [jnp.where(in_high, split_up[f][piece], 0.0) for piece in range(2) for f in range(5)]
        moved = moved + lax.dot_general(
            jnp.concatenate(leaving, axis=0).astype(BF16), in_low, across, preferred_element_type=F32
        )
    moved = moved[: 5 * B] + moved[5 * B :]
    for d in range(4):
        for f in range(5):
            for half in range(2):
                at = f * B + 2 * d + half
                r = 2 * f + half
                parcels[d, r // B, r % B : r % B + 1, :] = moved[at : at + 1]
        parcels[d, 1, 2:, :] = jnp.zeros((B - 2, NZ), F32)


def spread_kernel(rows, cell, on, when, head, _, sources):
    at_z = counting(NZ)
    at_xy = counting(B * B)
    total = jnp.zeros((4 * B * B, NZ), F32)
    across = (((1,), (1,)), ((), ()))
    for n in range(PD // CHUNK):
        part = slice(n * CHUNK, (n + 1) * CHUNK)
        cells = cell[:, part]
        in_z = one_hot(at_z, cells & (NZ - 1))
        in_xy = at_xy == exact(cells >> 8)
        pieces = [*split(rows[0:1, part]), *split(rows[1:2, part])]
        given = jnp.concatenate([jnp.where(in_xy, piece.astype(BF16), jnp.zeros((), BF16)) for piece in pieces], axis=0)
        total = total + lax.dot_general(given, in_z, across, preferred_element_type=F32)
    q = B * B
    steam = total[2 * q : 3 * q] + total[3 * q :]
    sources[0] = total[:q] + total[q : 2 * q]
    sources[1] = -2.0 * steam
    sources[2] = steam
    lanes = lax.broadcasted_iota(jnp.int32, (1, NZ), 1)
    for s in range(B):
        ramp = jnp.clip((100.0 - when[0, s].astype(F32)) / 50.0, 0.0, 1.0)
        strength = 3.0 * ramp * on[0, s].astype(F32)
        where = head[0, s]
        row = pl.ds(where >> 8, 1)
        taken = jnp.where(lanes == (where & (NZ - 1)), strength, 0.0)
        for f in range(2):
            sources[f, row, :] = sources[f, row, :] - taken


def pack_x_kernel(gas, guess, y_odd, y_even, parcels, even, odd):
    def planes(low, high):
        for side, near, step, heading in ((low, 0, 1, 1), (high, B - 1, -1, 0)):
            side[NL + 1] = parcels[heading, 0]
            side[NL + 2] = parcels[heading, 1]
            for r, (field, depth) in enumerate(X_LAYERS):
                x = near + step * depth
                side[r] = guess[x] if field == 5 else gas[field, x]

            def corners(below, above, side=side, near=near, step=step):
                for h, halo in enumerate((below, above)):
                    for r, (layer, x) in enumerate(((3, near), (4, near), (0, near), (0, near + step))):
                        side[NL, 4 * h + r : 4 * h + r + 1, :] = halo[layer, x : x + 1, :]

            by_parity("gy", corners, y_even, y_odd)

    by_parity("gx", planes, even, odd)


def beside(value, by):
    lane = lax.broadcasted_iota(jnp.int32, value.shape, 1)
    turned = pltpu.roll(value, (-by) % NZ, axis=1)
    return jnp.where((lane < NZ - by) if by > 0 else (lane >= -by), turned, 0.0)


def advance(e, f, x, rows, first):
    def at(field, dx, dy):
        return e[field, x + dx, first + dy : first + dy + rows, :]

    centre = at(f, 0, 0)
    xs = {s: at(f, s, 0) for s in (-2, -1, 1, 2)}
    ys = {s: at(f, 0, s) for s in (-2, -1, 1, 2)}
    zs = {s: beside(centre, s) for s in (-2, -1, 1, 2)}
    laplace = xs[1] + xs[-1] + ys[1] + ys[-1] + zs[1] + zs[-1] - 6.0 * centre
    transport = 0.0
    for axis, shifted in enumerate((xs, ys, zs)):
        slope = 8.0 * (shifted[1] - shifted[-1]) - (shifted[2] - shifted[-2])
        transport = transport + at(axis, 0, 0) * slope
    return centre + (0.02 * laplace - (0.2 / 12.0) * transport)


def fill_own(gas, e, fields):
    for k, f in enumerate(fields):
        e[k, 3 : 3 + B, B : 2 * B, :] = gas[f]


def predict_kernel(gas, guess, y_odd, y_even, x_odd, x_even, sources, parcels, star, source_out, even, odd, e, wide, tall, q):
    gx = lax.axis_index("gx")
    gy = lax.axis_index("gy")
    has_left, has_right = gx > 0, gx < lax.axis_size("gx") - 1
    has_below, has_above = gy > 0, gy < lax.axis_size("gy") - 1
    fill_own(gas, e, range(3))
    q[1 : 1 + B, B : 2 * B, :] = guess[...]

    def fill_y(below, above):
        for r, (field, depth) in enumerate(Y_LAYERS):
            for halo, y in ((below, B - 1 - depth), (above, 2 * B + depth)):
                if field == 5:
                    q[1 : 1 + B, y, :] = halo[r]
                elif field < 3:
                    e[field, 3 : 3 + B, y, :] = halo[r]

    def fill_x(left, right):
        for r, (field, depth) in enumerate(X_LAYERS):
            for halo, x in ((left, -1 - depth), (right, B + depth)):
                if field == 5:
                    q[x + 1, B : 2 * B, :] = halo[r]
                elif field < 3:
                    e[field, x + 3, B : 2 * B, :] = halo[r]
        for halo, near, step in ((left, 2, -1), (right, 3 + B, 1)):
            for h, (y, onward) in enumerate(((B - 1, -1), (2 * B, 1))):
                spots = ((0, near, y), (0, near, y + onward), (1, near, y), (1, near + step, y))
                for r, (field, x, row) in enumerate(spots):
                    e[field, x, row : row + 1, :] = halo[NL, 4 * h + r : 4 * h + r + 1, :]

    by_parity("gy", fill_y, y_even, y_odd)
    by_parity("gx", fill_x, x_even, x_odd)
    for x in range(-1, B + 1):
        value = advance(e, 0, x + 3, B, B)
        if x < 0:
            value = jnp.where(has_left, value, 0.0)
        if x == B:
            value = jnp.where(has_right, value, 0.0)
        wide[x + 1] = value
        if 0 <= x < B:
            star[0, x] = value
    for x in range(B):
        value = advance(e, 1, x + 3, B + 2, B - 1)
        row = lax.broadcasted_iota(jnp.int32, value.shape, 0)
        inside = ((row > 0) | has_below) & ((row < B + 1) | has_above)
        value = jnp.where(inside, value, 0.0)
        tall[x, : B + 2, :] = value
        star[1, x] = value[1 : 1 + B]
    for x in range(B):
        w = advance(e, 2, x + 3, B, B) + 0.2 * sources[0, x]
        star[2, x] = w
        spread = wide[x + 2] - wide[x] + (tall[x, 2 : 2 + B, :] - tall[x, :B, :])
        source = 2.5 * (spread + (beside(w, 1) - beside(w, -1)))
        centre = q[x + 1, B : 2 * B, :]
        around = q[x + 2, B : 2 * B, :] + q[x, B : 2 * B, :]
        around = around + q[x + 1, B + 1 : 2 * B + 1, :] + q[x + 1, B - 1 : 2 * B - 1, :]
        field = (around + beside(centre, 1) + beside(centre, -1) - source) * (1.0 / 6.0)
        source_out[x] = source
        for side in (even, odd):
            side[x] = field
            side[B + x] = source

    def attach(low, high):
        for side, heading, row in ((high, 2, 0), (low, 3, B - 1)):
            for x in range(B):
                side[B + x, row : row + 1, :] = parcels[heading, 0, x : x + 1, :]
            side[2 * B] = parcels[heading, 1]

    by_parity("gy", attach, even, odd)


def scalars_kernel(gas, y_odd, y_even, x_odd, x_even, sources, _, star, e):
    fill_own(gas, e, range(5))

    def fill_y(below, above):
        for r, (field, depth) in enumerate(Y_LAYERS):
            if field in (3, 4):
                e[field, 3 : 3 + B, B - 1 - depth, :] = below[r]
                e[field, 3 : 3 + B, 2 * B + depth, :] = above[r]

    def fill_x(left, right):
        for r, (field, depth) in enumerate(X_LAYERS):
            if field in (3, 4):
                e[field, 2 - depth, B : 2 * B, :] = left[r]
                e[field, B + 3 + depth, B : 2 * B, :] = right[r]

    by_parity("gy", fill_y, y_even, y_odd)
    by_parity("gx", fill_x, x_even, x_odd)
    for f in (3, 4):
        for x in range(B):
            star[f - 3, x] = advance(e, f, x + 3, B, B) + 0.2 * sources[f - 2, x]


NH = 15
HALF = NZ // 2


def load(ref, *lead):
    return [[ref[(*lead, slice(B * t, B * t + B), slice(HALF * h, HALF * h + HALF))] for h in range(2)] for t in range(3)]


def store(ref, plane, *lead):
    for t in range(3):
        for h in range(2):
            ref[(*lead, slice(B * t, B * t + B), slice(HALF * h, HALF * h + HALF))] = plane[t][h]


def add(*planes):
    planes = [p for p in planes if p is not None]
    return [[sum((p[t][h] for p in planes[1:]), planes[0][t][h]) for h in range(2)] for t in range(3)]


def beside_plane(c):
    row = lax.broadcasted_iota(jnp.int32, (B, HALF), 0)
    lane = lax.broadcasted_iota(jnp.int32, (B, HALF), 1)
    top, bottom, start, end = row == 0, row == B - 1, lane == 0, lane == HALF - 1
    out = []
    for t in range(3):
        after = [pltpu.roll(c[t][h], 1, axis=1) for h in range(2)]
        ahead = [pltpu.roll(c[t][h], HALF - 1, axis=1) for h in range(2)]
        along_z = [
            jnp.where(start, 0.0, after[0]) + jnp.where(end, ahead[1], ahead[0]),
            jnp.where(start, after[0], after[1]) + jnp.where(end, 0.0, ahead[1]),
        ]
        tile = []
        for h in range(2):
            down = pltpu.roll(c[t][h], 1, axis=0)
            if t > 0:
                down = jnp.where(top, pltpu.roll(c[t - 1][h], 1, axis=0), down)
            up = pltpu.roll(c[t][h], B - 1, axis=0)
            if t < 2:
                up = jnp.where(bottom, pltpu.roll(c[t + 1][h], B - 1, axis=0), up)
            tile.append(along_z[h] + (down + up))
        out.append(tile)
    return out


def relax(centre, others, source, scale):
    total = add(*others, None if centre is None else beside_plane(centre))
    if source is not None:
        total = [[total[t][h] - source[t][h] for h in range(2)] for t in range(3)]
    return [[total[t][h] * scale[t] for h in range(2)] for t in range(3)]


def weights(flags_x, flags_y):
    out = []
    for flag_y in flags_y:
        value = jnp.full((B, HALF), 1.0 / 6.0, F32)
        for flag in (*flags_x, flag_y):
            if flag is not None:
                value = jnp.where(flag, value, 0.0)
        out.append(value)
    return out


def slab_kernel(own, own_source, y_odd, y_even, even, odd, first, source, f2, f3, f4, f5, f6, low, high):
    gy = lax.axis_index("gy")
    scale = weights((), (gy > 0, None, gy < lax.axis_size("gy") - 1))
    row = lax.broadcasted_iota(jnp.int32, (B, HALF), 0)
    for x in range(B):
        first[x, B : 2 * B, :] = own[x]
        source[x, B : 2 * B, :] = own_source[x]

    def fill(below, above):
        for x in range(B):
            for k, halo in ((0, below), (2, above)):
                first[x, k * B : (k + 1) * B, :] = halo[x]
                source[x, k * B : (k + 1) * B, :] = halo[B + x]

    by_parity("gy", fill, y_even, y_odd)

    def keep(side, k, plane):
        for h in range(2):
            part = slice(HALF * h, HALF * h + HALF)
            side[k - 1, :, part] = plane[1][h]
            if k < B:
                side[B - 1 + k, k:, part] = plane[0][h][k:]
                side[2 * B - 1 - k, : B - k, part] = plane[2][h][: B - k]

    for side, x in ((low, 0), (high, B - 1)):
        keep(side, 1, load(first, x))
    levels = {1: first, 2: f2, 3: f3, 4: f4, 5: f5, 6: f6, 7: f5}
    for k in range(2, 9):
        depth = 9 - k
        now = levels[k - 1]
        for x in range(B):
            if depth <= x < B - depth:
                continue
            others = [load(now, y) for y in (x - 1, x + 1) if 0 <= y < B]
            plane = relax(load(now, x), others, load(source, x), scale)
            if k < 8:
                store(levels[k], plane, x)
            for side, face in ((low, 0), (high, B - 1)):
                if x == face:
                    keep(side, k, plane)

    def send(low_out, high_out):
        low_out[...] = low[...]
        high_out[...] = high[...]

    by_parity("gx", send, even, odd)


def finish_kernel(star, star_rest, first, source, f2, f3, f4, early_odd, early_even, y_even, y_odd, x_odd, x_even, gas_next, pressure, arrived, o0, o1, r0, r1, hist):
    gx = lax.axis_index("gx")
    gy = lax.axis_index("gy")
    flags_y = (gy > 0, None, gy < lax.axis_size("gy") - 1)
    inner = weights((), flags_y)
    outer = [weights((gx > 0,), flags_y), weights((gx < lax.axis_size("gx") - 1,), flags_y)]

    def arrive(d, halo, at):
        for f in range(5):
            for half in range(2):
                r = 2 * f + half
                arrived[d, f, :, half * NZ : (half + 1) * NZ] = halo[at + r // B, r % B : r % B + 1, :]

    def take_y(below, above):
        for d, halo, row in ((2, below, 0), (3, above, B - 1)):
            for r in range(10):
                at, line = (B + r, row) if r < B else (2 * B, r - B)
                part = slice(r % 2 * NZ, r % 2 * NZ + NZ)
                arrived[d, r // 2, :, part] = halo[at, line : line + 1, :]

    def take_x(left, right):
        hist[0] = left[...]
        hist[1] = right[...]

    by_parity("gy", take_y, y_even, y_odd)
    by_parity("gx", take_x, x_even, x_odd)

    def take_early(left, right):
        arrive(0, left, NL + 1)
        arrive(1, right, NL + 1)

    by_parity("gx", take_early, early_even, early_odd)

    def history(side, k):
        at = (B - 1 + k, k - 1, 2 * B - 1 - k)
        return [[hist[side, at[t], :, slice(HALF * h, HALF * h + HALF)] for h in range(2)] for t in range(3)]

    slabs = {1: first, 2: f2, 3: f3, 4: f4}
    owns = {k: (o0, o1)[k % 2] for k in range(2, 9)}

    def alone(k, x):
        return k in slabs and k - 1 <= x <= B - k

    responses = {k: (r0, r1)[k % 2] for k in range(2, 9)}

    def at(k, x):
        if 0 <= x < B:
            return load(slabs[k] if alone(k, x) else owns[k], x)
        side, depth = (0, -x) if x < 0 else (1, x - B + 1)
        return load(responses[k], side, depth - 1) if depth < k else None

    for k in range(2, 9):
        depth = min(k - 1, 9 - k)
        for x in range(-depth, B + depth):
            if alone(k, x):
                continue
            if k == 2 and 0 <= x < B:
                drive = history(0 if x == 0 else 1, 1)
                drive = [[drive[t][h] * inner[t] for h in range(2)] for t in range(3)]
                store(owns[k], add(load(f2, x), drive), x)
                continue
            others = [at(k - 1, x - 1), at(k - 1, x + 1)]
            if 0 <= x < B:
                if x == 0:
                    others.append(history(0, k - 1))
                if x == B - 1:
                    others.append(history(1, k - 1))
                store(owns[k], relax(at(k - 1, x), others, load(source, x), inner), x)
            else:
                side, far = (0, -x) if x < 0 else (1, x - B + 1)
                store(responses[k], relax(at(k - 1, x), others, None, outer[side]), side, far - 1)
    last, edge = owns[8], responses[8]

    def level(x):
        if x < 0:
            return edge[0, 0, B : 2 * B, :] + hist[0, B - 1]
        if x >= B:
            return edge[1, 0, B : 2 * B, :] + hist[1, B - 1]
        return last[x, B : 2 * B, :]

    for x in range(B):
        centre = level(x)
        pressure[x] = centre
        gas_next[0, x] = star[0, x] - 0.1 * (level(x + 1) - level(x - 1))
        gas_next[1, x] = star[1, x] - 0.1 * (last[x, B + 1 : 2 * B + 1, :] - last[x, B - 1 : 2 * B - 1, :])
        gas_next[2, x] = star[2, x] - 0.1 * (beside(centre, 1) - beside(centre, -1))
        gas_next[3, x] = star_rest[0, x]
        gas_next[4, x] = star_rest[1, x]


def body(gas, guess, motion, size, cell, target, on, when, head):
    shape = jax.ShapeDtypeStruct
    [first] = call(first_kernel, [shape((B, 128), F32)], 0, 10**10)()
    y_even, y_odd = call(pack_y_kernel, [tiles(NL)] * 2, 3, 10**6)(first, gas, guess)
    y_odd = swap(y_odd, "gy", 1)
    y_even = swap(y_even, "gy", 0)
    kept, rows, parcels = call(
        renew_kernel,
        [shape((5, 1, PD), F32), shape((2, PD), F32), shape((4, 2, B, NZ), F32)],
        5,
        10**9,
        scratch=[pltpu.VMEM((1, PD), jnp.int32)],
    )(gas, motion, size, cell, target)
    x_even, x_odd = call(pack_x_kernel, [tiles(NL + 3)] * 2, 5, 10**6)(gas, guess, y_odd, y_even, parcels)
    [sources] = call(spread_kernel, [shape((3, B * B, NZ), F32)], 6, 10**9, smem=(2, 3, 4))(
        rows, cell, on, when, head, x_even
    )
    sources = sources.reshape(3, B, B, NZ)
    x_odd = swap(x_odd, "gx", 1)
    x_even = swap(x_even, "gx", 0)
    wide = pltpu.VMEM((5, B + 6, 3 * B, NZ), F32)
    star, own_source, ps_even, ps_odd = call(
        predict_kernel,
        [shape((3, B, B, NZ), F32), tiles(B), tiles(2 * B + 1), tiles(2 * B + 1)],
        8,
        10**7,
        scratch=[
            wide,
            pltpu.VMEM((B + 2, B, NZ), F32),
            pltpu.VMEM((B, 2 * B, NZ), F32),
            pltpu.VMEM((B + 2, 3 * B, NZ), F32),
        ],
    )(gas, guess, y_odd, y_even, x_odd, x_even, sources, parcels)
    [star_rest] = call(scalars_kernel, [shape((2, B, B, NZ), F32)], 7, 10**8, scratch=[wide])(
        gas, y_odd, y_even, x_odd, x_even, sources, ps_odd
    )
    y_odd = swap(ps_odd, "gy", 1)
    y_even = swap(ps_even, "gy", 0)
    slab = shape((B, 3 * B, NZ), F32)
    scratch = pltpu.VMEM((B, 3 * B, NZ), F32)
    early_odd, early_even = x_odd, x_even
    x_even, x_odd, *slabs = call(
        slab_kernel,
        [tiles(NH), tiles(NH)] + [slab] * 5,
        4,
        10**7,
        scratch=[scratch, scratch, pltpu.VMEM((NH, B, NZ), F32), pltpu.VMEM((NH, B, NZ), F32)],
    )(ps_even, own_source, y_odd, y_even)
    x_odd = swap(x_odd, "gx", 1)
    x_even = swap(x_even, "gx", 0)
    response = pltpu.VMEM((2, 4, 3 * B, NZ), F32)
    gas_next, pressure, arrived = call(
        finish_kernel,
        [shape((5, B, B, NZ), F32), shape((B, B, NZ), F32), shape((4, 5, 1, CAP), F32)],
        13,
        10**7,
        scratch=[scratch, scratch, response, response, pltpu.VMEM((2, NH, B, NZ), F32)],
    )(star, star_rest, *slabs, early_odd, early_even, y_even, y_odd, x_odd, x_even)
    return gas_next, pressure, kept, arrived


def solution(mesh):
    in_specs = (
        P(None, "gx", "gy", None),
        P("gx", "gy", None),
        P(None, "gx", "gy"),
        P("gx", "gy"),
        P("gx", "gy"),
        P("gx", "gy"),
        P("gx", "gy"),
        P("gx", "gy"),
        P("gx", "gy"),
    )
    out_specs = (
        P(None, "gx", "gy", None),
        P("gx", "gy", None),
        P(None, "gx", "gy"),
        P(None, None, "gx", "gy"),
    )
    return jax.shard_map(body, mesh=mesh, in_specs=in_specs, out_specs=out_specs, check_vma=False)
```

```python
import jax
import jax.numpy as jnp
from jax import lax
from jax.experimental import pallas as pl
from jax.experimental.pallas import tpu as pltpu
from jax.sharding import PartitionSpec as P

B = 8
NZ = 256
PD = 4096
CAP = 512
CHUNK = 512
LONG = 2048
F32 = jnp.float32
BF16 = jnp.bfloat16
VMEM = pl.BlockSpec(memory_space=pltpu.VMEM)
SMEM = pl.BlockSpec(memory_space=pltpu.SMEM)

Y_LAYERS = [(1, 0), (1, 1), (1, 2), (0, 0), (0, 1), (2, 0), (2, 1), (3, 0), (3, 1), (4, 0), (4, 1), (5, 0)]
X_LAYERS = [(0, 0), (0, 1), (0, 2), (1, 0), (1, 1), (2, 0), (2, 1), (3, 0), (3, 1), (4, 0), (4, 1), (5, 0)]
NL = 12


def params(limit=16):
    return pltpu.CompilerParams(vmem_limit_bytes=limit * 1024 * 1024)


def tiles(n):
    return jax.ShapeDtypeStruct((n, B, NZ), F32)


def call(kernel, outs, n_in, cost, scratch=(), smem=(), limit=16):
    return pl.pallas_call(
        kernel,
        out_shape=outs,
        in_specs=[SMEM if i in smem else VMEM for i in range(n_in)],
        out_specs=[VMEM] * len(outs),
        scratch_shapes=list(scratch),
        compiler_params=params(limit),
        cost_estimate=pl.CostEstimate(flops=cost, bytes_accessed=cost // 8, transcendentals=0),
    )


def by_parity(axis, act, even, odd):
    first = lax.rem(lax.axis_index(axis), 2) == 0

    @pl.when(first)
    def _():
        act(odd, even)

    @pl.when(jnp.logical_not(first))
    def _():
        act(even, odd)


def swap(shard, axis, start):
    peers = lax.axis_size(axis)
    pairs = [(i + a, i + 1 - a) for i in range(start, peers - 1, 2) for a in range(2)]
    return lax.ppermute(shard, axis, pairs)


def first_kernel(out):
    out[...] = jnp.zeros_like(out)


def pack_y_kernel(_, gas, guess, even, odd):
    def act(low, high):
        for r, (field, depth) in enumerate(Y_LAYERS):
            for side, y in ((low, depth), (high, B - 1 - depth)):
                side[r] = guess[:, y, :] if field == 5 else gas[field, :, y, :]

    by_parity("gy", act, even, odd)


def split(value):
    high = value.astype(BF16).astype(F32)
    return high, value - high


def counting(rows, lanes=CHUNK):
    return lax.broadcasted_iota(jnp.int32, (rows, lanes), 0).astype(F32).astype(BF16)


def exact(numbers):
    return numbers.astype(F32).astype(BF16)


def one_hot(counted, numbers):
    return jnp.where(counted == exact(numbers), jnp.ones((), BF16), jnp.zeros((), BF16))


def renew_kernel(gas, motion, size, cell, target, kept, rows, parcels, places):
    table = jnp.concatenate([gas[f].reshape(B * B, NZ) for f in range(4)], axis=0)
    high, low = split(table)
    table = jnp.concatenate([high.astype(BF16), low.astype(BF16)], axis=1)
    at_z = counting(NZ)
    at_xy = lax.broadcasted_iota(jnp.int32, (B * B, CHUNK), 0)
    heading = lax.broadcasted_iota(jnp.int32, (B, NZ), 0)
    blocks = [heading == target[:, n * NZ : (n + 1) * NZ] for n in range(PD // NZ)]
    a = lax.broadcasted_iota(jnp.int32, (NZ, NZ), 0)
    b = lax.broadcasted_iota(jnp.int32, (NZ, NZ), 1)
    upper = jnp.where(a <= b, 1.0, 0.0).astype(BF16)
    marks = jnp.concatenate([jnp.where(chosen, 1.0, 0.0) for chosen in blocks], axis=0).astype(BF16)
    ranks = jnp.dot(marks, upper, preferred_element_type=F32)
    before = jnp.zeros((B, 1), F32)
    for n, chosen in enumerate(blocks):
        rank = ranks[B * n : B * n + B] + before
        before = rank[:, NZ - 1 :]
        place = jnp.where(chosen & (heading < 4), rank + heading.astype(F32) * float(CAP), 0.0)
        places[:, n * NZ : (n + 1) * NZ] = jnp.sum(place, axis=0, keepdims=True).astype(jnp.int32) - 1
    moved = jnp.zeros((10 * B, NZ), F32)
    at_high = lax.broadcasted_iota(jnp.int32, (B, CHUNK), 0)
    across = (((1,), (1,)), ((), ()))
    for n in range(PD // CHUNK):
        part = slice(n * CHUNK, (n + 1) * CHUNK)
        cells = cell[:, part]
        goal = target[:, part]
        in_z = one_hot(at_z, cells & (NZ - 1))
        in_xy = at_xy == (cells >> 8)
        found = jnp.dot(table, jnp.concatenate([in_z, in_z], axis=0), preferred_element_type=F32)
        local = [
            jnp.sum(jnp.where(in_xy, found[f * B * B : (f + 1) * B * B], 0.0), axis=0, keepdims=True)
            for f in range(4)
        ]
        u, v, w, temperature = (motion[f, :, part] for f in range(4))
        diameter = size[:, part]
        excess = local[3] - temperature
        vapour = 0.5 * diameter * jax.nn.sigmoid(excess)
        renewed = [
            u + 0.4 * (local[0] - u),
            v + 0.4 * (local[1] - v),
            w + 0.2 * ((local[2] - w) * 2.0 - 1.0),
            temperature + 0.2 * excess,
            diameter - 0.2 * vapour,
        ]
        drag = 0.5 * diameter * diameter * (w - local[2])
        alive = goal >= 0
        for f in range(5):
            kept[f, :, part] = jnp.where(goal == 4, renewed[f], 0.0)
        rows[0:1, part] = jnp.where(alive, drag, 0.0)
        rows[1:2, part] = jnp.where(alive, vapour, 0.0)
        place = places[:, part]
        in_low = one_hot(at_z, place & (NZ - 1))
        in_high = at_high == (place >> 8)
        split_up = [split(value) for value in renewed]
        leaving = [jnp.where(in_high, split_up[f][piece], 0.0) for piece in range(2) for f in range(5)]
        moved = moved + lax.dot_general(
            jnp.concatenate(leaving, axis=0).astype(BF16), in_low, across, preferred_element_type=F32
        )
    moved = moved[: 5 * B] + moved[5 * B :]
    for d in range(4):
        for f in range(5):
            for half in range(2):
                at = f * B + 2 * d + half
                r = 2 * f + half
                parcels[d, r // B, r % B : r % B + 1, :] = moved[at : at + 1]
        parcels[d, 1, 2:, :] = jnp.zeros((B - 2, NZ), F32)


def spread_kernel(rows, cell, on, when, head, _, sources):
    at_z = counting(NZ, LONG)
    at_xy = counting(B * B, LONG)
    total = jnp.zeros((4 * B * B, NZ), F32)
    across = (((1,), (1,)), ((), ()))
    for n in range(PD // LONG):
        part = slice(n * LONG, (n + 1) * LONG)
        cells = cell[:, part]
        in_z = one_hot(at_z, cells & (NZ - 1))
        in_xy = at_xy == exact(cells >> 8)
        pieces = [*split(rows[0:1, part]), *split(rows[1:2, part])]
        given = jnp.concatenate([jnp.where(in_xy, piece.astype(BF16), jnp.zeros((), BF16)) for piece in pieces], axis=0)
        total = total + lax.dot_general(given, in_z, across, preferred_element_type=F32)
    q = B * B
    steam = total[2 * q : 3 * q] + total[3 * q :]
    sources[0] = total[:q] + total[q : 2 * q]
    sources[1] = -2.0 * steam
    sources[2] = steam
    lanes = lax.broadcasted_iota(jnp.int32, (1, NZ), 1)
    for s in range(B):
        ramp = jnp.clip((100.0 - when[0, s].astype(F32)) / 50.0, 0.0, 1.0)
        strength = 3.0 * ramp * on[0, s].astype(F32)
        where = head[0, s]
        row = pl.ds(where >> 8, 1)
        taken = jnp.where(lanes == (where & (NZ - 1)), strength, 0.0)
        for f in range(2):
            sources[f, row, :] = sources[f, row, :] - taken


def pack_x_kernel(gas, guess, y_odd, y_even, parcels, even, odd):
    def planes(low, high):
        for side, near, step, heading in ((low, 0, 1, 1), (high, B - 1, -1, 0)):
            side[NL + 1] = parcels[heading, 0]
            side[NL + 2] = parcels[heading, 1]
            for r, (field, depth) in enumerate(X_LAYERS):
                x = near + step * depth
                side[r] = guess[x] if field == 5 else gas[field, x]

            def corners(below, above, side=side, near=near, step=step):
                for h, halo in enumerate((below, above)):
                    for r, (layer, x) in enumerate(((3, near), (4, near), (0, near), (0, near + step))):
                        side[NL, 4 * h + r : 4 * h + r + 1, :] = halo[layer, x : x + 1, :]

            by_parity("gy", corners, y_even, y_odd)

    by_parity("gx", planes, even, odd)


def beside(value, by):
    lane = lax.broadcasted_iota(jnp.int32, value.shape, 1)
    turned = pltpu.roll(value, (-by) % NZ, axis=1)
    return jnp.where((lane < NZ - by) if by > 0 else (lane >= -by), turned, 0.0)


def advance(e, f, x, rows, first):
    def at(field, dx, dy):
        return e[field, x + dx, first + dy : first + dy + rows, :]

    centre = at(f, 0, 0)
    xs = {s: at(f, s, 0) for s in (-2, -1, 1, 2)}
    ys = {s: at(f, 0, s) for s in (-2, -1, 1, 2)}
    zs = {s: beside(centre, s) for s in (-2, -1, 1, 2)}
    laplace = xs[1] + xs[-1] + ys[1] + ys[-1] + zs[1] + zs[-1] - 6.0 * centre
    transport = 0.0
    for axis, shifted in enumerate((xs, ys, zs)):
        slope = 8.0 * (shifted[1] - shifted[-1]) - (shifted[2] - shifted[-2])
        transport = transport + at(axis, 0, 0) * slope
    return centre + (0.02 * laplace - (0.2 / 12.0) * transport)


def fill_own(gas, e, fields):
    for k, f in enumerate(fields):
        e[k, 3 : 3 + B, B : 2 * B, :] = gas[f]


def predict_kernel(gas, guess, y_odd, y_even, x_odd, x_even, sources, parcels, star, source_out, even, odd, e, wide, tall, q):
    gx = lax.axis_index("gx")
    gy = lax.axis_index("gy")
    has_left, has_right = gx > 0, gx < lax.axis_size("gx") - 1
    has_below, has_above = gy > 0, gy < lax.axis_size("gy") - 1
    fill_own(gas, e, range(3))
    q[1 : 1 + B, B : 2 * B, :] = guess[...]

    def fill_y(below, above):
        for r, (field, depth) in enumerate(Y_LAYERS):
            for halo, y in ((below, B - 1 - depth), (above, 2 * B + depth)):
                if field == 5:
                    q[1 : 1 + B, y, :] = halo[r]
                elif field < 3:
                    e[field, 3 : 3 + B, y, :] = halo[r]

    def fill_x(left, right):
        for r, (field, depth) in enumerate(X_LAYERS):
            for halo, x in ((left, -1 - depth), (right, B + depth)):
                if field == 5:
                    q[x + 1, B : 2 * B, :] = halo[r]
                elif field < 3:
                    e[field, x + 3, B : 2 * B, :] = halo[r]
        for halo, near, step in ((left, 2, -1), (right, 3 + B, 1)):
            for h, (y, onward) in enumerate(((B - 1, -1), (2 * B, 1))):
                spots = ((0, near, y), (0, near, y + onward), (1, near, y), (1, near + step, y))
                for r, (field, x, row) in enumerate(spots):
                    e[field, x, row : row + 1, :] = halo[NL, 4 * h + r : 4 * h + r + 1, :]

    by_parity("gy", fill_y, y_even, y_odd)
    by_parity("gx", fill_x, x_even, x_odd)
    for x in range(-1, B + 1):
        value = advance(e, 0, x + 3, B, B)
        if x < 0:
            value = jnp.where(has_left, value, 0.0)
        if x == B:
            value = jnp.where(has_right, value, 0.0)
        wide[x + 1] = value
        if 0 <= x < B:
            star[0, x] = value
    for x in range(B):
        value = advance(e, 1, x + 3, B + 2, B - 1)
        row = lax.broadcasted_iota(jnp.int32, value.shape, 0)
        inside = ((row > 0) | has_below) & ((row < B + 1) | has_above)
        value = jnp.where(inside, value, 0.0)
        tall[x, : B + 2, :] = value
        star[1, x] = value[1 : 1 + B]
    for x in range(B):
        w = advance(e, 2, x + 3, B, B) + 0.2 * sources[0, x]
        star[2, x] = w
        spread = wide[x + 2] - wide[x] + (tall[x, 2 : 2 + B, :] - tall[x, :B, :])
        source = 2.5 * (spread + (beside(w, 1) - beside(w, -1)))
        centre = q[x + 1, B : 2 * B, :]
        around = q[x + 2, B : 2 * B, :] + q[x, B : 2 * B, :]
        around = around + q[x + 1, B + 1 : 2 * B + 1, :] + q[x + 1, B - 1 : 2 * B - 1, :]
        field = (around + beside(centre, 1) + beside(centre, -1) - source) * (1.0 / 6.0)
        source_out[x] = source
        for side in (even, odd):
            side[x] = field
            side[B + x] = source

    def attach(low, high):
        for side, heading, row in ((high, 2, 0), (low, 3, B - 1)):
            for x in range(B):
                side[B + x, row : row + 1, :] = parcels[heading, 0, x : x + 1, :]
            side[2 * B] = parcels[heading, 1]

    by_parity("gy", attach, even, odd)


def scalars_kernel(gas, y_odd, y_even, x_odd, x_even, sources, _, star, e):
    fill_own(gas, e, range(5))

    def fill_y(below, above):
        for r, (field, depth) in enumerate(Y_LAYERS):
            if field in (3, 4):
                e[field, 3 : 3 + B, B - 1 - depth, :] = below[r]
                e[field, 3 : 3 + B, 2 * B + depth, :] = above[r]

    def fill_x(left, right):
        for r, (field, depth) in enumerate(X_LAYERS):
            if field in (3, 4):
                e[field, 2 - depth, B : 2 * B, :] = left[r]
                e[field, B + 3 + depth, B : 2 * B, :] = right[r]

    by_parity("gy", fill_y, y_even, y_odd)
    by_parity("gx", fill_x, x_even, x_odd)
    for f in (3, 4):
        for x in range(B):
            star[f - 3, x] = advance(e, f, x + 3, B, B) + 0.2 * sources[f - 2, x]


NH = 15
HALF = NZ // 2


def load(ref, *lead):
    return [[ref[(*lead, slice(B * t, B * t + B), slice(HALF * h, HALF * h + HALF))] for h in range(2)] for t in range(3)]


def store(ref, plane, *lead):
    for t in range(3):
        for h in range(2):
            ref[(*lead, slice(B * t, B * t + B), slice(HALF * h, HALF * h + HALF))] = plane[t][h]


def add(*planes):
    planes = [p for p in planes if p is not None]
    return [[sum((p[t][h] for p in planes[1:]), planes[0][t][h]) for h in range(2)] for t in range(3)]


def beside_plane(c):
    row = lax.broadcasted_iota(jnp.int32, (B, HALF), 0)
    lane = lax.broadcasted_iota(jnp.int32, (B, HALF), 1)
    top, bottom, start, end = row == 0, row == B - 1, lane == 0, lane == HALF - 1
    out = []
    for t in range(3):
        after = [pltpu.roll(c[t][h], 1, axis=1) for h in range(2)]
        ahead = [pltpu.roll(c[t][h], HALF - 1, axis=1) for h in range(2)]
        along_z = [
            jnp.where(start, 0.0, after[0]) + jnp.where(end, ahead[1], ahead[0]),
            jnp.where(start, after[0], after[1]) + jnp.where(end, 0.0, ahead[1]),
        ]
        tile = []
        for h in range(2):
            down = pltpu.roll(c[t][h], 1, axis=0)
            if t > 0:
                down = jnp.where(top, pltpu.roll(c[t - 1][h], 1, axis=0), down)
            up = pltpu.roll(c[t][h], B - 1, axis=0)
            if t < 2:
                up = jnp.where(bottom, pltpu.roll(c[t + 1][h], B - 1, axis=0), up)
            tile.append(along_z[h] + (down + up))
        out.append(tile)
    return out


def relax(centre, others, source, scale):
    total = add(*others, None if centre is None else beside_plane(centre))
    if source is not None:
        total = [[total[t][h] - source[t][h] for h in range(2)] for t in range(3)]
    return [[total[t][h] * scale[t] for h in range(2)] for t in range(3)]


def weights(flags_x, flags_y):
    out = []
    for flag_y in flags_y:
        value = jnp.full((B, HALF), 1.0 / 6.0, F32)
        for flag in (*flags_x, flag_y):
            if flag is not None:
                value = jnp.where(flag, value, 0.0)
        out.append(value)
    return out


def slab_kernel(own, own_source, y_odd, y_even, even, odd, first, source, f2, f3, f4, f5, f6, low, high):
    gy = lax.axis_index("gy")
    scale = weights((), (gy > 0, None, gy < lax.axis_size("gy") - 1))
    row = lax.broadcasted_iota(jnp.int32, (B, HALF), 0)
    for x in range(B):
        first[x, B : 2 * B, :] = own[x]
        source[x, B : 2 * B, :] = own_source[x]

    def fill(below, above):
        for x in range(B):
            for k, halo in ((0, below), (2, above)):
                first[x, k * B : (k + 1) * B, :] = halo[x]
                source[x, k * B : (k + 1) * B, :] = halo[B + x]

    by_parity("gy", fill, y_even, y_odd)

    def keep(side, k, plane):
        for h in range(2):
            part = slice(HALF * h, HALF * h + HALF)
            side[k - 1, :, part] = plane[1][h]
            if k < B:
                side[B - 1 + k, k:, part] = plane[0][h][k:]
                side[2 * B - 1 - k, : B - k, part] = plane[2][h][: B - k]

    for side, x in ((low, 0), (high, B - 1)):
        keep(side, 1, load(first, x))
    levels = {1: first, 2: f2, 3: f3, 4: f4, 5: f5, 6: f6, 7: f5}
    for k in range(2, 9):
        depth = 9 - k
        now = levels[k - 1]
        for x in range(B):
            if depth <= x < B - depth:
                continue
            others = [load(now, y) for y in (x - 1, x + 1) if 0 <= y < B]
            plane = relax(load(now, x), others, load(source, x), scale)
            if k < 8:
                store(levels[k], plane, x)
            for side, face in ((low, 0), (high, B - 1)):
                if x == face:
                    keep(side, k, plane)

    def send(low_out, high_out):
        low_out[...] = low[...]
        high_out[...] = high[...]

    by_parity("gx", send, even, odd)


def finish_kernel(star, star_rest, first, source, f2, f3, f4, early_odd, early_even, y_even, y_odd, x_odd, x_even, gas_next, pressure, arrived, o0, o1, r0, r1, hist):
    gx = lax.axis_index("gx")
    gy = lax.axis_index("gy")
    flags_y = (gy > 0, None, gy < lax.axis_size("gy") - 1)
    inner = weights((), flags_y)
    outer = [weights((gx > 0,), flags_y), weights((gx < lax.axis_size("gx") - 1,), flags_y)]

    def arrive(d, halo, at):
        for f in range(5):
            for half in range(2):
                r = 2 * f + half
                arrived[d, f, :, half * NZ : (half + 1) * NZ] = halo[at + r // B, r % B : r % B + 1, :]

    def take_y(below, above):
        for d, halo, row in ((2, below, 0), (3, above, B - 1)):
            for r in range(10):
                at, line = (B + r, row) if r < B else (2 * B, r - B)
                part = slice(r % 2 * NZ, r % 2 * NZ + NZ)
                arrived[d, r // 2, :, part] = halo[at, line : line + 1, :]

    def take_x(left, right):
        hist[0] = left[...]
        hist[1] = right[...]

    by_parity("gy", take_y, y_even, y_odd)
    by_parity("gx", take_x, x_even, x_odd)

    def take_early(left, right):
        arrive(0, left, NL + 1)
        arrive(1, right, NL + 1)

    by_parity("gx", take_early, early_even, early_odd)

    def history(side, k):
        at = (B - 1 + k, k - 1, 2 * B - 1 - k)
        return [[hist[side, at[t], :, slice(HALF * h, HALF * h + HALF)] for h in range(2)] for t in range(3)]

    slabs = {1: first, 2: f2, 3: f3, 4: f4}
    owns = {k: (o0, o1)[k % 2] for k in range(2, 9)}

    def alone(k, x):
        return k in slabs and k - 1 <= x <= B - k

    responses = {k: (r0, r1)[k % 2] for k in range(2, 9)}

    def at(k, x):
        if 0 <= x < B:
            return load(slabs[k] if alone(k, x) else owns[k], x)
        side, depth = (0, -x) if x < 0 else (1, x - B + 1)
        return load(responses[k], side, depth - 1) if depth < k else None

    for k in range(2, 9):
        depth = min(k - 1, 9 - k)
        for x in range(-depth, B + depth):
            if alone(k, x):
                continue
            if k == 2 and 0 <= x < B:
                drive = history(0 if x == 0 else 1, 1)
                drive = [[drive[t][h] * inner[t] for h in range(2)] for t in range(3)]
                store(owns[k], add(load(f2, x), drive), x)
                continue
            others = [at(k - 1, x - 1), at(k - 1, x + 1)]
            if 0 <= x < B:
                if x == 0:
                    others.append(history(0, k - 1))
                if x == B - 1:
                    others.append(history(1, k - 1))
                store(owns[k], relax(at(k - 1, x), others, load(source, x), inner), x)
            else:
                side, far = (0, -x) if x < 0 else (1, x - B + 1)
                store(responses[k], relax(at(k - 1, x), others, None, outer[side]), side, far - 1)
    last, edge = owns[8], responses[8]

    def level(x):
        if x < 0:
            return edge[0, 0, B : 2 * B, :] + hist[0, B - 1]
        if x >= B:
            return edge[1, 0, B : 2 * B, :] + hist[1, B - 1]
        return last[x, B : 2 * B, :]

    for x in range(B):
        centre = level(x)
        pressure[x] = centre
        gas_next[0, x] = star[0, x] - 0.1 * (level(x + 1) - level(x - 1))
        gas_next[1, x] = star[1, x] - 0.1 * (last[x, B + 1 : 2 * B + 1, :] - last[x, B - 1 : 2 * B - 1, :])
        gas_next[2, x] = star[2, x] - 0.1 * (beside(centre, 1) - beside(centre, -1))
        gas_next[3, x] = star_rest[0, x]
        gas_next[4, x] = star_rest[1, x]


def body(gas, guess, motion, size, cell, target, on, when, head):
    shape = jax.ShapeDtypeStruct
    [first] = call(first_kernel, [shape((B, 128), F32)], 0, 10**10)()
    y_even, y_odd = call(pack_y_kernel, [tiles(NL)] * 2, 3, 10**6)(first, gas, guess)
    y_odd = swap(y_odd, "gy", 1)
    y_even = swap(y_even, "gy", 0)
    kept, rows, parcels = call(
        renew_kernel,
        [shape((5, 1, PD), F32), shape((2, PD), F32), shape((4, 2, B, NZ), F32)],
        5,
        10**9,
        scratch=[pltpu.VMEM((1, PD), jnp.int32)],
    )(gas, motion, size, cell, target)
    x_even, x_odd = call(pack_x_kernel, [tiles(NL + 3)] * 2, 5, 10**6)(gas, guess, y_odd, y_even, parcels)
    [sources] = call(spread_kernel, [shape((3, B * B, NZ), F32)], 6, 10**9, smem=(2, 3, 4))(
        rows, cell, on, when, head, x_even
    )
    sources = sources.reshape(3, B, B, NZ)
    x_odd = swap(x_odd, "gx", 1)
    x_even = swap(x_even, "gx", 0)
    wide = pltpu.VMEM((5, B + 6, 3 * B, NZ), F32)
    star, own_source, ps_even, ps_odd = call(
        predict_kernel,
        [shape((3, B, B, NZ), F32), tiles(B), tiles(2 * B + 1), tiles(2 * B + 1)],
        8,
        10**7,
        scratch=[
            wide,
            pltpu.VMEM((B + 2, B, NZ), F32),
            pltpu.VMEM((B, 2 * B, NZ), F32),
            pltpu.VMEM((B + 2, 3 * B, NZ), F32),
        ],
    )(gas, guess, y_odd, y_even, x_odd, x_even, sources, parcels)
    [star_rest] = call(scalars_kernel, [shape((2, B, B, NZ), F32)], 7, 10**8, scratch=[wide])(
        gas, y_odd, y_even, x_odd, x_even, sources, ps_odd
    )
    y_odd = swap(ps_odd, "gy", 1)
    y_even = swap(ps_even, "gy", 0)
    slab = shape((B, 3 * B, NZ), F32)
    scratch = pltpu.VMEM((B, 3 * B, NZ), F32)
    early_odd, early_even = x_odd, x_even
    x_even, x_odd, *slabs = call(
        slab_kernel,
        [tiles(NH), tiles(NH)] + [slab] * 5,
        4,
        10**7,
        scratch=[scratch, scratch, pltpu.VMEM((NH, B, NZ), F32), pltpu.VMEM((NH, B, NZ), F32)],
    )(ps_even, own_source, y_odd, y_even)
    x_odd = swap(x_odd, "gx", 1)
    x_even = swap(x_even, "gx", 0)
    response = pltpu.VMEM((2, 4, 3 * B, NZ), F32)
    gas_next, pressure, arrived = call(
        finish_kernel,
        [shape((5, B, B, NZ), F32), shape((B, B, NZ), F32), shape((4, 5, 1, CAP), F32)],
        13,
        10**7,
        scratch=[scratch, scratch, response, response, pltpu.VMEM((2, NH, B, NZ), F32)],
    )(star, star_rest, *slabs, early_odd, early_even, y_even, y_odd, x_odd, x_even)
    return gas_next, pressure, kept, arrived


def solution(mesh):
    in_specs = (
        P(None, "gx", "gy", None),
        P("gx", "gy", None),
        P(None, "gx", "gy"),
        P("gx", "gy"),
        P("gx", "gy"),
        P("gx", "gy"),
        P("gx", "gy"),
        P("gx", "gy"),
        P("gx", "gy"),
    )
    out_specs = (
        P(None, "gx", "gy", None),
        P("gx", "gy", None),
        P(None, "gx", "gy"),
        P(None, None, "gx", "gy"),
    )
    return jax.shard_map(body, mesh=mesh, in_specs=in_specs, out_specs=out_specs, check_vma=False)
```
